32 devices in a mesh: dp: 8 (over z, y), mp: 4 (over x, core).
Axes of the slice: x: 2, y: 2, z: 4, core: 2. Of those that a mesh axis runs over, the one named last changes fastest.
Arguments:
- tokens: bfloat16 [16384, 2048], P(('dp', 'mp')), may hold values from -6 to 6
- patches: bfloat16 [32768, 2048], P('dp'), may hold values from -6 to 6
- text_lengths: int32 [128], P('dp'), may hold values from 8 to 128, as said below
- prefix_lengths: int32 [128], P('dp'), may hold values from 1 to 128, as said below
- group_map: int32 [128], P('dp'), may hold values from 0 to 1, as said below
- ratio: int32 [2], replicated, may hold values from 1 to 4
- cotangent: bfloat16 [16384, 2048], P(('dp', 'mp')), may hold values from -6 to 6
- q_self: bfloat16 [2048, 2048], P(None, 'mp'), may hold values from -0.125 to 0.125
- k_self: bfloat16 [2048, 2048], P(None, 'mp'), may hold values from -0.125 to 0.125
- v_self: bfloat16 [2048, 2048], P(None, 'mp'), may hold values from -0.125 to 0.125
- o_self: bfloat16 [2048, 2048], P('mp'), may hold values from -0.375 to 0.375
- q_cross: bfloat16 [2048, 2048], P(None, 'mp'), may hold values from -0.125 to 0.125
- k_cross: bfloat16 [2048, 2048], P(None, 'mp'), may hold values from -0.125 to 0.125
- v_cross: bfloat16 [2048, 2048], P(None, 'mp'), may hold values from -0.125 to 0.125
- o_cross: bfloat16 [2048, 2048], P('mp'), may hold values from -0.5 to 0.5
- w_gate: bfloat16 [2048, 5120], P(None, 'mp'), may hold values from -0.125 to 0.125
- w_up: bfloat16 [2048, 5120], P(None, 'mp'), may hold values from -0.125 to 0.125
- w_down: bfloat16 [5120, 2048], P('mp'), may hold values from -0.15625 to 0.15625
- gain_attn: float32 [2048], replicated, may hold values from 0.1 to 1.9
- gain_cross: float32 [2048], replicated, may hold values from 0.1 to 1.9
- gain_mlp: float32 [2048], replicated, may hold values from 0.1 to 1.9
Outputs:
- output: bfloat16 [16384, 2048], P(('dp', 'mp'))
- grad_tokens: float32 [16384, 2048], P(('dp', 'mp'))
- grad_q_self: float32 [2048, 2048], P(None, 'mp')
- grad_k_self: float32 [2048, 2048], P(None, 'mp')
- grad_v_self: float32 [2048, 2048], P(None, 'mp')
- grad_o_self: float32 [2048, 2048], P('mp')
- grad_q_cross: float32 [2048, 2048], P(None, 'mp')
- grad_k_cross: float32 [2048, 2048], P(None, 'mp')
- grad_v_cross: float32 [2048, 2048], P(None, 'mp')
- grad_o_cross: float32 [2048, 2048], P('mp')
- grad_w_gate: float32 [2048, 5120], P(None, 'mp')
- grad_w_up: float32 [2048, 5120], P(None, 'mp')
- grad_w_down: float32 [5120, 2048], P('mp')
- grad_gain_attn: float32 [2048], replicated
- grad_gain_cross: float32 [2048], replicated
- grad_gain_mlp: float32 [2048], replicated
The draws below stay inside these ranges and needn't reach their ends.
Inputs may be any that keep to these rules, and one draw needn't show every extreme that they name: `text_lengths`: each of the two groups holds an example of length 128. `prefix_lengths`: at most the example's text length. `group_map`: both groups occur.
All inputs are finite; a program needn't handle non-finite values.
Results may differ from the reference program's by a relative error of at most 0.028.
Values may be sent and summed in bfloat16 or wider, within the bound.
A program may use at most 384 MiB of HBM per device.

```python
import jax
import jax.numpy as jnp
from jax import lax

D = 2048
HEADS = 32
HEAD = 64
FF = 5120
SEQ = 128
PATCH = 256
EXAMPLES = 128
TOKENS = 16384
PATCH_ROWS = 32768


def pair_of(key):
    order = jax.random.permutation(key, EXAMPLES)
    return (order[0], order[1])


def lengths_of(key):
    first, second = pair_of(key)
    sub_key = jax.random.fold_in(key, 2)
    drawn = jax.random.randint(sub_key, (EXAMPLES,), 8, SEQ + 1, dtype=jnp.int32)
    return drawn.at[first].set(SEQ).at[second].set(SEQ)


def draw_text_lengths(key, part):
    shared = lengths_of(key)
    return shared


def draw_prefix_lengths(key, part):
    shared = lengths_of(key)
    key = jax.random.fold_in(key, 12)
    return jax.random.randint(key, (EXAMPLES,), 1, shared + 1, dtype=jnp.int32)


def draw_group_map(key, part):
    first, second = pair_of(key)
    key = jax.random.fold_in(key, 13)
    drawn = jax.random.randint(key, (EXAMPLES,), 0, 2, dtype=jnp.int32)
    return drawn.at[first].set(0).at[second].set(1)


def shard_levels(key, extent, shards, smallest, top_value):
    def one(axis_at, blocks):
        heights = jax.random.uniform(jax.random.fold_in(jax.random.fold_in(key, 6), axis_at), (blocks,), jnp.float32, smallest / len(shards), top_value / len(shards))
        return jnp.repeat(jnp.exp(heights), extent[axis_at] // blocks).reshape((-1,) + (1,) * (len(extent) - axis_at - 1))

    loudness = one(*shards[0])
    for cut in shards[1:]:
        loudness = loudness * one(*cut)
    return loudness


def gaussian(key, dims, deviation, reach, shards=(), kind=jnp.bfloat16):
    level = shard_levels(key, dims, shards, -0.22, 0.18) if shards else 1.0
    entries = jax.random.normal(key, dims, jnp.float32) * deviation * level
    return jnp.minimum(jnp.maximum(entries, -reach), reach).astype(kind)


def setup_inputs(seed: int = 0) -> dict:
    seeds = jax.random.split(jax.random.key(seed), 22)
    return {
        "tokens": gaussian(seeds[0], (TOKENS, D), 1.0, 6.0, ((0, 32),)),
        "patches": gaussian(seeds[1], (PATCH_ROWS, D), 1.0, 6.0, ((0, 8),)),
        "text_lengths": draw_text_lengths(jax.random.fold_in(seeds[21], 71), 0),
        "prefix_lengths": draw_prefix_lengths(jax.random.fold_in(seeds[21], 71), 0),
        "group_map": draw_group_map(jax.random.fold_in(seeds[21], 71), 0),
        "ratio": jax.random.randint(seeds[5], (2,), 1, 5).astype(jnp.int32),
        "cotangent": gaussian(seeds[6], (TOKENS, D), 1.0, 6.0, ((0, 32),)),
        "q_self": gaussian(seeds[7], (D, HEADS * HEAD), D ** -0.5, 0.125, ((1, 4),)),
        "k_self": gaussian(seeds[8], (D, HEADS * HEAD), D ** -0.5, 0.125, ((1, 4),)),
        "v_self": gaussian(seeds[9], (D, HEADS * HEAD), D ** -0.5, 0.125, ((1, 4),)),
        "o_self": gaussian(seeds[10], (HEADS * HEAD, D), (HEADS * HEAD // 8) ** -0.5, 0.375, ((0, 4),)),
        "q_cross": gaussian(seeds[11], (D, HEADS * HEAD), D ** -0.5, 0.125, ((1, 4),)),
        "k_cross": gaussian(seeds[12], (D, HEADS * HEAD), D ** -0.5, 0.125, ((1, 4),)),
        "v_cross": gaussian(seeds[13], (D, HEADS * HEAD), D ** -0.5, 0.125, ((1, 4),)),
        "o_cross": gaussian(seeds[14], (HEADS * HEAD, D), (HEADS * HEAD // 16) ** -0.5, 0.5, ((0, 4),)),
        "w_gate": gaussian(seeds[15], (D, FF), D ** -0.5, 0.125, ((1, 4),)),
        "w_up": gaussian(seeds[16], (D, FF), D ** -0.5, 0.125, ((1, 4),)),
        "w_down": gaussian(seeds[17], (FF, D), (FF // 4) ** -0.5, 0.15625, ((0, 4),)),
        "gain_attn": jnp.clip(1.0 + 0.18 * jax.random.normal(seeds[18], (D,), jnp.float32), 0.1, 1.9),
        "gain_cross": jnp.clip(1.0 + 0.18 * jax.random.normal(seeds[19], (D,), jnp.float32), 0.1, 1.9),
        "gain_mlp": jnp.clip(1.0 + 0.18 * jax.random.normal(seeds[20], (D,), jnp.float32), 0.1, 1.9),
    }


@jax.custom_vjp
def low(v):
    return lax.optimization_barrier(v.astype(jnp.bfloat16)).astype(jnp.float32)

@jax.custom_vjp
def low_back(v):
    return v

def low_keep(v):
    return (low(v), None)

def low_pass(kept, grad):
    return (grad,)

def back_keep(v):
    return (v, None)

def back_low(kept, grad):
    return (low(grad),)
low.defvjp(low_keep, low_pass)
low_back.defvjp(back_keep, back_low)
epsilon = 1e-06
highest = lax.Precision.HIGHEST

def matmul(left, right):
    return jnp.matmul(left, right, precision=highest)

def norm_rows(values_in, gain):
    return values_in * lax.rsqrt(lax.optimization_barrier(jnp.mean(values_in * values_in, axis=-1, keepdims=True)) + epsilon) * gain

def project(rows, weight):
    return low(low_back(matmul(rows, weight)))

def heads_of(tensor):
    return tensor.reshape(tensor.shape[0], tensor.shape[1], HEADS, HEAD)

def attention(queries, keys, values, key_mask):
    scores = low_back(jnp.einsum('eqhd,ekhd->ehqk', heads_of(queries), heads_of(keys), precision=highest) * HEAD ** (-0.5))
    if key_mask is not None:
        scores = jnp.where(key_mask, scores, -1e+30)
    highest_score = lax.optimization_barrier(jnp.max(scores, axis=-1, keepdims=True))
    expd = jnp.exp(scores - highest_score)
    attn_probs = expd / lax.optimization_barrier(jnp.sum(expd, axis=-1, keepdims=True))
    mixed = jnp.einsum('ehqk,ekhd->eqhd', low(attn_probs), heads_of(values), precision=highest)
    return low(low_back(mixed.reshape(queries.shape[0], queries.shape[1], HEADS * HEAD)))

def reference(tokens, patches, text_lengths, prefix_lengths, group_map, ratio, cotangent, q_self, k_self, v_self, o_self, q_cross, k_cross, v_cross, o_cross, w_gate, w_up, w_down, gain_attn, gain_cross, gain_mlp):
    lens_f = text_lengths.astype(jnp.float32)
    robot = (group_map == 0).astype(jnp.float32)
    web = 1.0 - robot
    counts = jnp.stack([jnp.sum(lens_f * robot), jnp.sum(lens_f * web)])
    ratio_f = ratio.astype(jnp.float32)
    share = ratio_f / jnp.sum(ratio_f)
    group_scale = share * jnp.sum(counts) / jnp.maximum(counts, 1.0)
    example_scale = robot * group_scale[0] + web * group_scale[1]
    place = jnp.arange(SEQ, dtype=jnp.int32)
    live = (place[None, :] < text_lengths[:, None]).astype(jnp.float32)
    outer_grad = cotangent.astype(jnp.float32).reshape(EXAMPLES, SEQ, D) * (example_scale[:, None] * live)[:, :, None]
    key_ok = place[None, None, :] < text_lengths[:, None, None]
    causal = (place[None, None, :] <= place[None, :, None]) | (place[None, None, :] < prefix_lengths[:, None, None])
    allowed = (key_ok & causal)[:, None]
    image = patches.astype(jnp.float32).reshape(EXAMPLES, PATCH, D)

    def forward(rows, wqs, wks, wvs, wos, wqc, wkc, wvc, woc, wgt, wupp, wdn, gone, gtwo, gthree):
        n_attn = low(norm_rows(rows, gone))
        a_s = attention(project(n_attn, wqs), project(n_attn, wks), project(n_attn, wvs), allowed)
        x_one = rows + low_back(matmul(a_s, wos))
        n_cross = low(norm_rows(x_one, gtwo))
        a_c = attention(project(n_cross, wqc), project(image, wkc), project(image, wvc), None)
        x_two = x_one + low_back(matmul(a_c, woc))
        n_mlp = low(norm_rows(x_two, gthree))
        gate = low_back(matmul(n_mlp, wgt))
        up_proj = low_back(matmul(n_mlp, wupp))
        hidden = low(jax.nn.gelu(gate, approximate=True) * up_proj)
        return x_two + low_back(matmul(hidden, wdn))
    params = (q_self, k_self, v_self, o_self, q_cross, k_cross, v_cross, o_cross, w_gate, w_up, w_down, gain_attn, gain_cross, gain_mlp)
    params = tuple((item.astype(jnp.float32) for item in params))
    result, pull = jax.vjp(forward, tokens.astype(jnp.float32).reshape(EXAMPLES, SEQ, D), *params)
    grads = pull(outer_grad)
    return (result.reshape(TOKENS, D).astype(jnp.bfloat16), grads[0].reshape(TOKENS, D), grads[1], grads[2], grads[3], grads[4], grads[5], grads[6], grads[7], grads[8], grads[9], grads[10], grads[11], grads[12], grads[13], grads[14])
```

```python
from functools import partial

import jax
import jax.numpy as jnp
from jax import lax
from jax.experimental import pallas as pl
from jax.experimental.pallas import tpu as pltpu
from jax.sharding import PartitionSpec as P

HEAD = 64
SEQ = 128
PAIR = 2 * HEAD
epsilon = 1e-06
f32 = jnp.float32
bf16 = jnp.bfloat16
VMEM_LIMIT = 56 * 1024 * 1024


def dot_nn(left, right):
    return jnp.dot(left, right, preferred_element_type=f32)


def dot_tn(left, right):
    return lax.dot_general(left, right, (((0,), (0,)), ((), ())), preferred_element_type=f32)


def dot_nt(left, right):
    return lax.dot_general(left, right, (((1,), (1,)), ((), ())), preferred_element_type=f32)


def normalize(values_in, gain):
    row_scale = lax.rsqrt(jnp.mean(values_in * values_in, axis=-1, keepdims=True) + epsilon)
    return ((values_in * row_scale * gain).astype(bf16), row_scale)


def norm_back(values_in, row_scale, gain, incoming):
    weighted = incoming * gain
    inner = jnp.mean(weighted * values_in, axis=-1, keepdims=True)
    return (
        row_scale * weighted - values_in * row_scale**3 * inner,
        jnp.sum(incoming * values_in * row_scale, axis=0),
    )


def first_head():
    return lax.broadcasted_iota(jnp.int32, (SEQ, PAIR), 1) < HEAD


def stack_pair(rows, first):
    zero = jnp.zeros_like(rows)
    return jnp.concatenate([jnp.where(first, rows, zero), jnp.where(first, zero, rows)], axis=0)


def unstack_pair(stacked, first):
    return jnp.where(first, stacked[:SEQ], stacked[SEQ:])


def self_mask(length, prefix):
    query_at = lax.broadcasted_iota(jnp.int32, (2 * SEQ, SEQ), 0) % SEQ
    key_at = lax.broadcasted_iota(jnp.int32, (2 * SEQ, SEQ), 1)
    return (key_at < length) & ((key_at <= query_at) | (key_at < prefix))


def pair_probs(stacked_query, keys, mask):
    scores = dot_nt(stacked_query, keys)
    if mask is not None:
        scores = jnp.where(mask, scores, -1e30)
    expd = jnp.exp(scores - jnp.max(scores, axis=-1, keepdims=True))
    return expd * (1.0 / jnp.sum(expd, axis=-1, keepdims=True))


def pair_forward(query, keys, values, mask, first):
    scaled = stack_pair(query * jnp.asarray(HEAD**-0.5, bf16), first)
    probs = pair_probs(scaled, keys, mask)
    return unstack_pair(dot_nn(probs.astype(bf16), values), first).astype(bf16)


def pair_backward(grad, query, keys, values, mask, first):
    scaled = stack_pair(query * jnp.asarray(HEAD**-0.5, bf16), first)
    probs = pair_probs(scaled, keys, mask)
    grads = stack_pair(grad, first)
    d_probs = dot_nt(grads, values)
    d_scores = (
        probs * (d_probs - jnp.sum(probs * d_probs, axis=-1, keepdims=True))
    ).astype(bf16)
    d_query = unstack_pair(dot_nn(d_scores, keys), first) * HEAD**-0.5
    d_keys = dot_tn(d_scores, scaled)
    d_values = dot_tn(probs.astype(bf16), grads)
    return d_query.astype(bf16), d_keys.astype(bf16), d_values.astype(bf16)


def lanes(part, width, pair):
    return slice(part * width + pair * PAIR, part * width + (pair + 1) * PAIR)


def self_forward_kernel(length_ref, prefix_ref, qkv_ref, out_ref):
    at = pl.program_id(0)
    width = out_ref.shape[1]
    first = first_head()
    mask = self_mask(length_ref[at], prefix_ref[at])
    for pair in range(width // PAIR):
        out_ref[:, lanes(0, width, pair)] = pair_forward(
            qkv_ref[:, lanes(0, width, pair)],
            qkv_ref[:, lanes(1, width, pair)],
            qkv_ref[:, lanes(2, width, pair)],
            mask,
            first,
        )


def self_backward_kernel(length_ref, prefix_ref, qkv_ref, grad_ref, out_ref):
    at = pl.program_id(0)
    width = grad_ref.shape[1]
    first = first_head()
    mask = self_mask(length_ref[at], prefix_ref[at])
    for pair in range(width // PAIR):
        for part, value in enumerate(
            pair_backward(
                grad_ref[:, lanes(0, width, pair)],
                qkv_ref[:, lanes(0, width, pair)],
                qkv_ref[:, lanes(1, width, pair)],
                qkv_ref[:, lanes(2, width, pair)],
                mask,
                first,
            )
        ):
            out_ref[:, lanes(part, width, pair)] = value


def cross_forward_kernel(which_ref, query_ref, kv_ref, out_ref):
    width = out_ref.shape[1]
    first = first_head()
    for pair in range(width // PAIR):
        out_ref[:, lanes(0, width, pair)] = pair_forward(
            query_ref[:, lanes(0, width, pair)],
            kv_ref[:, lanes(0, width, pair)],
            kv_ref[:, lanes(1, width, pair)],
            None,
            first,
        )


def cross_backward_kernel(which_ref, query_ref, kv_ref, grad_ref, *rest):
    d_query_ref, d_kv_ref = rest[-2:]
    width = query_ref.shape[1]
    first = first_head()
    for pair in range(width // PAIR):
        d_query, d_keys, d_values = pair_backward(
            grad_ref[:, lanes(0, width, pair)],
            query_ref[:, lanes(0, width, pair)],
            kv_ref[:, lanes(0, width, pair)],
            kv_ref[:, lanes(1, width, pair)],
            None,
            first,
        )
        d_query_ref[:, lanes(0, width, pair)] = d_query
        d_kv_ref[:, lanes(0, width, pair)] = d_keys
        d_kv_ref[:, lanes(1, width, pair)] = d_values


def params():
    return pltpu.CompilerParams(vmem_limit_bytes=VMEM_LIMIT)


def by_row(width):
    return pl.BlockSpec((SEQ, width), lambda i, *_: (i, 0))


def attention_cost(examples, width, keys, dots, moved):
    return pl.CostEstimate(
        flops=dots * 2 * examples * SEQ * keys * width * 2,
        bytes_accessed=moved,
        transcendentals=examples * SEQ * keys * width // HEAD,
    )


def self_forward(qkv, length, prefix):
    rows, triple = qkv.shape
    width = triple // 3
    return pl.pallas_call(
        self_forward_kernel,
        grid_spec=pltpu.PrefetchScalarGridSpec(
            num_scalar_prefetch=2,
            grid=(rows // SEQ,),
            in_specs=[by_row(triple)],
            out_specs=by_row(width),
        ),
        out_shape=jax.ShapeDtypeStruct((rows, width), bf16),
        compiler_params=params(),
        cost_estimate=attention_cost(rows // SEQ, width, SEQ, 2, rows * width * 8),
    )(length, prefix, qkv)


def self_backward(qkv, grad, length, prefix):
    rows, triple = qkv.shape
    width = triple // 3
    return pl.pallas_call(
        self_backward_kernel,
        grid_spec=pltpu.PrefetchScalarGridSpec(
            num_scalar_prefetch=2,
            grid=(rows // SEQ,),
            in_specs=[by_row(triple), by_row(width)],
            out_specs=by_row(triple),
        ),
        out_shape=jax.ShapeDtypeStruct((rows, triple), bf16),
        compiler_params=params(),
        cost_estimate=attention_cost(rows // SEQ, width, SEQ, 5, rows * width * 14),
    )(length, prefix, qkv, grad)


def cross_forward(query, kv, which, patch):
    rows, width = query.shape
    return pl.pallas_call(
        cross_forward_kernel,
        grid_spec=pltpu.PrefetchScalarGridSpec(
            num_scalar_prefetch=1,
            grid=(rows // SEQ,),
            in_specs=[
                by_row(width),
                pl.BlockSpec((patch, 2 * width), lambda i, which: (which[i], 0)),
            ],
            out_specs=by_row(width),
        ),
        out_shape=jax.ShapeDtypeStruct((rows, width), bf16),
        compiler_params=params(),
        cost_estimate=attention_cost(rows // SEQ, width, patch, 2, rows * width * 12),
    )(which, query, kv)


def cross_backward(query, kv, grad, which, patch, earlier):
    rows, width = query.shape
    kv_spec = pl.BlockSpec((patch, 2 * width), lambda i, which: (which[i], 0))
    in_specs = [by_row(width), kv_spec, by_row(width)]
    operands = [which, query, kv, grad]
    aliases = {}
    if earlier is not None:
        in_specs.append(pl.BlockSpec(memory_space=pl.ANY))
        aliases = {len(operands): 1}
        operands.append(earlier)
    return pl.pallas_call(
        cross_backward_kernel,
        grid_spec=pltpu.PrefetchScalarGridSpec(
            num_scalar_prefetch=1,
            grid=(rows // SEQ,),
            in_specs=in_specs,
            out_specs=[by_row(width), kv_spec],
        ),
        out_shape=[
            jax.ShapeDtypeStruct((rows, width), bf16),
            jax.ShapeDtypeStruct(kv.shape, bf16),
        ],
        input_output_aliases=aliases,
        compiler_params=params(),
        cost_estimate=attention_cost(rows // SEQ, width, patch, 5, rows * width * 24),
    )(*operands)


def mlp_kernel(norm_ref, grad_ref, gate_ref, up_ref, down_ref, hidden_ref, d_gate_ref, d_up_ref):
    rows = norm_ref.shape[0]
    step = min(rows, 256)
    curve = 0.7978845608028654
    for start in range(0, rows, step):
        at = slice(start, start + step)
        gate = dot_nn(norm_ref[at, :], gate_ref[...])
        up = dot_nn(norm_ref[at, :], up_ref[...])
        d_hidden = dot_nt(grad_ref[at, :], down_ref[...])
        square = gate * gate
        bend = jnp.tanh(curve * gate * (1.0 + 0.044715 * square))
        half = 0.5 * (1.0 + bend)
        value = gate * half
        slope = half + 0.5 * curve * gate * (1.0 - bend * bend) * (1.0 + 0.134145 * square)
        hidden_ref[at, :] = (value * up).astype(bf16)
        d_gate_ref[at, :] = (d_hidden * up * slope).astype(bf16)
        d_up_ref[at, :] = (d_hidden * value).astype(bf16)


def mlp(norm, grad, w_gate, w_up, w_down):
    rows, model = norm.shape
    units = w_gate.shape[1]
    tile = 256 if units % 256 == 0 else units
    whole = pl.BlockSpec((rows, model), lambda i: (0, 0))
    columns = pl.BlockSpec((model, tile), lambda i: (0, i))
    out = pl.BlockSpec((rows, tile), lambda i: (0, i))
    shape = jax.ShapeDtypeStruct((rows, units), bf16)
    return pl.pallas_call(
        mlp_kernel,
        grid=(units // tile,),
        in_specs=[whole, whole, columns, columns, pl.BlockSpec((tile, model), lambda i: (i, 0))],
        out_specs=[out, out, out],
        out_shape=[shape, shape, shape],
        compiler_params=params(),
        cost_estimate=pl.CostEstimate(
            flops=6 * rows * model * units,
            bytes_accessed=4 * rows * model + 6 * model * units + 6 * rows * units,
            transcendentals=rows * units,
        ),
    )(norm, grad, w_gate, w_up, w_down)


def flip(tensor, axis, bit):
    count = lax.axis_size(axis)
    return lax.ppermute(tensor, axis, [(i, i ^ bit) for i in range(count)])


def butterfly(tensor, axis):
    count = lax.axis_size(axis)
    if count & (count - 1):
        return lax.psum(tensor, axis)
    bit = 1
    while bit < count:
        tensor = tensor + flip(tensor, axis, bit)
        bit *= 2
    return tensor


def block_owners():
    count = lax.axis_size("mp")
    if count == 4:
        me = lax.axis_index("mp")
        return jnp.stack([me, me ^ 2, me ^ 1, me ^ 3])
    return jnp.arange(count, dtype=jnp.int32)


def gather(rows_local):
    if lax.axis_size("mp") != 4:
        return lax.all_gather(rows_local, "mp", axis=0, tiled=True)
    across = flip(rows_local, "mp", 2)
    beside = flip(rows_local, "mp", 1)
    corner = flip(across, "mp", 1)
    return jnp.concatenate([rows_local, across, beside, corner], axis=0)


def scatter(product, rows, wide):
    count = lax.axis_size("mp")
    if count != 4:
        term = product(0, rows * count)
        term = term if wide else term.astype(bf16)
        return lax.psum_scatter(term, "mp", scatter_dimension=0, tiled=True).astype(f32)
    given = flip(product(2 * rows, 4 * rows).astype(bf16), "mp", 1)
    kept = product(0, 2 * rows) + given.astype(f32)
    return kept[:rows] + flip(kept[rows:].astype(bf16), "mp", 2).astype(f32)


def pairs(line, across=False):
    return [(a * 2 + y, b * 2 + (1 - y if across else y)) for a, b in line for y in (0, 1)]


Y_ALL = pairs([(z, z) for z in range(4)], True)
Y_INNER = pairs([(1, 1), (2, 2)], True)
INWARD = pairs([(0, 1), (3, 2)])
MIDDLE = pairs([(1, 2), (2, 1)])
OUTWARD = pairs([(1, 0), (2, 3)])


def send(tensor, which):
    return lax.ppermute(tensor, "dp", which)


def plus(left, right):
    return (left.astype(f32) + right.astype(f32)).astype(bf16)


def cut(tensor, index):
    both = tensor.reshape(2, tensor.shape[0] // 2, tensor.shape[1])
    return (
        lax.dynamic_index_in_dim(both, index, 0, False),
        lax.dynamic_index_in_dim(both, 1 - index, 0, False),
    )


def join(mine, other, index):
    return jnp.concatenate(
        [jnp.where(index == 0, mine, other), jnp.where(index == 0, other, mine)], axis=0
    )


def sum_y_first(tensor):
    at = lax.axis_index("dp")
    y, z = at % 2, at // 2
    mine, other = cut(tensor, y)
    total = plus(mine, send(other, Y_ALL))
    total = plus(total, send(total, INWARD))
    total = plus(total, send(total, MIDDLE))
    total = jnp.where((z == 1) | (z == 2), total, send(total, OUTWARD))
    return join(total, send(total, Y_ALL), y)


def sum_z_first(tensor):
    at = lax.axis_index("dp")
    z = at // 2
    side = (z == 2).astype(jnp.int32)
    total = plus(tensor, send(tensor, INWARD))
    mine, other = cut(total, side)
    mine = plus(mine, send(other, MIDDLE))
    mine = plus(mine, send(mine, Y_INNER))
    total = join(mine, send(mine, MIDDLE), side)
    return jnp.where((z == 1) | (z == 2), total, send(total, OUTWARD))


def sum_dp(tensor, y_first):
    tensor = tensor.astype(bf16)
    if lax.axis_size("dp") != 8:
        return lax.psum(tensor, "dp").astype(f32)
    return (sum_y_first if y_first else sum_z_first)(tensor).astype(f32)


def on_device(
    tokens,
    patches,
    text_lengths,
    prefix_lengths,
    group_map,
    ratio,
    cotangent,
    q_self,
    k_self,
    v_self,
    o_self,
    q_cross,
    k_cross,
    v_cross,
    o_cross,
    w_gate,
    w_up,
    w_down,
    gain_attn,
    gain_cross,
    gain_mlp,
):
    local_rows = tokens.shape[0]
    examples = text_lengths.shape[0]
    patch = patches.shape[0] // examples
    local_examples = local_rows // SEQ
    batches = 2 if local_examples % 2 == 0 else 1
    each = local_examples // batches
    rows = each * SEQ
    width = q_self.shape[1]

    lens_f = text_lengths.astype(f32)
    robot = (group_map == 0).astype(f32)
    web = 1.0 - robot
    local_counts = jnp.stack([jnp.sum(lens_f * robot), jnp.sum(lens_f * web)])
    counts = butterfly(jnp.broadcast_to(local_counts[:, None], (2, 128)), "dp")[:, 0]
    ratio_f = ratio.astype(f32)
    share = ratio_f / jnp.sum(ratio_f)
    group_scale = share * jnp.sum(counts) / jnp.maximum(counts, 1.0)
    example_scale = robot * group_scale[0] + web * group_scale[1]
    mine = lax.axis_index("mp") * local_examples
    own_scale = lax.dynamic_slice_in_dim(example_scale, mine, local_examples, 0)
    own_length = lax.dynamic_slice_in_dim(text_lengths, mine, local_examples, 0)
    place = jnp.arange(SEQ, dtype=jnp.int32)
    live = (place[None, :] < own_length[:, None]).astype(f32)
    row_weight = (own_scale[:, None] * live).reshape(local_rows)

    owners = block_owners()
    which, lengths, prefixes = [], [], []
    for b in range(batches):
        ids = (
            owners[:, None] * local_examples + b * each + jnp.arange(each, dtype=jnp.int32)[None, :]
        ).reshape(-1).astype(jnp.int32)
        which.append(ids)
        lengths.append(jnp.take(text_lengths, ids))
        prefixes.append(jnp.take(prefix_lengths, ids))

    w_qkv = jnp.concatenate([q_self, k_self, v_self], axis=1)
    w_kv = jnp.concatenate([k_cross, v_cross], axis=1)

    each_batch = range(batches)

    def part(tensor, b):
        return tensor[b * rows : (b + 1) * rows]

    def product(left, right, dot):
        return lambda low, high: dot(left[low:high], right)

    outer = [part(cotangent, b).astype(f32) * part(row_weight, b)[:, None] for b in each_batch]
    x_zero = [part(tokens, b).astype(f32) for b in each_batch]

    norm_one = [normalize(x_zero[b], gain_attn) for b in each_batch]
    full_one = [gather(norm_one[b][0]) for b in each_batch]
    qkv = [dot_nn(full_one[b], w_qkv).astype(bf16) for b in each_batch]
    mixed_self = [self_forward(qkv[b], lengths[b], prefixes[b]) for b in each_batch]
    x_one = [
        x_zero[b] + scatter(product(mixed_self[b], o_self, dot_nn), rows, True) for b in each_batch
    ]
    norm_two = [normalize(x_one[b], gain_cross) for b in each_batch]
    full_two = [gather(norm_two[b][0]) for b in each_batch]
    query = [dot_nn(full_two[b], q_cross).astype(bf16) for b in each_batch]
    kv = dot_nn(patches, w_kv).astype(bf16)
    mixed_cross = [cross_forward(query[b], kv, which[b], patch) for b in each_batch]
    x_two = [
        x_one[b] + scatter(product(mixed_cross[b], o_cross, dot_nn), rows, True)
        for b in each_batch
    ]
    norm_three = [normalize(x_two[b], gain_mlp) for b in each_batch]
    full_three = [gather(norm_three[b][0]) for b in each_batch]
    grad_three = [gather(outer[b].astype(bf16)) for b in each_batch]
    hidden, d_gate, d_up = zip(
        *[mlp(full_three[b], grad_three[b], w_gate, w_up, w_down) for b in each_batch]
    )

    def weight_grad(left, right):
        return sum(dot_tn(left[b], right[b]) for b in each_batch)

    d_wdown = sum_dp(weight_grad(hidden, grad_three), False)
    d_wgate = sum_dp(weight_grad(full_three, d_gate), True)
    d_wup = sum_dp(weight_grad(full_three, d_up), False)

    def mlp_back(b):
        return lambda low, high: (
            dot_nt(d_gate[b][low:high], w_gate) + dot_nt(d_up[b][low:high], w_up)
        )

    back = [
        norm_back(x_two[b], norm_three[b][1], gain_mlp, scatter(mlp_back(b), rows, False))
        for b in each_batch
    ]
    d_gain_mlp = sum(item[1] for item in back)
    grad_two_rows = [outer[b] + back[b][0] for b in each_batch]
    grad_two = [gather(grad_two_rows[b].astype(bf16)) for b in each_batch]
    d_ocross = sum_dp(weight_grad(mixed_cross, grad_two), True)
    d_mixed_cross = [dot_nt(grad_two[b], o_cross).astype(bf16) for b in each_batch]
    d_query, d_kv = [], None
    for b in each_batch:
        dq, d_kv = cross_backward(query[b], kv, d_mixed_cross[b], which[b], patch, d_kv)
        d_query.append(dq)
    d_qcross = sum_dp(weight_grad(full_two, d_query), False)
    d_wkv = sum_dp(dot_tn(patches, d_kv), True)

    back = [
        norm_back(
            x_one[b],
            norm_two[b][1],
            gain_cross,
            scatter(product(d_query[b], q_cross, dot_nt), rows, False),
        )
        for b in each_batch
    ]
    d_gain_cross = sum(item[1] for item in back)
    grad_one_rows = [grad_two_rows[b] + back[b][0] for b in each_batch]
    grad_one = [gather(grad_one_rows[b].astype(bf16)) for b in each_batch]
    d_oself = sum_dp(weight_grad(mixed_self, grad_one), False)
    d_mixed_self = [dot_nt(grad_one[b], o_self).astype(bf16) for b in each_batch]
    d_qkv = [
        self_backward(qkv[b], d_mixed_self[b], lengths[b], prefixes[b]) for b in each_batch
    ]
    d_wqkv = sum_dp(weight_grad(full_one, d_qkv), True)

    back = [
        norm_back(
            x_zero[b],
            norm_one[b][1],
            gain_attn,
            scatter(product(d_qkv[b], w_qkv, dot_nt), rows, False),
        )
        for b in each_batch
    ]
    d_gain_attn = sum(item[1] for item in back)
    grad_input = jnp.concatenate([grad_one_rows[b] + back[b][0] for b in each_batch], axis=0)
    output = jnp.concatenate(
        [
            (x_two[b] + scatter(product(hidden[b], w_down, dot_nn), rows, True)).astype(bf16)
            for b in each_batch
        ],
        axis=0,
    )
    gains = butterfly(butterfly(jnp.stack([d_gain_attn, d_gain_cross, d_gain_mlp]), "mp"), "dp")
    return (
        output,
        grad_input,
        d_wqkv[:, :width],
        d_wqkv[:, width : 2 * width],
        d_wqkv[:, 2 * width :],
        d_oself,
        d_qcross,
        d_wkv[:, :width],
        d_wkv[:, width:],
        d_ocross,
        d_wgate,
        d_wup,
        d_wdown,
        gains[0],
        gains[1],
        gains[2],
    )


def solution(mesh):
    by_rows = P(("dp", "mp"), None)
    columns = P(None, "mp")
    rows = P("mp", None)
    weights = (columns, columns, columns, rows, columns, columns, columns, rows, columns, columns, rows)
    in_specs = (
        (by_rows, P("dp", None), P("dp"), P("dp"), P("dp"), P(), by_rows) + weights + (P(), P(), P())
    )
    out_specs = (by_rows, by_rows) + weights + (P(), P(), P())
    return jax.shard_map(
        on_device, mesh=mesh, in_specs=in_specs, out_specs=out_specs, check_vma=False
    )
```

```python
from functools import partial

import jax
import jax.numpy as jnp
from jax import lax
from jax.experimental import pallas as pl
from jax.experimental.pallas import tpu as pltpu
from jax.sharding import PartitionSpec as P

HEAD = 64
SEQ = 128
PAIR = 2 * HEAD
epsilon = 1e-06
f32 = jnp.float32
bf16 = jnp.bfloat16
VMEM_LIMIT = 56 * 1024 * 1024
MESH = pl.DeviceIdType.MESH


def dot_nn(left, right):
    return jnp.dot(left, right, preferred_element_type=f32)


def dot_tn(left, right):
    return lax.dot_general(left, right, (((0,), (0,)), ((), ())), preferred_element_type=f32)


def dot_nt(left, right):
    return lax.dot_general(left, right, (((1,), (1,)), ((), ())), preferred_element_type=f32)


def normalize(values_in, gain):
    row_scale = lax.rsqrt(jnp.mean(values_in * values_in, axis=-1, keepdims=True) + epsilon)
    return ((values_in * row_scale * gain).astype(bf16), row_scale)


def norm_back(values_in, row_scale, gain, incoming):
    weighted = incoming * gain
    inner = jnp.mean(weighted * values_in, axis=-1, keepdims=True)
    return (
        row_scale * weighted - values_in * row_scale**3 * inner,
        jnp.sum(incoming * values_in * row_scale, axis=0),
    )


def first_head():
    return lax.broadcasted_iota(jnp.int32, (SEQ, PAIR), 1) < HEAD


def stack_pair(rows, first):
    zero = jnp.zeros_like(rows)
    return jnp.concatenate([jnp.where(first, rows, zero), jnp.where(first, zero, rows)], axis=0)


def unstack_pair(stacked, first):
    return jnp.where(first, stacked[:SEQ], stacked[SEQ:])


def self_mask(length, prefix):
    query_at = lax.broadcasted_iota(jnp.int32, (2 * SEQ, SEQ), 0) % SEQ
    key_at = lax.broadcasted_iota(jnp.int32, (2 * SEQ, SEQ), 1)
    return (key_at < length) & ((key_at <= query_at) | (key_at < prefix))


def pair_probs(stacked_query, keys, mask):
    scores = dot_nt(stacked_query, keys)
    if mask is not None:
        scores = jnp.where(mask, scores, -1e30)
    expd = jnp.exp(scores - jnp.max(scores, axis=-1, keepdims=True))
    return expd * (1.0 / jnp.sum(expd, axis=-1, keepdims=True))


def pair_forward(query, keys, values, mask, first):
    scaled = stack_pair(query * jnp.asarray(HEAD**-0.5, bf16), first)
    probs = pair_probs(scaled, keys, mask)
    return unstack_pair(dot_nn(probs.astype(bf16), values), first).astype(bf16)


def pair_backward(grad, query, keys, values, mask, first):
    scaled = stack_pair(query * jnp.asarray(HEAD**-0.5, bf16), first)
    probs = pair_probs(scaled, keys, mask)
    grads = stack_pair(grad, first)
    d_probs = dot_nt(grads, values)
    d_scores = (
        probs * (d_probs - jnp.sum(probs * d_probs, axis=-1, keepdims=True))
    ).astype(bf16)
    d_query = unstack_pair(dot_nn(d_scores, keys), first) * HEAD**-0.5
    d_keys = dot_tn(d_scores, scaled)
    d_values = dot_tn(probs.astype(bf16), grads)
    return d_query.astype(bf16), d_keys.astype(bf16), d_values.astype(bf16)


def lanes(part, width, pair):
    return slice(part * width + pair * PAIR, part * width + (pair + 1) * PAIR)


def self_forward_kernel(length_ref, prefix_ref, qkv_ref, out_ref):
    at = pl.program_id(0)
    width = out_ref.shape[1]
    first = first_head()
    mask = self_mask(length_ref[at], prefix_ref[at])
    for pair in range(width // PAIR):
        out_ref[:, lanes(0, width, pair)] = pair_forward(
            qkv_ref[:, lanes(0, width, pair)],
            qkv_ref[:, lanes(1, width, pair)],
            qkv_ref[:, lanes(2, width, pair)],
            mask,
            first,
        )


def self_backward_kernel(length_ref, prefix_ref, qkv_ref, grad_ref, out_ref):
    at = pl.program_id(0)
    width = grad_ref.shape[1]
    first = first_head()
    mask = self_mask(length_ref[at], prefix_ref[at])
    for pair in range(width // PAIR):
        for part, value in enumerate(
            pair_backward(
                grad_ref[:, lanes(0, width, pair)],
                qkv_ref[:, lanes(0, width, pair)],
                qkv_ref[:, lanes(1, width, pair)],
                qkv_ref[:, lanes(2, width, pair)],
                mask,
                first,
            )
        ):
            out_ref[:, lanes(part, width, pair)] = value


def cross_forward_kernel(which_ref, query_ref, key_ref, value_ref, out_ref):
    width = out_ref.shape[1]
    first = first_head()
    for pair in range(width // PAIR):
        at = lanes(0, width, pair)
        out_ref[:, at] = pair_forward(
            query_ref[:, at], key_ref[:, at], value_ref[:, at], None, first
        )


def cross_backward_kernel(which_ref, query_ref, key_ref, value_ref, grad_ref, *rest):
    d_query_ref, d_key_ref, d_value_ref = rest[-3:]
    width = query_ref.shape[1]
    first = first_head()
    for pair in range(width // PAIR):
        at = lanes(0, width, pair)
        d_query_ref[:, at], d_key_ref[:, at], d_value_ref[:, at] = pair_backward(
            grad_ref[:, at], query_ref[:, at], key_ref[:, at], value_ref[:, at], None, first
        )


def params():
    return pltpu.CompilerParams(vmem_limit_bytes=ROOM)


def by_row(width):
    return pl.BlockSpec((SEQ, width), lambda i, *_: (i, 0))


def attention_cost(examples, width, keys, dots, moved):
    return pl.CostEstimate(
        flops=dots * 2 * examples * SEQ * keys * width * 2,
        bytes_accessed=moved,
        transcendentals=examples * SEQ * keys * width // HEAD,
    )


def self_forward(qkv, length, prefix):
    rows, triple = qkv.shape
    width = triple // 3
    return pl.pallas_call(
        self_forward_kernel,
        grid_spec=pltpu.PrefetchScalarGridSpec(
            num_scalar_prefetch=2,
            grid=(rows // SEQ,),
            in_specs=[by_row(triple)],
            out_specs=by_row(width),
        ),
        out_shape=jax.ShapeDtypeStruct((rows, width), bf16),
        compiler_params=params(),
        cost_estimate=attention_cost(rows // SEQ, width, SEQ, 2, rows * width * 8),
    )(length, prefix, qkv)


def self_backward(qkv, grad, length, prefix):
    rows, triple = qkv.shape
    width = triple // 3
    return pl.pallas_call(
        self_backward_kernel,
        grid_spec=pltpu.PrefetchScalarGridSpec(
            num_scalar_prefetch=2,
            grid=(rows // SEQ,),
            in_specs=[by_row(triple), by_row(width)],
            out_specs=by_row(triple),
        ),
        out_shape=jax.ShapeDtypeStruct((rows, triple), bf16),
        compiler_params=params(),
        cost_estimate=attention_cost(rows // SEQ, width, SEQ, 5, rows * width * 14),
    )(length, prefix, qkv, grad)


def cross_forward(query, keys, values, which, patch):
    rows, width = query.shape
    by_patch = pl.BlockSpec((patch, width), lambda i, which: (which[i], 0))
    return pl.pallas_call(
        cross_forward_kernel,
        grid_spec=pltpu.PrefetchScalarGridSpec(
            num_scalar_prefetch=1,
            grid=(rows // SEQ,),
            in_specs=[by_row(width), by_patch, by_patch],
            out_specs=by_row(width),
        ),
        out_shape=jax.ShapeDtypeStruct((rows, width), bf16),
        compiler_params=params(),
        cost_estimate=attention_cost(rows // SEQ, width, patch, 2, rows * width * 12),
    )(which, query, keys, values)


def cross_backward(query, keys, values, grad, which, patch, earlier):
    rows, width = query.shape
    by_patch = pl.BlockSpec((patch, width), lambda i, which: (which[i], 0))
    in_specs = [by_row(width), by_patch, by_patch, by_row(width)]
    operands = [which, query, keys, values, grad]
    aliases = {}
    for at, item in enumerate(earlier):
        in_specs.append(pl.BlockSpec(memory_space=pl.ANY))
        aliases[len(operands)] = 1 + at
        operands.append(item)
    whole = jax.ShapeDtypeStruct(keys.shape, bf16)
    return pl.pallas_call(
        cross_backward_kernel,
        grid_spec=pltpu.PrefetchScalarGridSpec(
            num_scalar_prefetch=1,
            grid=(rows // SEQ,),
            in_specs=in_specs,
            out_specs=[by_row(width), by_patch, by_patch],
        ),
        out_shape=[jax.ShapeDtypeStruct((rows, width), bf16), whole, whole],
        input_output_aliases=aliases,
        compiler_params=params(),
        cost_estimate=attention_cost(rows // SEQ, width, patch, 5, rows * width * 24),
    )(*operands)


def other_core():
    me = lax.axis_index("mp")
    return me + 1 - 2 * lax.rem(me, 2)


def meet(partner):
    barrier = pltpu.get_barrier_semaphore()
    pl.semaphore_signal(barrier, inc=1, device_id={"mp": partner}, device_id_type=MESH)
    pl.semaphore_wait(barrier, 1)


def to_partner(source, target, send_sem, recv_sem, partner):
    return pltpu.make_async_remote_copy(
        src_ref=source,
        dst_ref=target,
        send_sem=send_sem,
        recv_sem=recv_sem,
        device_id={"mp": partner},
        device_id_type=MESH,
    )


def columns_of(weight, tile, size, transposed):
    at = pl.ds(pl.multiple_of(tile * size, size), size)
    return weight[at, :] if transposed else weight[:, at]


def gathered_kernel(transposed, size, own, beside, across, weight, full, out, corner, sems, local):
    dot = dot_nt if transposed else dot_nn
    rows = own.shape[0]
    blocks = (own, beside, across, corner)
    partner = other_core()
    given = to_partner(across, corner, sems.at[0], sems.at[1], partner)
    keep = [
        pltpu.make_async_copy(block, full.at[pl.ds(at * rows, rows)], local.at[at])
        for at, block in enumerate(blocks)
    ]
    meet(partner)
    given.start()
    for at in range(3):
        keep[at].start()

    def multiply(places):
        @pl.loop(0, out.shape[1] // size)
        def _(tile):
            right = columns_of(weight, tile, size, transposed)
            to = pl.ds(pl.multiple_of(tile * size, size), size)
            for at in places:
                out[at * rows : (at + 1) * rows, to] = dot(blocks[at][...], right).astype(bf16)

    multiply((0, 1, 2))
    given.wait()
    keep[3].start()
    multiply((3,))
    for at in range(4):
        keep[at].wait()


IN_VMEM = pl.BlockSpec(memory_space=pltpu.VMEM)
ROOM = 24 * 1024 * 1024


def gathered_dot(own, arrived, weight, transposed, ident):
    if lax.axis_size("mp") != 4:
        dot = dot_nt if transposed else dot_nn
        return arrived, dot(arrived, weight).astype(bf16)
    across, beside = arrived
    rows, model = own.shape
    units = weight.shape[0 if transposed else 1]
    return pl.pallas_call(
        partial(gathered_kernel, transposed, 512),
        in_specs=[IN_VMEM] * 4,
        out_specs=[pl.BlockSpec(memory_space=pl.ANY), IN_VMEM],
        out_shape=[
            jax.ShapeDtypeStruct((4 * rows, model), bf16),
            jax.ShapeDtypeStruct((4 * rows, units), bf16),
        ],
        scratch_shapes=[
            pltpu.VMEM((rows, model), bf16),
            pltpu.SemaphoreType.DMA((2,)),
            pltpu.SemaphoreType.DMA((4,)),
        ],
        compiler_params=pltpu.CompilerParams(
            collective_id=ident, has_side_effects=True, vmem_limit_bytes=ROOM
        ),
        cost_estimate=pl.CostEstimate(
            flops=8 * rows * model * units,
            bytes_accessed=14 * rows * model + 4 * model * units + 8 * rows * units,
            transcendentals=0,
        ),
    )(own, beside, across, weight)


def scattered_kernel(transposed, count, size, *refs):
    dot = dot_nt if transposed else dot_nn
    lefts, weights = refs[:count], refs[count : 2 * count]
    kept, passed, ready, landed, send_sem, recv_sem = refs[2 * count :]
    rows, model = kept.shape
    tiles = model // size
    partner = other_core()

    def given(tile):
        return to_partner(
            ready.at[tile], landed.at[tile], send_sem.at[tile], recv_sem.at[tile], partner
        )

    def block(at, tile):
        return sum(
            dot(
                left[at * rows : (at + 1) * rows, :],
                columns_of(weight, tile, size, transposed),
            )
            for left, weight in zip(lefts, weights)
        )

    meet(partner)

    @pl.loop(0, tiles)
    def _(tile):
        ready[tile, :rows, :] = block(1, tile).astype(bf16)
        ready[tile, rows:, :] = block(3, tile).astype(bf16)
        given(tile).start()

    @pl.loop(0, tiles)
    def _(tile):
        mine = block(0, tile)
        across = block(2, tile)
        given(tile).wait()
        to = pl.ds(pl.multiple_of(tile * size, size), size)
        kept[:, to] = mine + landed[tile, :rows, :].astype(f32)
        passed[:, to] = (across + landed[tile, rows:, :].astype(f32)).astype(bf16)


def scattered_dot(lefts, weights, transposed, wide, ident):
    if lax.axis_size("mp") != 4:
        dot = dot_nt if transposed else dot_nn
        term = sum(dot(left, weight) for left, weight in zip(lefts, weights))
        return (term if wide else term.astype(bf16),)
    rows = lefts[0].shape[0] // 4
    model = weights[0].shape[0 if transposed else 1]
    size = 512
    tiles = model // size
    depth = sum(item.shape[1] for item in lefts)
    return pl.pallas_call(
        partial(scattered_kernel, transposed, len(lefts), size),
        in_specs=[IN_VMEM] * (2 * len(lefts)),
        out_specs=[IN_VMEM, IN_VMEM],
        out_shape=[
            jax.ShapeDtypeStruct((rows, model), f32),
            jax.ShapeDtypeStruct((rows, model), bf16),
        ],
        scratch_shapes=[
            pltpu.VMEM((tiles, 2 * rows, size), bf16),
            pltpu.VMEM((tiles, 2 * rows, size), bf16),
            pltpu.SemaphoreType.DMA((tiles,)),
            pltpu.SemaphoreType.DMA((tiles,)),
        ],
        compiler_params=pltpu.CompilerParams(
            collective_id=ident,
            has_side_effects=True,
            vmem_limit_bytes=ROOM if depth < 2048 else 2 * ROOM,
        ),
        cost_estimate=pl.CostEstimate(
            flops=8 * rows * model * depth,
            bytes_accessed=8 * rows * depth + 4 * model * depth + 14 * rows * model,
            transcendentals=0,
        ),
    )(*lefts, *weights)


def mlp_rows(norm, grad, gate_ref, up_ref, down_ref):
    curve = 0.7978845608028654
    gate = dot_nn(norm, gate_ref[...])
    up = dot_nn(norm, up_ref[...])
    d_hidden = dot_nt(grad, down_ref[...])
    square = gate * gate
    bend = jnp.tanh(curve * gate * (1.0 + 0.044715 * square))
    half = 0.5 * (1.0 + bend)
    value = gate * half
    slope = half + 0.5 * curve * gate * (1.0 - bend * bend) * (1.0 + 0.134145 * square)
    return (
        (value * up).astype(bf16),
        (d_hidden * up * slope).astype(bf16),
        (d_hidden * value).astype(bf16),
    )


def mlp_kernel(norm_ref, grad_ref, gate_ref, up_ref, down_ref, hidden_ref, d_gate_ref, d_up_ref):
    rows = norm_ref.shape[0]
    step = min(rows, 256)
    for start in range(0, rows, step):
        at = slice(start, start + step)
        hidden_ref[at, :], d_gate_ref[at, :], d_up_ref[at, :] = mlp_rows(
            norm_ref[at, :], grad_ref[at, :], gate_ref, up_ref, down_ref
        )


def gathered_mlp_kernel(tiles, *refs):
    norms, grads = refs[:3], refs[3:6]
    gate_ref, up_ref, down_ref = refs[6:9]
    full_norm, full_grad, hidden_ref, d_gate_ref, d_up_ref = refs[9:14]
    corner_norm, corner_grad, sems, local = refs[14:]
    tile = pl.program_id(0)
    rows = norms[0].shape[0]
    partner = other_core()
    norms = (*norms, corner_norm)
    grads = (*grads, corner_grad)

    def given(at):
        source, target = ((norms[2], corner_norm), (grads[2], corner_grad))[at]
        return to_partner(source, target, sems.at[2 * at], sems.at[2 * at + 1], partner)

    def keep(which, at):
        source, target = ((norms, full_norm), (grads, full_grad))[which]
        return pltpu.make_async_copy(
            source[at], target.at[pl.ds(at * rows, rows)], local.at[which, at]
        )

    @pl.when(tile == 0)
    def _():
        meet(partner)
        for which in range(2):
            given(which).start()
        for which in range(2):
            for at in range(3):
                keep(which, at).start()

    for at in range(4):
        if at == 3:

            @pl.when(tile == 0)
            def _():
                for which in range(2):
                    given(which).wait()
                    keep(which, 3).start()

        place = slice(at * rows, (at + 1) * rows)
        hidden_ref[place, :], d_gate_ref[place, :], d_up_ref[place, :] = mlp_rows(
            norms[at][...], grads[at][...], gate_ref, up_ref, down_ref
        )

    @pl.when(tile == tiles - 1)
    def _():
        for which in range(2):
            for at in range(4):
                keep(which, at).wait()


def gathered_mlp(own_norm, arrived_norm, own_grad, arrived_grad, w_gate, w_up, w_down, ident):
    model, units = w_gate.shape
    if lax.axis_size("mp") != 4:
        return (
            arrived_norm,
            arrived_grad,
            *mlp(arrived_norm, arrived_grad, w_gate, w_up, w_down),
        )
    rows = own_norm.shape[0]
    tile = 256
    whole = pl.BlockSpec((rows, model), lambda i: (0, 0))
    columns = pl.BlockSpec((model, tile), lambda i: (0, i))
    out = pl.BlockSpec((4 * rows, tile), lambda i: (0, i))
    full = pl.BlockSpec(memory_space=pl.ANY)
    shape = jax.ShapeDtypeStruct((4 * rows, units), bf16)
    full_shape = jax.ShapeDtypeStruct((4 * rows, model), bf16)
    return pl.pallas_call(
        partial(gathered_mlp_kernel, units // tile),
        grid=(units // tile,),
        in_specs=[whole] * 6 + [columns, columns, pl.BlockSpec((tile, model), lambda i: (i, 0))],
        out_specs=[full, full, out, out, out],
        out_shape=[full_shape, full_shape, shape, shape, shape],
        scratch_shapes=[
            pltpu.VMEM((rows, model), bf16),
            pltpu.VMEM((rows, model), bf16),
            pltpu.SemaphoreType.DMA((4,)),
            pltpu.SemaphoreType.DMA((2, 4)),
        ],
        compiler_params=pltpu.CompilerParams(
            collective_id=ident, has_side_effects=True, vmem_limit_bytes=VMEM_LIMIT
        ),
        cost_estimate=pl.CostEstimate(
            flops=24 * rows * model * units,
            bytes_accessed=28 * rows * model + 6 * model * units + 24 * rows * units,
            transcendentals=4 * rows * units,
        ),
    )(
        own_norm,
        arrived_norm[1],
        arrived_norm[0],
        own_grad,
        arrived_grad[1],
        arrived_grad[0],
        w_gate,
        w_up,
        w_down,
    )


def mlp(norm, grad, w_gate, w_up, w_down):
    rows, model = norm.shape
    units = w_gate.shape[1]
    tile = 256 if units % 256 == 0 else units
    whole = pl.BlockSpec((rows, model), lambda i: (0, 0))
    columns = pl.BlockSpec((model, tile), lambda i: (0, i))
    out = pl.BlockSpec((rows, tile), lambda i: (0, i))
    shape = jax.ShapeDtypeStruct((rows, units), bf16)
    return pl.pallas_call(
        mlp_kernel,
        grid=(units // tile,),
        in_specs=[whole, whole, columns, columns, pl.BlockSpec((tile, model), lambda i: (i, 0))],
        out_specs=[out, out, out],
        out_shape=[shape, shape, shape],
        compiler_params=params(),
        cost_estimate=pl.CostEstimate(
            flops=6 * rows * model * units,
            bytes_accessed=4 * rows * model + 6 * model * units + 6 * rows * units,
            transcendentals=rows * units,
        ),
    )(norm, grad, w_gate, w_up, w_down)


def flip(tensor, axis, bit):
    count = lax.axis_size(axis)
    return lax.ppermute(tensor, axis, [(i, i ^ bit) for i in range(count)])


def butterfly(tensor, axis):
    count = lax.axis_size(axis)
    if count & (count - 1):
        return lax.psum(tensor, axis)
    bit = 1
    while bit < count:
        tensor = tensor + flip(tensor, axis, bit)
        bit *= 2
    return tensor


def block_owners():
    blocks = jnp.arange(lax.axis_size("mp"), dtype=jnp.int32)
    return lax.axis_index("mp") ^ blocks if lax.axis_size("mp") == 4 else blocks


def fence(*values):
    return lax.optimization_barrier(values)


def gather_start(rows_local):
    if lax.axis_size("mp") != 4:
        return lax.all_gather(rows_local, "mp", axis=0, tiled=True)
    return flip(rows_local, "mp", 2), flip(rows_local, "mp", 1)


def scatter_move(sent):
    if lax.axis_size("mp") != 4:
        return None, lax.psum_scatter(sent[0], "mp", scatter_dimension=0, tiled=True)
    return sent[0], flip(sent[1], "mp", 2)


def scatter_end(arrived):
    if lax.axis_size("mp") != 4:
        return arrived[1].astype(f32)
    return arrived[0] + arrived[1].astype(f32)


CHUNK = 128
WIDE = 512
CYCLE = 4
LANDINGS = 7


class Late:
    def __init__(self, make):
        self.make = make

    def start(self):
        self.make().start()

    def wait(self):
        self.make().wait()

    def wait_send(self):
        self.make().wait_send()

    def wait_recv(self):
        self.make().wait_recv()


def sum_kernel(cycles, x_ref, out_ref, land, send_sem, recv_sem, local_sem):
    at = lax.axis_index("dp")
    y = lax.rem(at, 2)
    z = lax.div(at, 2)
    inner = (z == 1) | (z == 2)
    outer = (z == 0) | (z == 3)
    beside = z * 2 + (1 - y)
    along = at + jnp.where(lax.rem(z, 2) == 0, 2, -2)
    facing = (3 - z) * 2 + y
    side = z - 1

    barrier = pltpu.get_barrier_semaphore()

    def greet(target):
        pl.semaphore_signal(barrier, inc=1, device_id={"dp": target}, device_id_type=MESH)

    greet(beside)
    greet(along)

    @pl.when(inner)
    def _():
        greet(facing)
        pl.semaphore_wait(barrier, 3)

    @pl.when(outer)
    def _():
        pl.semaphore_wait(barrier, 2)

    def row(stream, cycle, index):
        start = ((stream * cycles + cycle) * CYCLE + index) * CHUNK
        return pl.ds(pl.multiple_of(start, CHUNK), CHUNK)

    def remote(stream, cycle, slot, source, target, device):
        return Late(
            lambda: pltpu.make_async_remote_copy(
                src_ref=source,
                dst_ref=target,
                send_sem=send_sem.at[stream, cycle, slot],
                recv_sem=recv_sem.at[stream, cycle, slot],
                device_id={"dp": device},
                device_id_type=MESH,
            )
        )

    def add(place, landing):
        @pl.loop(0, CHUNK // 32)
        def _(step):
            rows = pl.ds(pl.multiple_of(step * 32, 32), 32)
            x = x_ref.at[place]
            x[rows, :] = (x[rows, :].astype(f32) + landing[rows, :].astype(f32)).astype(bf16)

    def stages(stream, cycle):
        mine = row(stream, cycle, y)
        other = row(stream, cycle, 1 - y)
        low = row(stream, cycle, 2)
        high = row(stream, cycle, 3)
        own = row(stream, cycle, 2 + side)
        given = row(stream, cycle, 3 - side)
        landing = [land.at[stream, cycle, i] for i in range(LANDINGS)]

        def copy(slot, source, target, device):
            return remote(stream, cycle, slot, source, target, device)

        def keep(place, slot):
            return Late(
                lambda: pltpu.make_async_copy(
                    x_ref.at[place], out_ref.at[place], local_sem.at[stream, cycle, slot]
                )
            )

        def everyone(descriptor, after):
            def finish():
                descriptor.wait()
                after()

            return descriptor.start, finish

        def inward(descriptor, place, landed):
            def start():
                pl.when(outer)(descriptor.start)

            def finish():
                pl.when(outer)(descriptor.wait_send)

                @pl.when(inner)
                def _():
                    descriptor.wait_recv()
                    add(place, landed)

            return start, finish

        def between(descriptor, after, local=None):
            def start():
                @pl.when(inner)
                def _():
                    descriptor.start()
                    if local is not None:
                        local.start()

            def finish():
                @pl.when(inner)
                def _():
                    descriptor.wait()
                    if local is not None:
                        local.wait()
                    after()

            return start, finish

        def outward(descriptor, local=None):
            def start():
                @pl.when(inner)
                def _():
                    descriptor.start()
                    if local is not None:
                        local.start()

            def finish():
                @pl.when(inner)
                def _():
                    descriptor.wait_send()
                    if local is not None:
                        local.wait()

                pl.when(outer)(descriptor.wait_recv)

            return start, finish

        def nothing():
            return None

        x, out = x_ref, out_ref
        return [
            (0, inward(copy(0, x.at[low], landing[0], along), low, landing[0])),
            (1, inward(copy(1, x.at[high], landing[1], along), high, landing[1])),
            (2, between(copy(2, x.at[given], landing[2], facing), lambda: add(own, landing[2]))),
            (3, between(copy(3, x.at[own], landing[3], beside), lambda: add(own, landing[3]))),
            (4, between(copy(4, x.at[own], out.at[own], facing), nothing, keep(own, 0))),
            (5, outward(copy(5, out.at[low], out.at[low], along))),
            (6, outward(copy(6, out.at[high], out.at[high], along))),
            (1, everyone(copy(7, x.at[other], landing[4], beside), lambda: add(mine, landing[4]))),
            (2, inward(copy(8, x.at[mine], landing[5], along), mine, landing[5])),
            (3, between(copy(9, x.at[mine], landing[6], facing), lambda: add(mine, landing[6]))),
            (4, outward(copy(10, x.at[mine], out.at[mine], along), keep(mine, 1))),
            (5, everyone(copy(11, out.at[mine], out.at[mine], beside), nothing)),
        ]

    def body(step, carry):
        for phase in range(3):
            for stream in range(2):

                def each(back, offset, what):
                    cycle = step - back

                    @pl.when((cycle >= 0) & (cycle < cycles))
                    def _():
                        for when, (start, finish) in stages(stream, cycle):
                            if when == offset:
                                (start if what == 0 else finish)()

                for offset in range(7):
                    if (offset + 1) % 3 == phase:
                        each((offset + 1) // 3, offset, 1)
                for offset in range(7):
                    if offset % 3 == phase:
                        each(offset // 3, offset, 0)
        return carry

    lax.fori_loop(0, cycles + 3, body, 0)


def sum_chunks(stack):
    cycles = stack.shape[0] // (CHUNK * CYCLE * 2)
    size = stack.shape[0] * WIDE * 2
    return pl.pallas_call(
        partial(sum_kernel, cycles),
        in_specs=[pl.BlockSpec(memory_space=pltpu.VMEM)],
        out_specs=pl.BlockSpec(memory_space=pl.ANY),
        out_shape=jax.ShapeDtypeStruct(stack.shape, bf16),
        scratch_shapes=[
            pltpu.VMEM((2, cycles, LANDINGS, CHUNK, WIDE), bf16),
            pltpu.SemaphoreType.DMA((2, cycles, 12)),
            pltpu.SemaphoreType.DMA((2, cycles, 12)),
            pltpu.SemaphoreType.DMA((2, cycles, 2)),
        ],
        compiler_params=pltpu.CompilerParams(
            collective_id=0, has_side_effects=True, vmem_limit_bytes=63 * 1024 * 1024
        ),
        cost_estimate=pl.CostEstimate(
            flops=size, bytes_accessed=4 * size, transcendentals=0
        ),
    )(stack)


def to_chunks(tensor):
    height, width = tensor.shape
    return [tensor[:, at : at + WIDE] for at in range(0, width, WIDE)]


def chunked(tensors):
    size = sum(item.size for item in tensors)
    fits = size % (CHUNK * WIDE * CYCLE * 2) == 0 and all(
        item.shape[0] % CHUNK == 0 and item.shape[1] % WIDE == 0 for item in tensors
    )
    return lax.axis_size("dp") == 8 and fits


def sum_dp_start(tensors):
    low = [item.astype(bf16) for item in tensors]
    if not chunked(low):
        return lax.psum(low, "dp")
    return sum_chunks(jnp.concatenate([piece for item in low for piece in to_chunks(item)], axis=0))


def sum_dp_end(total, tensors):
    if not chunked(tensors):
        return [item.astype(f32) for item in total]
    out, at = [], 0
    for item in tensors:
        height, width = item.shape
        pieces = []
        for _ in range(width // WIDE):
            pieces.append(total[at : at + height])
            at += height
        out.append(jnp.concatenate(pieces, axis=1).astype(f32))
    return out


def on_device(
    tokens,
    patches,
    text_lengths,
    prefix_lengths,
    group_map,
    ratio,
    cotangent,
    q_self,
    k_self,
    v_self,
    o_self,
    q_cross,
    k_cross,
    v_cross,
    o_cross,
    w_gate,
    w_up,
    w_down,
    gain_attn,
    gain_cross,
    gain_mlp,
):
    local_rows = tokens.shape[0]
    examples = text_lengths.shape[0]
    patch = patches.shape[0] // examples
    local_examples = local_rows // SEQ
    batches = 2 if local_examples % 2 == 0 else 1
    each = local_examples // batches
    rows = each * SEQ
    width = q_self.shape[1]

    lens_f = text_lengths.astype(f32)
    robot = (group_map == 0).astype(f32)
    web = 1.0 - robot
    local_counts = jnp.stack([jnp.sum(lens_f * robot), jnp.sum(lens_f * web)])
    counts = butterfly(jnp.broadcast_to(local_counts[:, None], (2, 128)), "dp")[:, 0]
    ratio_f = ratio.astype(f32)
    share = ratio_f / jnp.sum(ratio_f)
    group_scale = share * jnp.sum(counts) / jnp.maximum(counts, 1.0)
    example_scale = robot * group_scale[0] + web * group_scale[1]
    mine = lax.axis_index("mp") * local_examples
    own_scale = lax.dynamic_slice_in_dim(example_scale, mine, local_examples, 0)
    own_length = lax.dynamic_slice_in_dim(text_lengths, mine, local_examples, 0)
    place = jnp.arange(SEQ, dtype=jnp.int32)
    live = (place[None, :] < own_length[:, None]).astype(f32)
    row_weight = (own_scale[:, None] * live).reshape(local_rows)

    owners = block_owners()
    which, lengths, prefixes = [], [], []
    for b in range(batches):
        ids = (
            owners[:, None] * local_examples + b * each + jnp.arange(each, dtype=jnp.int32)[None, :]
        ).reshape(-1).astype(jnp.int32)
        which.append(ids)
        lengths.append(jnp.take(text_lengths, ids))
        prefixes.append(jnp.take(prefix_lengths, ids))

    w_qkv = jnp.concatenate([q_self, k_self, v_self], axis=1)

    each_batch = range(batches)
    last = batches - 1

    def part(tensor, b):
        return tensor[b * rows : (b + 1) * rows]

    def product(left, right, dot):
        return lambda low, high: dot(left[low:high], right)

    outer = [part(cotangent, b).astype(f32) * part(row_weight, b)[:, None] for b in each_batch]
    outer_low = [item.astype(bf16) for item in outer]
    x_zero = [part(tokens, b).astype(f32) for b in each_batch]
    norm_one = [normalize(x_zero[b], gain_attn) for b in each_batch]
    scale_one = [item[1] for item in norm_one]
    norm_one = [item[0] for item in norm_one]

    none = [None] * batches
    full_one, qkv, mixed_self, x_one, norm_two, scale_two = ([None] * batches for _ in range(6))
    full_two, query, mixed_cross, x_two, norm_three, scale_three = (
        [None] * batches for _ in range(6)
    )
    full_three, grad_three, hidden, d_gate, d_up, back_three = ([None] * batches for _ in range(6))
    grad_two_rows, grad_two, d_query, grad_one_rows, grad_one, d_qkv = (
        [None] * batches for _ in range(6)
    )
    gain_mlp_parts, gain_cross_parts, gain_attn_parts, grad_input, output = (
        [None] * batches for _ in range(5)
    )

    def self_block(b, arrived):
        full_one[b], qkv[b] = gathered_dot(norm_one[b], arrived, w_qkv, False, 1)
        mixed_self[b] = self_forward(qkv[b], lengths[b], prefixes[b])
        return scattered_dot([mixed_self[b]], [o_self], False, True, 2)

    def self_norm(b, arrived):
        x_one[b] = x_zero[b] + scatter_end(arrived)
        norm_two[b], scale_two[b] = normalize(x_one[b], gain_cross)

    def cross_block(b, arrived, keys, values):
        full_two[b], query[b] = gathered_dot(norm_two[b], arrived, q_cross, False, 3)
        mixed_cross[b] = cross_forward(query[b], keys, values, which[b], patch)
        return scattered_dot([mixed_cross[b]], [o_cross], False, True, 4)

    def cross_norm(b, arrived):
        x_two[b] = x_one[b] + scatter_end(arrived)
        norm_three[b], scale_three[b] = normalize(x_two[b], gain_mlp)

    def mlp_block(b, arrived_norm, arrived_grad):
        full_three[b], grad_three[b], hidden[b], d_gate[b], d_up[b] = gathered_mlp(
            norm_three[b], arrived_norm, outer_low[b], arrived_grad, w_gate, w_up, w_down, 5
        )

    def mlp_back(b):
        return scattered_dot([d_gate[b], d_up[b]], [w_gate, w_up], True, False, 6)

    def mlp_norm_back(b, arrived):
        back, gain_mlp_parts[b] = norm_back(
            x_two[b], scale_three[b], gain_mlp, scatter_end(arrived)
        )
        grad_two_rows[b] = outer[b] + back
        return grad_two_rows[b].astype(bf16)

    def cross_back(b, own, arrived, keys, values, earlier):
        grad_two[b], d_mixed = gathered_dot(own, arrived, o_cross, True, 7)
        d_query[b], *d_kv = cross_backward(
            query[b], keys, values, d_mixed, which[b], patch, earlier
        )
        return scattered_dot([d_query[b]], [q_cross], True, False, 8), d_kv

    def cross_norm_back(b, arrived):
        back, gain_cross_parts[b] = norm_back(
            x_one[b], scale_two[b], gain_cross, scatter_end(arrived)
        )
        grad_one_rows[b] = grad_two_rows[b] + back
        return grad_one_rows[b].astype(bf16)

    def self_back(b, own, arrived):
        grad_one[b], d_mixed = gathered_dot(own, arrived, o_self, True, 9)
        d_qkv[b] = self_backward(qkv[b], d_mixed, lengths[b], prefixes[b])
        return scattered_dot([d_qkv[b]], [w_qkv], True, False, 10)

    def self_norm_back(b, arrived):
        back, gain_attn_parts[b] = norm_back(
            x_zero[b], scale_one[b], gain_attn, scatter_end(arrived)
        )
        grad_input[b] = grad_one_rows[b] + back

    def project_out(b):
        return scattered_dot([hidden[b]], [w_down], False, True, 11)

    def weight_grad(left, right):
        return sum(dot_tn(left[b], right[b]) for b in each_batch)

    def move_self(b, sent):
        return scatter_move(sent, product(mixed_self[b], o_self, dot_nn), rows)

    def move_cross(b, sent):
        return scatter_move(sent, product(mixed_cross[b], o_cross, dot_nn), rows)

    def mlp_product(b):
        return lambda low, high: (
            dot_nt(d_gate[b][low:high], w_gate) + dot_nt(d_up[b][low:high], w_up)
        )

    def move_mlp(b, sent):
        return scatter_move(sent, mlp_product(b), rows)

    def move_cross_back(b, sent):
        return scatter_move(sent, product(d_query[b], q_cross, dot_nt), rows)

    def move_self_back(b, sent):
        return scatter_move(sent, product(d_qkv[b], w_qkv, dot_nt), rows)

    def move_out(b, sent):
        return scatter_move(sent, product(hidden[b], w_down, dot_nn), rows)

    sent = list(none)
    got = list(none)
    back = list(none)
    grads = list(none)
    own = list(none)
    shown = list(none)
    if batches == 2:
        got[0] = gather_start(norm_one[0])
        got[0], norm_one[1], w_qkv, outer_low, outer, which, lengths, prefixes = fence(
            got[0], norm_one[1], w_qkv, outer_low, outer, which, lengths, prefixes
        )
        got[1] = gather_start(norm_one[1])
        sent[0] = self_block(0, got[0])
        sent[0], got[1], outer_low = fence(sent[0], got[1], outer_low)
        grads[0] = gather_start(outer_low[0])
        sent[1] = self_block(1, got[1])
        sent, grads[0], k_cross = fence(sent, grads[0], k_cross)
        back[0] = scatter_move(sent[0])
        keys = dot_nn(patches, k_cross).astype(bf16)
        back[0], sent[1], keys, v_cross = fence(back[0], sent[1], keys, v_cross)
        back[1] = scatter_move(sent[1])
        self_norm(0, back[0])
        values = dot_nn(patches, v_cross).astype(bf16)
        norm_two[0], back[1], values = fence(norm_two[0], back[1], values)
        got[0] = gather_start(norm_two[0])
        self_norm(1, back[1])
        norm_two[1], got[0], outer_low = fence(norm_two[1], got[0], outer_low)
        got[1] = gather_start(norm_two[1])
        sent[0] = cross_block(0, got[0], keys, values)
        sent[0], got[1] = fence(sent[0], got[1])
        back[0] = scatter_move(sent[0])
        sent[1] = cross_block(1, got[1], keys, values)
        sent[1], back[0] = fence(sent[1], back[0])
        back[1] = scatter_move(sent[1])
        cross_norm(0, back[0])
        norm_three[0], back[1], outer_low = fence(norm_three[0], back[1], outer_low)
        got[0] = gather_start(norm_three[0])
        cross_norm(1, back[1])
        got[0], outer_low, norm_three[1] = fence(got[0], outer_low, norm_three[1])
        got[1] = gather_start(norm_three[1])
        mlp_block(0, got[0], grads[0])
        got[1], d_gate[0], d_up[0], outer_low[1] = fence(
            got[1], d_gate[0], d_up[0], outer_low[1]
        )
        grads[1] = gather_start(outer_low[1])
        sent[0] = mlp_back(0)
        grads[1], got[1], sent[0] = fence(grads[1], got[1], sent[0])
        back[0] = scatter_move(sent[0])
        mlp_block(1, got[1], grads[1])
        back[0], d_gate[1], d_up[1], hidden = fence(back[0], d_gate[1], d_up[1], hidden)
        own[0] = mlp_norm_back(0, back[0])
        got[0] = gather_start(own[0])
        sent[1] = mlp_back(1)
        d_wdown = weight_grad(hidden, grad_three)
        own[0], got[0], sent[1], d_gate, d_up, d_wdown = fence(
            own[0], got[0], sent[1], d_gate, d_up, d_wdown
        )
        back[1] = scatter_move(sent[1])
        d_wgate = weight_grad(full_three, d_gate)
        d_wup = weight_grad(full_three, d_up)
        back[1], d_wgate, d_wup, d_wdown = fence(back[1], d_wgate, d_wup, d_wdown)
        d_mlp = lax.psum([item.astype(bf16) for item in (d_wdown, d_wgate, d_wup)], "dp")
        own[1] = mlp_norm_back(1, back[1])
        got[1] = gather_start(own[1])
        sent[0], d_kv = cross_back(0, own[0], got[0], keys, values, ())
        own[1], got[1], sent[0], d_kv = fence(own[1], got[1], sent[0], d_kv)
        back[0] = scatter_move(sent[0])
        sent[1], d_kv = cross_back(1, own[1], got[1], keys, values, d_kv)
        sent[1], back[0], d_kv, mixed_cross, hidden = fence(
            sent[1], back[0], d_kv, mixed_cross, hidden
        )
        back[1] = scatter_move(sent[1])
        own[0] = cross_norm_back(0, back[0])
        d_ocross = weight_grad(mixed_cross, grad_two)
        d_qcross = weight_grad(full_two, d_query)
        shown[0] = project_out(0)
        own[0], back[1], d_kv, d_ocross, d_qcross, shown[0] = fence(
            own[0], back[1], d_kv, d_ocross, d_qcross, shown[0]
        )
        got[0] = gather_start(own[0])
        own[1] = cross_norm_back(1, back[1])
        d_kcross = dot_tn(patches, d_kv[0])
        d_vcross = dot_tn(patches, d_kv[1])
        got[0], own[1], d_kcross, d_vcross, hidden = fence(
            got[0], own[1], d_kcross, d_vcross, hidden
        )
        got[1] = gather_start(own[1])
        sent[0] = self_back(0, own[0], got[0])
        got[1], sent[0] = fence(got[1], sent[0])
        back[0] = scatter_move(sent[0])
        sent[1] = self_back(1, own[1], got[1])
        back[0], sent[1], mixed_self, hidden = fence(back[0], sent[1], mixed_self, hidden)
        back[1] = scatter_move(sent[1])
        self_norm_back(0, back[0])
        d_oself = weight_grad(mixed_self, grad_one)
        d_wqkv = weight_grad(full_one, d_qkv)
        shown[1] = project_out(1)
        back[1], grad_input[0], d_wqkv, d_oself, shown = fence(
            back[1], grad_input[0], d_wqkv, d_oself, shown
        )
        self_norm_back(1, back[1])
    else:
        sent[0] = self_block(0, gather_start(norm_one[0]))
        self_norm(0, scatter_move(sent[0]))
        keys = dot_nn(patches, k_cross).astype(bf16)
        values = dot_nn(patches, v_cross).astype(bf16)
        sent[0] = cross_block(0, gather_start(norm_two[0]), keys, values)
        cross_norm(0, scatter_move(sent[0]))
        mlp_block(0, gather_start(norm_three[0]), gather_start(outer_low[0]))
        own[0] = mlp_norm_back(0, scatter_move(mlp_back(0)))
        sent[0], d_kv = cross_back(0, own[0], gather_start(own[0]), keys, values, ())
        own[0] = cross_norm_back(0, scatter_move(sent[0]))
        sent[0] = self_back(0, own[0], gather_start(own[0]))
        self_norm_back(0, scatter_move(sent[0]))
        d_wdown = weight_grad(hidden, grad_three)
        d_wgate = weight_grad(full_three, d_gate)
        d_wup = weight_grad(full_three, d_up)
        d_kcross = dot_tn(patches, d_kv[0])
        d_vcross = dot_tn(patches, d_kv[1])
        d_wqkv = weight_grad(full_one, d_qkv)
        d_qcross = weight_grad(full_two, d_query)
        d_oself = weight_grad(mixed_self, grad_one)
        d_ocross = weight_grad(mixed_cross, grad_two)
        d_mlp = lax.psum([item.astype(bf16) for item in (d_wdown, d_wgate, d_wup)], "dp")
        shown = [project_out(0)]
    back = [scatter_move(shown[b]) for b in each_batch]
    gains = jnp.stack(
        [sum(parts) for parts in (gain_attn_parts, gain_cross_parts, gain_mlp_parts)]
    )
    summed = sum_dp_start([d_ocross, d_qcross, d_kcross, d_vcross, d_oself, d_wqkv])
    summed, d_mlp, back, gains = fence(summed, d_mlp, back, gains)
    gains = butterfly(butterfly(gains, "mp"), "dp")
    d_ocross, d_qcross, d_kcross, d_vcross, d_oself, d_wqkv = sum_dp_end(
        summed, [d_ocross, d_qcross, d_kcross, d_vcross, d_oself, d_wqkv]
    )
    output = jnp.concatenate(
        [(x_two[b] + scatter_end(back[b])).astype(bf16) for b in each_batch], axis=0
    )
    grad_input = jnp.concatenate(grad_input, axis=0)
    d_wdown, d_wgate, d_wup = [item.astype(f32) for item in d_mlp]
    return (
        output,
        grad_input,
        d_wqkv[:, :width],
        d_wqkv[:, width : 2 * width],
        d_wqkv[:, 2 * width :],
        d_oself,
        d_qcross,
        d_kcross,
        d_vcross,
        d_ocross,
        d_wgate,
        d_wup,
        d_wdown,
        gains[0],
        gains[1],
        gains[2],
    )


def solution(mesh):
    by_rows = P(("dp", "mp"), None)
    columns = P(None, "mp")
    rows = P("mp", None)
    weights = (columns, columns, columns, rows, columns, columns, columns, rows, columns, columns, rows)
    in_specs = (
        (by_rows, P("dp", None), P("dp"), P("dp"), P("dp"), P(), by_rows) + weights + (P(), P(), P())
    )
    out_specs = (by_rows, by_rows) + weights + (P(), P(), P())
    return jax.shard_map(
        on_device, mesh=mesh, in_specs=in_specs, out_specs=out_specs, check_vma=False
    )
```

```python
from functools import partial

import jax
import jax.numpy as jnp
from jax import lax
from jax.experimental import pallas as pl
from jax.experimental.pallas import tpu as pltpu
from jax.sharding import PartitionSpec as P

HEAD = 64
SEQ = 128
PAIR = 2 * HEAD
epsilon = 1e-06
f32 = jnp.float32
bf16 = jnp.bfloat16
VMEM_LIMIT = 56 * 1024 * 1024
MESH = pl.DeviceIdType.MESH


def dot_nn(left, right):
    return jnp.dot(left, right, preferred_element_type=f32)


def dot_tn(left, right):
    return lax.dot_general(left, right, (((0,), (0,)), ((), ())), preferred_element_type=f32)


def dot_nt(left, right):
    return lax.dot_general(left, right, (((1,), (1,)), ((), ())), preferred_element_type=f32)


def normalize(values_in, gain):
    row_scale = lax.rsqrt(jnp.mean(values_in * values_in, axis=-1, keepdims=True) + epsilon)
    return ((values_in * row_scale * gain).astype(bf16), row_scale)


def norm_back(values_in, row_scale, gain, incoming):
    weighted = incoming * gain
    inner = jnp.mean(weighted * values_in, axis=-1, keepdims=True)
    return (
        row_scale * weighted - values_in * row_scale**3 * inner,
        jnp.sum(incoming * values_in * row_scale, axis=0),
    )


def first_head():
    return lax.broadcasted_iota(jnp.int32, (SEQ, PAIR), 1) < HEAD


def stack_pair(rows, first):
    zero = jnp.zeros_like(rows)
    return jnp.concatenate([jnp.where(first, rows, zero), jnp.where(first, zero, rows)], axis=0)


def unstack_pair(stacked, first):
    return jnp.where(first, stacked[:SEQ], stacked[SEQ:])


def self_mask(length, prefix):
    query_at = lax.broadcasted_iota(jnp.int32, (2 * SEQ, SEQ), 0) % SEQ
    key_at = lax.broadcasted_iota(jnp.int32, (2 * SEQ, SEQ), 1)
    return (key_at < length) & ((key_at <= query_at) | (key_at < prefix))


def pair_probs(stacked_query, keys, mask):
    scores = dot_nt(stacked_query, keys)
    if mask is not None:
        scores = jnp.where(mask, scores, -1e30)
    expd = jnp.exp(scores - jnp.max(scores, axis=-1, keepdims=True))
    return expd * (1.0 / jnp.sum(expd, axis=-1, keepdims=True))


def pair_forward(query, keys, values, mask, first):
    scaled = stack_pair(query * jnp.asarray(HEAD**-0.5, bf16), first)
    probs = pair_probs(scaled, keys, mask)
    return unstack_pair(dot_nn(probs.astype(bf16), values), first).astype(bf16)


def pair_backward(grad, query, keys, values, mask, first):
    scaled = stack_pair(query * jnp.asarray(HEAD**-0.5, bf16), first)
    probs = pair_probs(scaled, keys, mask)
    grads = stack_pair(grad, first)
    d_probs = dot_nt(grads, values)
    d_scores = (
        probs * (d_probs - jnp.sum(probs * d_probs, axis=-1, keepdims=True))
    ).astype(bf16)
    d_query = unstack_pair(dot_nn(d_scores, keys), first) * HEAD**-0.5
    d_keys = dot_tn(d_scores, scaled)
    d_values = dot_tn(probs.astype(bf16), grads)
    return d_query.astype(bf16), d_keys.astype(bf16), d_values.astype(bf16)


def lanes(part, width, pair):
    return slice(part * width + pair * PAIR, part * width + (pair + 1) * PAIR)


def self_forward_kernel(length_ref, prefix_ref, qkv_ref, out_ref):
    at = pl.program_id(0)
    width = out_ref.shape[1]
    first = first_head()
    mask = self_mask(length_ref[at], prefix_ref[at])
    for pair in range(width // PAIR):
        out_ref[:, lanes(0, width, pair)] = pair_forward(
            qkv_ref[:, lanes(0, width, pair)],
            qkv_ref[:, lanes(1, width, pair)],
            qkv_ref[:, lanes(2, width, pair)],
            mask,
            first,
        )


def self_backward_kernel(length_ref, prefix_ref, qkv_ref, grad_ref, out_ref):
    at = pl.program_id(0)
    width = grad_ref.shape[1]
    first = first_head()
    mask = self_mask(length_ref[at], prefix_ref[at])
    for pair in range(width // PAIR):
        for part, value in enumerate(
            pair_backward(
                grad_ref[:, lanes(0, width, pair)],
                qkv_ref[:, lanes(0, width, pair)],
                qkv_ref[:, lanes(1, width, pair)],
                qkv_ref[:, lanes(2, width, pair)],
                mask,
                first,
            )
        ):
            out_ref[:, lanes(part, width, pair)] = value


def cross_forward_kernel(which_ref, query_ref, key_ref, value_ref, out_ref):
    width = out_ref.shape[1]
    first = first_head()
    for pair in range(width // PAIR):
        at = lanes(0, width, pair)
        out_ref[:, at] = pair_forward(
            query_ref[:, at], key_ref[:, at], value_ref[:, at], None, first
        )


def cross_backward_kernel(which_ref, query_ref, key_ref, value_ref, grad_ref, *rest):
    d_query_ref, d_key_ref, d_value_ref = rest[-3:]
    width = query_ref.shape[1]
    first = first_head()
    for pair in range(width // PAIR):
        at = lanes(0, width, pair)
        d_query_ref[:, at], d_key_ref[:, at], d_value_ref[:, at] = pair_backward(
            grad_ref[:, at], query_ref[:, at], key_ref[:, at], value_ref[:, at], None, first
        )


def params():
    return pltpu.CompilerParams(vmem_limit_bytes=ROOM)


def by_row(width):
    return pl.BlockSpec((SEQ, width), lambda i, *_: (i, 0))


def attention_cost(examples, width, keys, dots, moved):
    return pl.CostEstimate(
        flops=dots * 2 * examples * SEQ * keys * width * 2,
        bytes_accessed=moved,
        transcendentals=examples * SEQ * keys * width // HEAD,
    )


def self_forward(qkv, length, prefix):
    rows, triple = qkv.shape
    width = triple // 3
    return pl.pallas_call(
        self_forward_kernel,
        grid_spec=pltpu.PrefetchScalarGridSpec(
            num_scalar_prefetch=2,
            grid=(rows // SEQ,),
            in_specs=[by_row(triple)],
            out_specs=by_row(width),
        ),
        out_shape=jax.ShapeDtypeStruct((rows, width), bf16),
        compiler_params=params(),
        cost_estimate=attention_cost(rows // SEQ, width, SEQ, 2, rows * width * 8),
    )(length, prefix, qkv)


def self_backward(qkv, grad, length, prefix):
    rows, triple = qkv.shape
    width = triple // 3
    return pl.pallas_call(
        self_backward_kernel,
        grid_spec=pltpu.PrefetchScalarGridSpec(
            num_scalar_prefetch=2,
            grid=(rows // SEQ,),
            in_specs=[by_row(triple), by_row(width)],
            out_specs=by_row(triple),
        ),
        out_shape=jax.ShapeDtypeStruct((rows, triple), bf16),
        compiler_params=params(),
        cost_estimate=attention_cost(rows // SEQ, width, SEQ, 5, rows * width * 14),
    )(length, prefix, qkv, grad)


def cross_forward(query, keys, values, which, patch):
    rows, width = query.shape
    by_patch = pl.BlockSpec((patch, width), lambda i, which: (which[i], 0))
    return pl.pallas_call(
        cross_forward_kernel,
        grid_spec=pltpu.PrefetchScalarGridSpec(
            num_scalar_prefetch=1,
            grid=(rows // SEQ,),
            in_specs=[by_row(width), by_patch, by_patch],
            out_specs=by_row(width),
        ),
        out_shape=jax.ShapeDtypeStruct((rows, width), bf16),
        compiler_params=params(),
        cost_estimate=attention_cost(rows // SEQ, width, patch, 2, rows * width * 12),
    )(which, query, keys, values)


def cross_backward(query, keys, values, grad, which, patch, earlier):
    rows, width = query.shape
    by_patch = pl.BlockSpec((patch, width), lambda i, which: (which[i], 0))
    in_specs = [by_row(width), by_patch, by_patch, by_row(width)]
    operands = [which, query, keys, values, grad]
    aliases = {}
    for at, item in enumerate(earlier):
        in_specs.append(pl.BlockSpec(memory_space=pl.ANY))
        aliases[len(operands)] = 1 + at
        operands.append(item)
    whole = jax.ShapeDtypeStruct(keys.shape, bf16)
    return pl.pallas_call(
        cross_backward_kernel,
        grid_spec=pltpu.PrefetchScalarGridSpec(
            num_scalar_prefetch=1,
            grid=(rows // SEQ,),
            in_specs=in_specs,
            out_specs=[by_row(width), by_patch, by_patch],
        ),
        out_shape=[jax.ShapeDtypeStruct((rows, width), bf16), whole, whole],
        input_output_aliases=aliases,
        compiler_params=params(),
        cost_estimate=attention_cost(rows // SEQ, width, patch, 5, rows * width * 24),
    )(*operands)


def other_core():
    me = lax.axis_index("mp")
    return me + 1 - 2 * lax.rem(me, 2)


def meet(partner):
    barrier = pltpu.get_barrier_semaphore()
    pl.semaphore_signal(barrier, inc=1, device_id={"mp": partner}, device_id_type=MESH)
    pl.semaphore_wait(barrier, 1)


def to_partner(source, target, send_sem, recv_sem, partner):
    return pltpu.make_async_remote_copy(
        src_ref=source,
        dst_ref=target,
        send_sem=send_sem,
        recv_sem=recv_sem,
        device_id={"mp": partner},
        device_id_type=MESH,
    )


def columns_of(weight, tile, size, transposed):
    at = pl.ds(pl.multiple_of(tile * size, size), size)
    return weight[at, :] if transposed else weight[:, at]


def gathered_kernel(transposed, size, own, beside, across, weight, full, out, corner, sems, local):
    dot = dot_nt if transposed else dot_nn
    rows = own.shape[0]
    blocks = (own, beside, across, corner)
    partner = other_core()
    given = to_partner(across, corner, sems.at[0], sems.at[1], partner)
    keep = [
        pltpu.make_async_copy(block, full.at[pl.ds(at * rows, rows)], local.at[at])
        for at, block in enumerate(blocks)
    ]
    meet(partner)
    given.start()
    for at in range(3):
        keep[at].start()

    def multiply(places):
        @pl.loop(0, out.shape[1] // size)
        def _(tile):
            right = columns_of(weight, tile, size, transposed)
            to = pl.ds(pl.multiple_of(tile * size, size), size)
            for at in places:
                out[at * rows : (at + 1) * rows, to] = dot(blocks[at][...], right).astype(bf16)

    multiply((0, 1, 2))
    given.wait()
    keep[3].start()
    multiply((3,))
    for at in range(4):
        keep[at].wait()


IN_VMEM = pl.BlockSpec(memory_space=pltpu.VMEM)
ROOM = 24 * 1024 * 1024


def gathered_dot(own, arrived, weight, transposed, ident):
    if lax.axis_size("mp") != 4:
        dot = dot_nt if transposed else dot_nn
        return arrived, dot(arrived, weight).astype(bf16)
    across, beside = arrived
    rows, model = own.shape
    units = weight.shape[0 if transposed else 1]
    return pl.pallas_call(
        partial(gathered_kernel, transposed, 512),
        in_specs=[IN_VMEM] * 4,
        out_specs=[pl.BlockSpec(memory_space=pl.ANY), IN_VMEM],
        out_shape=[
            jax.ShapeDtypeStruct((4 * rows, model), bf16),
            jax.ShapeDtypeStruct((4 * rows, units), bf16),
        ],
        scratch_shapes=[
            pltpu.VMEM((rows, model), bf16),
            pltpu.SemaphoreType.DMA((2,)),
            pltpu.SemaphoreType.DMA((4,)),
        ],
        compiler_params=pltpu.CompilerParams(
            collective_id=ident, has_side_effects=True, vmem_limit_bytes=ROOM
        ),
        cost_estimate=pl.CostEstimate(
            flops=8 * rows * model * units,
            bytes_accessed=14 * rows * model + 4 * model * units + 8 * rows * units,
            transcendentals=0,
        ),
    )(own, beside, across, weight)


def scattered_kernel(transposed, count, size, *refs):
    dot = dot_nt if transposed else dot_nn
    lefts, weights = refs[:count], refs[count : 2 * count]
    kept, passed, ready, landed, send_sem, recv_sem = refs[2 * count :]
    rows, model = kept.shape
    tiles = model // size
    partner = other_core()

    def given(tile):
        return to_partner(
            ready.at[tile], landed.at[tile], send_sem.at[tile], recv_sem.at[tile], partner
        )

    def block(at, tile):
        return sum(
            dot(
                left[at * rows : (at + 1) * rows, :],
                columns_of(weight, tile, size, transposed),
            )
            for left, weight in zip(lefts, weights)
        )

    meet(partner)

    @pl.loop(0, tiles)
    def _(tile):
        ready[tile, :rows, :] = block(1, tile).astype(bf16)
        ready[tile, rows:, :] = block(3, tile).astype(bf16)
        given(tile).start()

    @pl.loop(0, tiles)
    def _(tile):
        mine = block(0, tile)
        across = block(2, tile)
        given(tile).wait()
        to = pl.ds(pl.multiple_of(tile * size, size), size)
        kept[:, to] = mine + landed[tile, :rows, :].astype(f32)
        passed[:, to] = (across + landed[tile, rows:, :].astype(f32)).astype(bf16)


def scattered_dot(lefts, weights, transposed, wide, ident):
    if lax.axis_size("mp") != 4:
        dot = dot_nt if transposed else dot_nn
        term = sum(dot(left, weight) for left, weight in zip(lefts, weights))
        return (term if wide else term.astype(bf16),)
    rows = lefts[0].shape[0] // 4
    model = weights[0].shape[0 if transposed else 1]
    size = 512
    tiles = model // size
    depth = sum(item.shape[1] for item in lefts)
    return pl.pallas_call(
        partial(scattered_kernel, transposed, len(lefts), size),
        in_specs=[IN_VMEM] * (2 * len(lefts)),
        out_specs=[IN_VMEM, IN_VMEM],
        out_shape=[
            jax.ShapeDtypeStruct((rows, model), f32),
            jax.ShapeDtypeStruct((rows, model), bf16),
        ],
        scratch_shapes=[
            pltpu.VMEM((tiles, 2 * rows, size), bf16),
            pltpu.VMEM((tiles, 2 * rows, size), bf16),
            pltpu.SemaphoreType.DMA((tiles,)),
            pltpu.SemaphoreType.DMA((tiles,)),
        ],
        compiler_params=pltpu.CompilerParams(
            collective_id=ident,
            has_side_effects=True,
            vmem_limit_bytes=ROOM if depth < 2048 else 2 * ROOM,
        ),
        cost_estimate=pl.CostEstimate(
            flops=8 * rows * model * depth,
            bytes_accessed=8 * rows * depth + 4 * model * depth + 14 * rows * model,
            transcendentals=0,
        ),
    )(*lefts, *weights)


def mlp_rows(norm, grad, gate_ref, up_ref, down_ref):
    curve = 0.7978845608028654
    gate = dot_nn(norm, gate_ref[...])
    up = dot_nn(norm, up_ref[...])
    d_hidden = dot_nt(grad, down_ref[...])
    square = gate * gate
    bend = jnp.tanh(curve * gate * (1.0 + 0.044715 * square))
    half = 0.5 * (1.0 + bend)
    value = gate * half
    slope = half + 0.5 * curve * gate * (1.0 - bend * bend) * (1.0 + 0.134145 * square)
    return (
        (value * up).astype(bf16),
        (d_hidden * up * slope).astype(bf16),
        (d_hidden * value).astype(bf16),
    )


def mlp_kernel(norm_ref, grad_ref, gate_ref, up_ref, down_ref, hidden_ref, d_gate_ref, d_up_ref):
    rows = norm_ref.shape[0]
    step = min(rows, 256)
    for start in range(0, rows, step):
        at = slice(start, start + step)
        hidden_ref[at, :], d_gate_ref[at, :], d_up_ref[at, :] = mlp_rows(
            norm_ref[at, :], grad_ref[at, :], gate_ref, up_ref, down_ref
        )


def gathered_mlp_kernel(tiles, *refs):
    norms, grads = refs[:3], refs[3:6]
    gate_ref, up_ref, down_ref = refs[6:9]
    full_norm, full_grad, hidden_ref, d_gate_ref, d_up_ref = refs[9:14]
    corner_norm, corner_grad, sems, local = refs[14:]
    tile = pl.program_id(0)
    rows = norms[0].shape[0]
    partner = other_core()
    norms = (*norms, corner_norm)
    grads = (*grads, corner_grad)

    def given(at):
        source, target = ((norms[2], corner_norm), (grads[2], corner_grad))[at]
        return to_partner(source, target, sems.at[2 * at], sems.at[2 * at + 1], partner)

    def keep(which, at):
        source, target = ((norms, full_norm), (grads, full_grad))[which]
        return pltpu.make_async_copy(
            source[at], target.at[pl.ds(at * rows, rows)], local.at[which, at]
        )

    @pl.when(tile == 0)
    def _():
        meet(partner)
        for which in range(2):
            given(which).start()
        for which in range(2):
            for at in range(3):
                keep(which, at).start()

    for at in range(4):
        if at == 3:

            @pl.when(tile == 0)
            def _():
                for which in range(2):
                    given(which).wait()
                    keep(which, 3).start()

        place = slice(at * rows, (at + 1) * rows)
        hidden_ref[place, :], d_gate_ref[place, :], d_up_ref[place, :] = mlp_rows(
            norms[at][...], grads[at][...], gate_ref, up_ref, down_ref
        )

    @pl.when(tile == tiles - 1)
    def _():
        for which in range(2):
            for at in range(4):
                keep(which, at).wait()


def gathered_mlp(own_norm, arrived_norm, own_grad, arrived_grad, w_gate, w_up, w_down, ident):
    model, units = w_gate.shape
    if lax.axis_size("mp") != 4:
        return (
            arrived_norm,
            arrived_grad,
            *mlp(arrived_norm, arrived_grad, w_gate, w_up, w_down),
        )
    rows = own_norm.shape[0]
    tile = 256
    whole = pl.BlockSpec((rows, model), lambda i: (0, 0))
    columns = pl.BlockSpec((model, tile), lambda i: (0, i))
    out = pl.BlockSpec((4 * rows, tile), lambda i: (0, i))
    full = pl.BlockSpec(memory_space=pl.ANY)
    shape = jax.ShapeDtypeStruct((4 * rows, units), bf16)
    full_shape = jax.ShapeDtypeStruct((4 * rows, model), bf16)
    return pl.pallas_call(
        partial(gathered_mlp_kernel, units // tile),
        grid=(units // tile,),
        in_specs=[whole] * 6 + [columns, columns, pl.BlockSpec((tile, model), lambda i: (i, 0))],
        out_specs=[full, full, out, out, out],
        out_shape=[full_shape, full_shape, shape, shape, shape],
        scratch_shapes=[
            pltpu.VMEM((rows, model), bf16),
            pltpu.VMEM((rows, model), bf16),
            pltpu.SemaphoreType.DMA((4,)),
            pltpu.SemaphoreType.DMA((2, 4)),
        ],
        compiler_params=pltpu.CompilerParams(
            collective_id=ident, has_side_effects=True, vmem_limit_bytes=VMEM_LIMIT
        ),
        cost_estimate=pl.CostEstimate(
            flops=24 * rows * model * units,
            bytes_accessed=28 * rows * model + 6 * model * units + 24 * rows * units,
            transcendentals=4 * rows * units,
        ),
    )(
        own_norm,
        arrived_norm[1],
        arrived_norm[0],
        own_grad,
        arrived_grad[1],
        arrived_grad[0],
        w_gate,
        w_up,
        w_down,
    )


def mlp(norm, grad, w_gate, w_up, w_down):
    rows, model = norm.shape
    units = w_gate.shape[1]
    tile = 256 if units % 256 == 0 else units
    whole = pl.BlockSpec((rows, model), lambda i: (0, 0))
    columns = pl.BlockSpec((model, tile), lambda i: (0, i))
    out = pl.BlockSpec((rows, tile), lambda i: (0, i))
    shape = jax.ShapeDtypeStruct((rows, units), bf16)
    return pl.pallas_call(
        mlp_kernel,
        grid=(units // tile,),
        in_specs=[whole, whole, columns, columns, pl.BlockSpec((tile, model), lambda i: (i, 0))],
        out_specs=[out, out, out],
        out_shape=[shape, shape, shape],
        compiler_params=params(),
        cost_estimate=pl.CostEstimate(
            flops=6 * rows * model * units,
            bytes_accessed=4 * rows * model + 6 * model * units + 6 * rows * units,
            transcendentals=rows * units,
        ),
    )(norm, grad, w_gate, w_up, w_down)


def flip(tensor, axis, bit):
    count = lax.axis_size(axis)
    return lax.ppermute(tensor, axis, [(i, i ^ bit) for i in range(count)])


def butterfly(tensor, axis):
    count = lax.axis_size(axis)
    if count & (count - 1):
        return lax.psum(tensor, axis)
    bit = 1
    while bit < count:
        tensor = tensor + flip(tensor, axis, bit)
        bit *= 2
    return tensor


def block_owners():
    blocks = jnp.arange(lax.axis_size("mp"), dtype=jnp.int32)
    return lax.axis_index("mp") ^ blocks if lax.axis_size("mp") == 4 else blocks


def fence(*values):
    return lax.optimization_barrier(values)


def gather_start(rows_local):
    if lax.axis_size("mp") != 4:
        return lax.all_gather(rows_local, "mp", axis=0, tiled=True)
    return flip(rows_local, "mp", 2), flip(rows_local, "mp", 1)


def scatter_move(sent):
    if lax.axis_size("mp") != 4:
        return None, lax.psum_scatter(sent[0], "mp", scatter_dimension=0, tiled=True)
    return sent[0], flip(sent[1], "mp", 2)


def scatter_end(arrived):
    if lax.axis_size("mp") != 4:
        return arrived[1].astype(f32)
    return arrived[0] + arrived[1].astype(f32)


CHUNK = 256
WIDE = 256
LANDINGS = 7
PERIOD = 9
PAIRED = 6
LAST_HOP = (8, 9, 11, 13, 15, 16)


class Late:
    def __init__(self, make):
        self.make = make

    def start(self):
        self.make().start()

    def wait(self):
        self.make().wait()

    def wait_send(self):
        self.make().wait_send()

    def wait_recv(self):
        self.make().wait_recv()


def sum_kernel(cycles, open_count, paired_count, *refs):
    inputs, refs = refs[: open_count + 2 * paired_count], refs[open_count + 2 * paired_count :]
    open_in = inputs[:open_count]
    paired_in = inputs[open_count : open_count + paired_count]
    arrived_in = inputs[open_count + paired_count :]
    open_out, paired_out = refs[:2]
    (
        opened,
        paired,
        open_land,
        paired_land,
        open_send,
        open_recv,
        open_local,
        paired_send,
        paired_recv,
        paired_local,
        fill_sem,
        ring,
        ring_sem,
    ) = refs[2:]
    at = lax.axis_index("dp")
    y = lax.rem(at, 2)
    z = lax.div(at, 2)
    inner = (z == 1) | (z == 2)
    outer = (z == 0) | (z == 3)
    beside = z * 2 + (1 - y)
    along = at + jnp.where(lax.rem(z, 2) == 0, 2, -2)
    facing = (3 - z) * 2 + y
    side = z - 1
    paired_chunks = paired.shape[0] // CHUNK

    barrier = pltpu.get_barrier_semaphore()

    def greet(target):
        pl.semaphore_signal(barrier, inc=1, device_id={"dp": target}, device_id_type=MESH)

    greet(beside)
    greet(along)

    fills = []
    for sources, target in ((open_in, opened), (paired_in, paired)):
        start = 0
        for source in sources:
            place = target.at[pl.ds(start, source.shape[0])]
            fills.append(pltpu.make_async_copy(source, place, fill_sem.at[len(fills)]))
            start += source.shape[0]
    for fill in fills:
        fill.start()

    @pl.when(inner)
    def _():
        greet(facing)
        pl.semaphore_wait(barrier, 3)

    @pl.when(outer)
    def _():
        pl.semaphore_wait(barrier, 2)

    for fill in fills:
        fill.wait()

    def remote(source, target, send_sem, recv_sem, device):
        return Late(
            lambda: pltpu.make_async_remote_copy(
                src_ref=source,
                dst_ref=target,
                send_sem=send_sem,
                recv_sem=recv_sem,
                device_id={"dp": device},
                device_id_type=MESH,
            )
        )

    def add(place, landing):
        @pl.loop(0, CHUNK // 32)
        def _(step):
            rows = pl.ds(pl.multiple_of(step * 32, 32), 32)
            place[rows, :] = (
                place[rows, :].astype(f32) + landing[rows, :].astype(f32)
            ).astype(bf16)

    def everyone(descriptor, after):
        def finish():
            descriptor.wait()
            after()

        return descriptor.start, finish

    def inward(descriptor, place, landed):
        def start():
            pl.when(outer)(descriptor.start)

        def finish():
            pl.when(outer)(descriptor.wait_send)

            @pl.when(inner)
            def _():
                descriptor.wait_recv()
                add(place, landed)

        return start, finish

    def between(descriptor, after, local=None):
        def start():
            @pl.when(inner)
            def _():
                descriptor.start()
                if local is not None:
                    local.start()

        def finish():
            @pl.when(inner)
            def _():
                descriptor.wait()
                if local is not None:
                    local.wait()
                after()

        return start, finish

    def outward(descriptor, local=None):
        def start():
            @pl.when(inner)
            def _():
                descriptor.start()
                if local is not None:
                    local.start()

        def finish():
            @pl.when(inner)
            def _():
                descriptor.wait_send()
                if local is not None:
                    local.wait()

            pl.when(outer)(descriptor.wait_recv)

        return start, finish

    def nothing():
        return None

    def rows_of(index):
        return pl.ds(pl.multiple_of(index * CHUNK, CHUNK), CHUNK)

    def open_stages(stream, cycle):
        first = (stream * cycles + cycle) * 4
        x = [opened.at[rows_of(first + i)] for i in (y, 1 - y, 2, 3, 2 + side, 3 - side)]
        out = [open_out.at[rows_of(first + i)] for i in (y, 1 - y, 2, 3, 2 + side, 3 - side)]
        mine, other, low, high, own, given = range(6)
        land = [open_land.at[stream, cycle, i] for i in range(LANDINGS)]

        def copy(slot, source, target, device):
            return remote(
                source,
                target,
                open_send.at[stream, cycle, slot],
                open_recv.at[stream, cycle, slot],
                device,
            )

        def keep(which, slot):
            return Late(
                lambda: pltpu.make_async_copy(
                    x[which], out[which], open_local.at[stream, cycle, slot]
                )
            )

        return [
            (0, inward(copy(0, x[low], land[0], along), x[low], land[0])),
            (1, inward(copy(1, x[high], land[1], along), x[high], land[1])),
            (2, between(copy(2, x[given], land[2], facing), lambda: add(x[own], land[2]))),
            (3, between(copy(3, x[own], land[3], beside), lambda: add(x[own], land[3]))),
            (4, between(copy(4, x[own], out[own], facing), nothing, keep(own, 0))),
            (5, outward(copy(5, out[low], out[low], along))),
            (6, outward(copy(6, out[high], out[high], along))),
            (1, everyone(copy(7, x[other], land[4], beside), lambda: add(x[mine], land[4]))),
            (2, inward(copy(8, x[mine], land[5], along), x[mine], land[5])),
            (3, between(copy(9, x[mine], land[6], facing), lambda: add(x[mine], land[6]))),
            (4, outward(copy(10, x[mine], out[mine], along), keep(mine, 1))),
            (5, everyone(copy(11, out[mine], out[mine], beside), nothing)),
        ]

    def paired_stages(stream, cycle, index):
        chunk = (stream * cycles + cycle) * PAIRED + index
        x = paired.at[rows_of(chunk)]
        out = paired_out.at[y, rows_of(chunk)]
        land = [paired_land.at[chunk, i] for i in range(2)]

        def copy(slot, source, target, device):
            return remote(
                source, target, paired_send.at[chunk, slot], paired_recv.at[chunk, slot], device
            )

        keep = Late(lambda: pltpu.make_async_copy(x, out, paired_local.at[chunk]))
        slot, slot_sem = ring.at[stream, index], ring_sem.at[stream, index]

        def fetch():
            begin = 0
            for source in arrived_in:
                count = source.shape[0] // CHUNK

                @pl.when((chunk >= begin) & (chunk < begin + count))
                def _(source=source, begin=begin):
                    pltpu.make_async_copy(
                        source.at[rows_of(chunk - begin)], slot, slot_sem
                    ).start()

                begin += count

        def fetched():
            pltpu.make_async_copy(arrived_in[0].at[rows_of(0)], slot, slot_sem).wait()
            add(x, slot)

        return [
            (2 + index, (fetch, fetched)),
            (3 + index, inward(copy(0, x, land[0], along), x, land[0])),
            (5 + index, between(copy(1, x, land[1], facing), lambda: add(x, land[1]))),
            (7 + index, outward(copy(2, x, out, along), keep)),
            (LAST_HOP[index], everyone(copy(3, out, out, beside), nothing)),
        ]

    offsets = range(max(LAST_HOP) + 1)

    def run(step, stream, offset, back, what):
        cycle = step - back

        @pl.when((cycle >= 0) & (cycle < cycles))
        def _():
            for when, pair in open_stages(stream, cycle):
                if when == offset:
                    pair[what]()
            for index in range(PAIRED):
                chunk = (stream * cycles + cycle) * PAIRED + index

                def each(index=index):
                    for when, pair in paired_stages(stream, cycle, index):
                        if when == offset:
                            pair[what]()

                if offset in (2 + index, 3 + index, 5 + index, 7 + index, LAST_HOP[index]):
                    pl.when(chunk < paired_chunks)(each)

    def body(step, carry):
        for phase in range(PERIOD):

            @pl.loop(0, 2)
            def _(stream):
                for offset in offsets:
                    if (offset + 1) % PERIOD == phase:
                        run(step, stream, offset, (offset + 1) // PERIOD, 1)
                for offset in offsets:
                    if offset % PERIOD == phase:
                        run(step, stream, offset, offset // PERIOD, 0)

        return carry

    lax.fori_loop(0, cycles + 2, body, 0)


def sum_chunks(opened, paired, arrived):
    open_rows = sum(item.shape[0] for item in opened)
    paired_rows = sum(item.shape[0] for item in paired)
    cycles = open_rows // (CHUNK * 8)
    chunks = paired_rows // CHUNK
    assert cycles * CHUNK * 8 == open_rows and chunks <= 2 * cycles * PAIRED
    return pl.pallas_call(
        partial(sum_kernel, cycles, len(opened), len(paired)),
        in_specs=[pl.BlockSpec(memory_space=pl.ANY)] * (len(opened) + 2 * len(paired)),
        out_specs=[pl.BlockSpec(memory_space=pl.ANY)] * 2,
        out_shape=[
            jax.ShapeDtypeStruct((open_rows, WIDE), bf16),
            jax.ShapeDtypeStruct((2, paired_rows, WIDE), bf16),
        ],
        scratch_shapes=[
            pltpu.VMEM((open_rows, WIDE), bf16),
            pltpu.VMEM((paired_rows, WIDE), bf16),
            pltpu.VMEM((2, cycles, LANDINGS, CHUNK, WIDE), bf16),
            pltpu.VMEM((chunks, 2, CHUNK, WIDE), bf16),
            pltpu.SemaphoreType.DMA((2, cycles, 12)),
            pltpu.SemaphoreType.DMA((2, cycles, 12)),
            pltpu.SemaphoreType.DMA((2, cycles, 2)),
            pltpu.SemaphoreType.DMA((chunks, 4)),
            pltpu.SemaphoreType.DMA((chunks, 4)),
            pltpu.SemaphoreType.DMA((chunks,)),
            pltpu.SemaphoreType.DMA((len(opened) + len(paired),)),
            pltpu.VMEM((2, PAIRED, CHUNK, WIDE), bf16),
            pltpu.SemaphoreType.DMA((2, PAIRED)),
        ],
        compiler_params=pltpu.CompilerParams(
            collective_id=0, has_side_effects=True, vmem_limit_bytes=63 * 1024 * 1024
        ),
        cost_estimate=pl.CostEstimate(
            flops=open_rows * WIDE * 4,
            bytes_accessed=(open_rows + 2 * paired_rows) * WIDE * 8,
            transcendentals=0,
        ),
    )(*opened, *paired, *arrived)


def weight_grad_kernel(count, *refs):
    lefts, rights, out = refs[:count], refs[count : 2 * count], refs[-1]
    total = sum(dot_tn(left[...], right[...]) for left, right in zip(lefts, rights))
    for piece in range(out.shape[1]):
        out[0, piece] = total[:, piece * WIDE : (piece + 1) * WIDE].astype(bf16)


def weight_grad(lefts, rights):
    depth, height = lefts[0].shape
    width = rights[0].shape[1]
    half, pieces = height // 2, width // WIDE
    tile = half if half <= 640 else 512
    steps = half // tile
    count = len(lefts)
    return pl.pallas_call(
        partial(weight_grad_kernel, count),
        grid=(2 * steps,),
        in_specs=[pl.BlockSpec((depth, tile), lambda i: (0, i))] * count
        + [pl.BlockSpec((depth, width), lambda i: (0, 0))] * count,
        out_specs=pl.BlockSpec((1, pieces, tile, WIDE), lambda i: (i // steps, 0, i % steps, 0)),
        out_shape=jax.ShapeDtypeStruct((2, pieces, half, WIDE), bf16),
        compiler_params=pltpu.CompilerParams(vmem_limit_bytes=VMEM_LIMIT),
        cost_estimate=pl.CostEstimate(
            flops=2 * count * depth * height * width,
            bytes_accessed=2 * (count * depth * (height + width) + height * width),
            transcendentals=0,
        ),
    )(*lefts, *rights)


def side_grads_kernel(steps, count, y_ref, *refs):
    lefts, rights = refs[:count], refs[count : 2 * count]
    total = sum(dot_tn(left[...], right[...]) for left, right in zip(lefts, rights))
    for turn, out in enumerate(refs[-2:]):

        @pl.when(pl.program_id(0) // steps == turn)
        def _():
            for piece in range(out.shape[0]):
                out[piece] = total[:, piece * WIDE : (piece + 1) * WIDE].astype(bf16)


def side_grads(lefts, rights):
    depth, height = lefts[0].shape
    width = rights[0].shape[1]
    half, pieces = height // 2, width // WIDE
    tile = half if half <= 640 else 512
    steps = half // tile
    count = len(lefts)
    y = (lax.axis_index("dp") % 2).astype(jnp.int32).reshape(1)

    def left_at(i, y):
        owner = (i // steps) * y[0] + (1 - i // steps) * (1 - y[0])
        return (0, owner * steps + i % steps)

    shape = jax.ShapeDtypeStruct((pieces, half, WIDE), bf16)
    return pl.pallas_call(
        partial(side_grads_kernel, steps, count),
        grid_spec=pltpu.PrefetchScalarGridSpec(
            num_scalar_prefetch=1,
            grid=(2 * steps,),
            in_specs=[pl.BlockSpec((depth, tile), left_at)] * count
            + [pl.BlockSpec((depth, width), lambda i, y: (0, 0))] * count,
            out_specs=[
                pl.BlockSpec((pieces, tile, WIDE), lambda i, y: (0, jnp.minimum(i, steps - 1), 0)),
                pl.BlockSpec((pieces, tile, WIDE), lambda i, y: (0, jnp.maximum(i - steps, 0), 0)),
            ],
        ),
        out_shape=[shape, shape],
        compiler_params=pltpu.CompilerParams(vmem_limit_bytes=VMEM_LIMIT),
        cost_estimate=pl.CostEstimate(
            flops=2 * count * depth * height * width,
            bytes_accessed=2 * (count * depth * (height + width) + height * width),
            transcendentals=0,
        ),
    )(y, *lefts, *rights)


def stacked(grads):
    return grads.reshape(-1, WIDE)


def unpack_kernel(pieces, *refs):
    count = len(refs) // (pieces + 1)
    for at in range(count):
        out = refs[count * pieces + at]
        for piece in range(pieces):
            out[:, piece * WIDE : (piece + 1) * WIDE] = refs[at * pieces + piece][0].astype(f32)


def unpack(height, width, tile, *places):
    half, pieces = height // 2, width // WIDE
    steps = half // tile

    def piece_spec(first, second, piece):
        begin, step = first[1] // tile, (second[1] - first[1]) // tile
        assert first[1] % tile == 0 and second[1] % tile == 0
        return pl.BlockSpec(
            (1, tile, WIDE),
            lambda i, j: (
                first[0] + i * (second[0] - first[0]),
                begin + i * step + piece * steps + j,
                0,
            ),
        )

    count = len(places)
    return pl.pallas_call(
        partial(unpack_kernel, pieces),
        grid=(2, steps),
        in_specs=[
            piece_spec(first, second, piece)
            for _, first, second in places
            for piece in range(pieces)
        ],
        out_specs=[pl.BlockSpec((tile, width), lambda i, j: (i * steps + j, 0))] * count,
        out_shape=[jax.ShapeDtypeStruct((height, width), f32)] * count,
        compiler_params=pltpu.CompilerParams(vmem_limit_bytes=60 * 1024 * 1024),
        cost_estimate=pl.CostEstimate(
            flops=count * height * width,
            bytes_accessed=6 * count * height * width,
            transcendentals=0,
        ),
    )(*[stack for stack, _, _ in places for _ in range(pieces)])


def on_device(
    tokens,
    patches,
    text_lengths,
    prefix_lengths,
    group_map,
    ratio,
    cotangent,
    q_self,
    k_self,
    v_self,
    o_self,
    q_cross,
    k_cross,
    v_cross,
    o_cross,
    w_gate,
    w_up,
    w_down,
    gain_attn,
    gain_cross,
    gain_mlp,
):
    local_rows = tokens.shape[0]
    examples = text_lengths.shape[0]
    patch = patches.shape[0] // examples
    local_examples = local_rows // SEQ
    fast = lax.axis_size("mp") == 4 and lax.axis_size("dp") == 8 and local_examples % 2 == 0
    batches = 2 if fast else 1
    each = local_examples // batches
    rows = each * SEQ
    width = q_self.shape[1]

    lens_f = text_lengths.astype(f32)
    robot = (group_map == 0).astype(f32)
    web = 1.0 - robot
    local_counts = jnp.stack([jnp.sum(lens_f * robot), jnp.sum(lens_f * web)])
    counts = butterfly(jnp.broadcast_to(local_counts[:, None], (2, 128)), "dp")[:, 0]
    ratio_f = ratio.astype(f32)
    share = ratio_f / jnp.sum(ratio_f)
    group_scale = share * jnp.sum(counts) / jnp.maximum(counts, 1.0)
    example_scale = robot * group_scale[0] + web * group_scale[1]
    mine = lax.axis_index("mp") * local_examples
    own_scale = lax.dynamic_slice_in_dim(example_scale, mine, local_examples, 0)
    own_length = lax.dynamic_slice_in_dim(text_lengths, mine, local_examples, 0)
    place = jnp.arange(SEQ, dtype=jnp.int32)
    live = (place[None, :] < own_length[:, None]).astype(f32)
    row_weight = (own_scale[:, None] * live).reshape(local_rows)

    owners = block_owners()
    which, lengths, prefixes = [], [], []
    for b in range(batches):
        ids = (
            owners[:, None] * local_examples + b * each + jnp.arange(each, dtype=jnp.int32)[None, :]
        ).reshape(-1).astype(jnp.int32)
        which.append(ids)
        lengths.append(jnp.take(text_lengths, ids))
        prefixes.append(jnp.take(prefix_lengths, ids))

    w_qkv = jnp.concatenate([q_self, k_self, v_self], axis=1)

    each_batch = range(batches)
    last = batches - 1

    def part(tensor, b):
        return tensor[b * rows : (b + 1) * rows]

    def product(left, right, dot):
        return lambda low, high: dot(left[low:high], right)

    outer = [part(cotangent, b).astype(f32) * part(row_weight, b)[:, None] for b in each_batch]
    outer_low = [item.astype(bf16) for item in outer]
    x_zero = [part(tokens, b).astype(f32) for b in each_batch]
    norm_one = [normalize(x_zero[b], gain_attn) for b in each_batch]
    scale_one = [item[1] for item in norm_one]
    norm_one = [item[0] for item in norm_one]

    none = [None] * batches
    full_one, qkv, mixed_self, x_one, norm_two, scale_two = ([None] * batches for _ in range(6))
    full_two, query, mixed_cross, x_two, norm_three, scale_three = (
        [None] * batches for _ in range(6)
    )
    full_three, grad_three, hidden, d_gate, d_up, back_three = ([None] * batches for _ in range(6))
    grad_two_rows, grad_two, d_query, grad_one_rows, grad_one, d_qkv = (
        [None] * batches for _ in range(6)
    )
    gain_mlp_parts, gain_cross_parts, gain_attn_parts, grad_input, output = (
        [None] * batches for _ in range(5)
    )

    def self_block(b, arrived):
        full_one[b], qkv[b] = gathered_dot(norm_one[b], arrived, w_qkv, False, 1)
        mixed_self[b] = self_forward(qkv[b], lengths[b], prefixes[b])
        return scattered_dot([mixed_self[b]], [o_self], False, True, 2)

    def self_norm(b, arrived):
        x_one[b] = x_zero[b] + scatter_end(arrived)
        norm_two[b], scale_two[b] = normalize(x_one[b], gain_cross)

    def cross_block(b, arrived, keys, values):
        full_two[b], query[b] = gathered_dot(norm_two[b], arrived, q_cross, False, 3)
        mixed_cross[b] = cross_forward(query[b], keys, values, which[b], patch)
        return scattered_dot([mixed_cross[b]], [o_cross], False, True, 4)

    def cross_norm(b, arrived):
        x_two[b] = x_one[b] + scatter_end(arrived)
        norm_three[b], scale_three[b] = normalize(x_two[b], gain_mlp)

    def mlp_block(b, arrived_norm, arrived_grad):
        full_three[b], grad_three[b], hidden[b], d_gate[b], d_up[b] = gathered_mlp(
            norm_three[b], arrived_norm, outer_low[b], arrived_grad, w_gate, w_up, w_down, 5
        )

    def mlp_back(b):
        return scattered_dot([d_gate[b], d_up[b]], [w_gate, w_up], True, False, 6)

    def mlp_norm_back(b, arrived):
        back, gain_mlp_parts[b] = norm_back(
            x_two[b], scale_three[b], gain_mlp, scatter_end(arrived)
        )
        grad_two_rows[b] = outer[b] + back
        return grad_two_rows[b].astype(bf16)

    def cross_back(b, own, arrived, keys, values, earlier):
        grad_two[b], d_mixed = gathered_dot(own, arrived, o_cross, True, 7)
        d_query[b], *d_kv = cross_backward(
            query[b], keys, values, d_mixed, which[b], patch, earlier
        )
        return scattered_dot([d_query[b]], [q_cross], True, False, 8), d_kv

    def cross_norm_back(b, arrived):
        back, gain_cross_parts[b] = norm_back(
            x_one[b], scale_two[b], gain_cross, scatter_end(arrived)
        )
        grad_one_rows[b] = grad_two_rows[b] + back
        return grad_one_rows[b].astype(bf16)

    def self_back(b, own, arrived):
        grad_one[b], d_mixed = gathered_dot(own, arrived, o_self, True, 9)
        d_qkv[b] = self_backward(qkv[b], d_mixed, lengths[b], prefixes[b])
        return scattered_dot([d_qkv[b]], [w_qkv], True, False, 10)

    def self_norm_back(b, arrived):
        back, gain_attn_parts[b] = norm_back(
            x_zero[b], scale_one[b], gain_attn, scatter_end(arrived)
        )
        grad_input[b] = grad_one_rows[b] + back

    def project_out(b):
        return scattered_dot([hidden[b]], [w_down], False, True, 11)

    sent = list(none)
    got = list(none)
    back = list(none)
    grads = list(none)
    own = list(none)
    shown = list(none)
    if fast:
        got[0] = gather_start(norm_one[0])
        got[0], norm_one[1], w_qkv, outer_low, outer, which, lengths, prefixes = fence(
            got[0], norm_one[1], w_qkv, outer_low, outer, which, lengths, prefixes
        )
        got[1] = gather_start(norm_one[1])
        sent[0] = self_block(0, got[0])
        sent[0], got[1], outer_low = fence(sent[0], got[1], outer_low)
        grads[0] = gather_start(outer_low[0])
        sent[1] = self_block(1, got[1])
        sent, grads[0], k_cross = fence(sent, grads[0], k_cross)
        back[0] = scatter_move(sent[0])
        keys = dot_nn(patches, k_cross).astype(bf16)
        back[0], sent[1], keys, v_cross = fence(back[0], sent[1], keys, v_cross)
        back[1] = scatter_move(sent[1])
        self_norm(0, back[0])
        values = dot_nn(patches, v_cross).astype(bf16)
        norm_two[0], back[1], values = fence(norm_two[0], back[1], values)
        got[0] = gather_start(norm_two[0])
        self_norm(1, back[1])
        norm_two[1], got[0], outer_low = fence(norm_two[1], got[0], outer_low)
        got[1] = gather_start(norm_two[1])
        sent[0] = cross_block(0, got[0], keys, values)
        sent[0], got[1] = fence(sent[0], got[1])
        back[0] = scatter_move(sent[0])
        sent[1] = cross_block(1, got[1], keys, values)
        sent[1], back[0] = fence(sent[1], back[0])
        back[1] = scatter_move(sent[1])
        cross_norm(0, back[0])
        norm_three[0], back[1], outer_low = fence(norm_three[0], back[1], outer_low)
        got[0] = gather_start(norm_three[0])
        cross_norm(1, back[1])
        got[0], outer_low, norm_three[1] = fence(got[0], outer_low, norm_three[1])
        got[1] = gather_start(norm_three[1])
        mlp_block(0, got[0], grads[0])
        got[1], d_gate[0], d_up[0], outer_low[1] = fence(
            got[1], d_gate[0], d_up[0], outer_low[1]
        )
        grads[1] = gather_start(outer_low[1])
        sent[0] = mlp_back(0)
        grads[1], got[1], sent[0] = fence(grads[1], got[1], sent[0])
        back[0] = scatter_move(sent[0])
        mlp_block(1, got[1], grads[1])
        back[0], d_gate[1], d_up[1], hidden = fence(back[0], d_gate[1], d_up[1], hidden)
        own[0] = mlp_norm_back(0, back[0])
        got[0] = gather_start(own[0])
        sent[1] = mlp_back(1)
        down_other, down_mine = side_grads(hidden, grad_three)
        own[0], got[0], sent[1], d_gate, d_up, down_other = fence(
            own[0], got[0], sent[1], d_gate, d_up, down_other
        )
        back[1] = scatter_move(sent[1])
        down_sent = flip(down_other, "dp", 1)
        gate_other, gate_mine = side_grads(full_three, d_gate)
        up_other, up_mine = side_grads(full_three, d_up)
        back[1], gate_other, up_other = fence(back[1], gate_other, up_other)
        own[1] = mlp_norm_back(1, back[1])
        got[1] = gather_start(own[1])
        gate_sent = flip(gate_other, "dp", 1)
        sent[0], d_kv = cross_back(0, own[0], got[0], keys, values, ())
        own[1], got[1], sent[0], d_kv, down_sent, up_other = fence(
            own[1], got[1], sent[0], d_kv, down_sent, up_other
        )
        back[0] = scatter_move(sent[0])
        up_sent = flip(up_other, "dp", 1)
        sent[1], d_kv = cross_back(1, own[1], got[1], keys, values, d_kv)
        sent[1], back[0], d_kv, mixed_cross, hidden = fence(
            sent[1], back[0], d_kv, mixed_cross, hidden
        )
        back[1] = scatter_move(sent[1])
        own[0] = cross_norm_back(0, back[0])
        o_other, o_mine = side_grads(mixed_cross, grad_two)
        q_other, q_mine = side_grads(full_two, d_query)
        shown[0] = project_out(0)
        own[0], back[1], d_kv, o_other, q_other, shown[0], gate_sent, down_mine = fence(
            own[0], back[1], d_kv, o_other, q_other, shown[0], gate_sent, down_mine
        )
        got[0] = gather_start(own[0])
        o_sent, q_sent = flip(o_other, "dp", 1), flip(q_other, "dp", 1)
        own[1] = cross_norm_back(1, back[1])
        k_other, k_mine = side_grads([patches], [d_kv[0]])
        v_other, v_mine = side_grads([patches], [d_kv[1]])
        got[0], own[1], k_other, v_other, hidden, up_sent, gate_mine = fence(
            got[0], own[1], k_other, v_other, hidden, up_sent, gate_mine
        )
        got[1] = gather_start(own[1])
        k_sent, v_sent = flip(k_other, "dp", 1), flip(v_other, "dp", 1)
        sent[0] = self_back(0, own[0], got[0])
        got[1], sent[0], o_sent, q_sent, up_mine = fence(got[1], sent[0], o_sent, q_sent, up_mine)
        back[0] = scatter_move(sent[0])
        sent[1] = self_back(1, own[1], got[1])
        back[0], sent[1], mixed_self, hidden, o_mine, q_mine = fence(
            back[0], sent[1], mixed_self, hidden, o_mine, q_mine
        )
        back[1] = scatter_move(sent[1])
        self_norm_back(0, back[0])
        d_oself = weight_grad(mixed_self, grad_one)
        d_wqkv = weight_grad(full_one, d_qkv)
        shown[1] = project_out(1)
        back[1], grad_input[0], d_wqkv, d_oself, shown, k_sent, v_sent = fence(
            back[1], grad_input[0], d_wqkv, d_oself, shown, k_sent, v_sent
        )
        self_norm_back(1, back[1])
        back = [scatter_move(shown[b]) for b in each_batch]
        opened = [d_wqkv, d_oself]
        paired = [down_mine, gate_mine, up_mine, q_mine, k_mine, v_mine, o_mine]
        arrived = [down_sent, gate_sent, up_sent, q_sent, k_sent, v_sent, o_sent]
        open_sum, paired_sum = sum_chunks(
            *([stacked(item) for item in items] for items in (opened, paired, arrived))
        )
    else:
        sent[0] = self_block(0, gather_start(norm_one[0]))
        self_norm(0, scatter_move(sent[0]))
        keys = dot_nn(patches, k_cross).astype(bf16)
        values = dot_nn(patches, v_cross).astype(bf16)
        sent[0] = cross_block(0, gather_start(norm_two[0]), keys, values)
        cross_norm(0, scatter_move(sent[0]))
        mlp_block(0, gather_start(norm_three[0]), gather_start(outer_low[0]))
        own[0] = mlp_norm_back(0, scatter_move(mlp_back(0)))
        sent[0], d_kv = cross_back(0, own[0], gather_start(own[0]), keys, values, ())
        own[0] = cross_norm_back(0, scatter_move(sent[0]))
        sent[0] = self_back(0, own[0], gather_start(own[0]))
        self_norm_back(0, scatter_move(sent[0]))
        sums = lax.psum(
            [
                item.astype(bf16)
                for item in (
                    dot_tn(full_one[0], d_qkv[0]),
                    dot_tn(mixed_self[0], grad_one[0]),
                    dot_tn(full_two[0], d_query[0]),
                    dot_tn(patches, d_kv[0]),
                    dot_tn(patches, d_kv[1]),
                    dot_tn(mixed_cross[0], grad_two[0]),
                    dot_tn(full_three[0], d_gate[0]),
                    dot_tn(full_three[0], d_up[0]),
                    dot_tn(hidden[0], grad_three[0]),
                )
            ],
            "dp",
        )
        back = [scatter_move(project_out(0))]
    gains = jnp.stack(
        [sum(parts) for parts in (gain_attn_parts, gain_cross_parts, gain_mlp_parts)]
    )
    if fast:
        open_sum, paired_sum, back, gains = fence(open_sum, paired_sum, back, gains)

        whole = open_sum[None]
        half = q_self.shape[0] // 2
        pieces = width // WIDE
        places, start = [], 0
        for weight in (w_down, w_gate, w_up, q_cross, k_cross, v_cross, o_cross):
            places.append((paired_sum, (0, start), (1, start)))
            start += weight.size // WIDE // 2
        self_places = [
            (whole, (0, at * pieces * half), (0, (3 + at) * pieces * half)) for at in range(3)
        ]
        start = w_qkv.size // WIDE
        o_place = (whole, (0, start), (0, start + o_self.size // WIDE // 2))
        groups = [
            unpack(*w_down.shape, w_down.shape[0] // 4, places[0]),
            unpack(*w_gate.shape, 256, *places[1:3]),
            unpack(*q_self.shape, 256, *places[3:6], *self_places),
            unpack(*o_self.shape, o_self.shape[0] // 4, places[6], o_place),
        ]
        gains = gains + flip(gains, "mp", 1)
        for at, (axis, bit) in enumerate((("mp", 2), ("dp", 1), ("dp", 2), ("dp", 4))):
            arrived, groups[at] = fence(flip(gains, axis, bit), groups[at])
            gains = gains + arrived
        (d_wdown,), (d_wgate, d_wup), shared, (d_ocross, d_oself) = groups
        d_qcross, d_kcross, d_vcross, *d_self = shared
    else:
        (
            d_wqkv,
            d_oself,
            d_qcross,
            d_kcross,
            d_vcross,
            d_ocross,
            d_wgate,
            d_wup,
            d_wdown,
        ) = [item.astype(f32) for item in sums]
        d_self = [d_wqkv[:, at * width : (at + 1) * width] for at in range(3)]
    output = jnp.concatenate(
        [(x_two[b] + scatter_end(back[b])).astype(bf16) for b in each_batch], axis=0
    )
    grad_input = jnp.concatenate(grad_input, axis=0)
    if not fast:
        gains = butterfly(butterfly(gains, "mp"), "dp")
    return (
        output,
        grad_input,
        *d_self,
        d_oself,
        d_qcross,
        d_kcross,
        d_vcross,
        d_ocross,
        d_wgate,
        d_wup,
        d_wdown,
        gains[0],
        gains[1],
        gains[2],
    )


def solution(mesh):
    by_rows = P(("dp", "mp"), None)
    columns = P(None, "mp")
    rows = P("mp", None)
    weights = (columns, columns, columns, rows, columns, columns, columns, rows, columns, columns, rows)
    in_specs = (
        (by_rows, P("dp", None), P("dp"), P("dp"), P("dp"), P(), by_rows) + weights + (P(), P(), P())
    )
    out_specs = (by_rows, by_rows) + weights + (P(), P(), P())
    return jax.shard_map(
        on_device, mesh=mesh, in_specs=in_specs, out_specs=out_specs, check_vma=False
    )
```

```python
from functools import partial

import jax
import jax.numpy as jnp
from jax import lax
from jax.experimental import pallas as pl
from jax.experimental.pallas import tpu as pltpu
from jax.sharding import PartitionSpec as P

HEAD = 64
SEQ = 128
PAIR = 2 * HEAD
epsilon = 1e-06
f32 = jnp.float32
bf16 = jnp.bfloat16
VMEM_LIMIT = 56 * 1024 * 1024
MESH = pl.DeviceIdType.MESH


def dot_nn(left, right):
    return jnp.dot(left, right, preferred_element_type=f32)


def dot_tn(left, right):
    return lax.dot_general(left, right, (((0,), (0,)), ((), ())), preferred_element_type=f32)


def dot_nt(left, right):
    return lax.dot_general(left, right, (((1,), (1,)), ((), ())), preferred_element_type=f32)


def normalize(values_in, gain):
    row_scale = lax.rsqrt(jnp.mean(values_in * values_in, axis=-1, keepdims=True) + epsilon)
    return ((values_in * row_scale * gain).astype(bf16), row_scale)


def norm_back(values_in, row_scale, gain, incoming):
    weighted = incoming * gain
    inner = jnp.mean(weighted * values_in, axis=-1, keepdims=True)
    return (
        row_scale * weighted - values_in * row_scale**3 * inner,
        jnp.sum(incoming * values_in * row_scale, axis=0),
    )


def first_head():
    return lax.broadcasted_iota(jnp.int32, (SEQ, PAIR), 1) < HEAD


def stack_pair(rows, first):
    zero = jnp.zeros_like(rows)
    return jnp.concatenate([jnp.where(first, rows, zero), jnp.where(first, zero, rows)], axis=0)


def unstack_pair(stacked, first):
    return jnp.where(first, stacked[:SEQ], stacked[SEQ:])


def self_mask(length, prefix):
    query_at = lax.broadcasted_iota(jnp.int32, (2 * SEQ, SEQ), 0) % SEQ
    key_at = lax.broadcasted_iota(jnp.int32, (2 * SEQ, SEQ), 1)
    return (key_at < length) & ((key_at <= query_at) | (key_at < prefix))


def pair_probs(stacked_query, keys, mask):
    scores = dot_nt(stacked_query, keys)
    if mask is not None:
        scores = jnp.where(mask, scores, -1e30)
    expd = jnp.exp(scores - jnp.max(scores, axis=-1, keepdims=True))
    return expd * (1.0 / jnp.sum(expd, axis=-1, keepdims=True))


def pair_forward(query, keys, values, mask, first):
    scaled = stack_pair(query * jnp.asarray(HEAD**-0.5, bf16), first)
    probs = pair_probs(scaled, keys, mask).astype(bf16)
    return unstack_pair(dot_nn(probs, values), first).astype(bf16), probs


def pair_backward(grad, query, keys, values, probs, first):
    scaled = stack_pair(query * jnp.asarray(HEAD**-0.5, bf16), first)
    grads = stack_pair(grad, first)
    d_probs = dot_nt(grads, values)
    wide = probs.astype(f32)
    weighted = wide * d_probs
    d_scores = (weighted - wide * jnp.sum(weighted, axis=-1, keepdims=True)).astype(bf16)
    d_query = unstack_pair(dot_nn(d_scores, keys), first) * HEAD**-0.5
    d_keys = dot_tn(d_scores, scaled)
    d_values = dot_tn(probs, grads)
    return d_query.astype(bf16), d_keys.astype(bf16), d_values.astype(bf16)


def lanes(part, width, pair):
    return slice(part * width + pair * PAIR, part * width + (pair + 1) * PAIR)


def self_forward_kernel(length_ref, prefix_ref, qkv_ref, out_ref, probs_ref):
    at = pl.program_id(0)
    width = out_ref.shape[1]
    first = first_head()
    mask = self_mask(length_ref[at], prefix_ref[at])
    for pair in range(width // PAIR):
        out_ref[:, lanes(0, width, pair)], probs_ref[0, pair] = pair_forward(
            qkv_ref[:, lanes(0, width, pair)],
            qkv_ref[:, lanes(1, width, pair)],
            qkv_ref[:, lanes(2, width, pair)],
            mask,
            first,
        )


def self_backward_kernel(qkv_ref, probs_ref, grad_ref, out_ref):
    width = grad_ref.shape[1]
    first = first_head()
    for pair in range(width // PAIR):
        for part, value in enumerate(
            pair_backward(
                grad_ref[:, lanes(0, width, pair)],
                qkv_ref[:, lanes(0, width, pair)],
                qkv_ref[:, lanes(1, width, pair)],
                qkv_ref[:, lanes(2, width, pair)],
                probs_ref[0, pair],
                first,
            )
        ):
            out_ref[:, lanes(part, width, pair)] = value


def cross_forward_kernel(which_ref, query_ref, key_ref, value_ref, out_ref, probs_ref):
    width = out_ref.shape[1]
    first = first_head()
    for pair in range(width // PAIR):
        at = lanes(0, width, pair)
        out_ref[:, at], probs_ref[0, pair] = pair_forward(
            query_ref[:, at], key_ref[:, at], value_ref[:, at], None, first
        )


def cross_backward_kernel(which_ref, query_ref, key_ref, value_ref, probs_ref, grad_ref, *rest):
    d_query_ref, d_key_ref, d_value_ref = rest[-3:]
    width = query_ref.shape[1]
    first = first_head()
    for pair in range(width // PAIR):
        at = lanes(0, width, pair)
        d_query_ref[:, at], d_key_ref[:, at], d_value_ref[:, at] = pair_backward(
            grad_ref[:, at],
            query_ref[:, at],
            key_ref[:, at],
            value_ref[:, at],
            probs_ref[0, pair],
            first,
        )


def params():
    return pltpu.CompilerParams(vmem_limit_bytes=ROOM)


def by_row(width):
    return pl.BlockSpec((SEQ, width), lambda i, *_: (i, 0))


def attention_cost(examples, width, keys, dots, moved):
    return pl.CostEstimate(
        flops=dots * 2 * examples * SEQ * keys * width * 2,
        bytes_accessed=moved,
        transcendentals=examples * SEQ * keys * width // HEAD,
    )


def probs_spec(width, keys):
    return pl.BlockSpec((1, width // PAIR, 2 * SEQ, keys), lambda i, *_: (i, 0, 0, 0))


def probs_shape(rows, width, keys):
    return pltpu.HBM((rows // SEQ, width // PAIR, 2 * SEQ, keys), bf16)


def self_forward(qkv, length, prefix):
    rows, triple = qkv.shape
    width = triple // 3
    return pl.pallas_call(
        self_forward_kernel,
        grid_spec=pltpu.PrefetchScalarGridSpec(
            num_scalar_prefetch=2,
            grid=(rows // SEQ,),
            in_specs=[by_row(triple)],
            out_specs=[by_row(width), probs_spec(width, SEQ)],
        ),
        out_shape=[
            jax.ShapeDtypeStruct((rows, width), bf16),
            probs_shape(rows, width, SEQ),
        ],
        compiler_params=params(),
        cost_estimate=attention_cost(rows // SEQ, width, SEQ, 2, rows * width * 12),
    )(length, prefix, qkv)


def self_backward(qkv, probs, grad):
    rows, triple = qkv.shape
    width = triple // 3
    return pl.pallas_call(
        self_backward_kernel,
        grid=(rows // SEQ,),
        in_specs=[by_row(triple), probs_spec(width, SEQ), by_row(width)],
        out_specs=by_row(triple),
        out_shape=jax.ShapeDtypeStruct((rows, triple), bf16),
        compiler_params=params(),
        cost_estimate=attention_cost(rows // SEQ, width, SEQ, 4, rows * width * 18),
    )(qkv, probs, grad)


def cross_forward(query, keys, values, which, patch):
    rows, width = query.shape
    by_patch = pl.BlockSpec((patch, width), lambda i, which: (which[i], 0))
    return pl.pallas_call(
        cross_forward_kernel,
        grid_spec=pltpu.PrefetchScalarGridSpec(
            num_scalar_prefetch=1,
            grid=(rows // SEQ,),
            in_specs=[by_row(width), by_patch, by_patch],
            out_specs=[by_row(width), probs_spec(width, patch)],
        ),
        out_shape=[
            jax.ShapeDtypeStruct((rows, width), bf16),
            probs_shape(rows, width, patch),
        ],
        compiler_params=params(),
        cost_estimate=attention_cost(rows // SEQ, width, patch, 2, rows * width * 20),
    )(which, query, keys, values)


def cross_backward(query, keys, values, probs, grad, which, patch, earlier):
    rows, width = query.shape
    by_patch = pl.BlockSpec((patch, width), lambda i, which: (which[i], 0))
    in_specs = [by_row(width), by_patch, by_patch, probs_spec(width, patch), by_row(width)]
    operands = [which, query, keys, values, probs, grad]
    aliases = {}
    for at, item in enumerate(earlier):
        in_specs.append(pl.BlockSpec(memory_space=pl.ANY))
        aliases[len(operands)] = 1 + at
        operands.append(item)
    whole = pltpu.HBM(keys.shape, bf16)
    return pl.pallas_call(
        cross_backward_kernel,
        grid_spec=pltpu.PrefetchScalarGridSpec(
            num_scalar_prefetch=1,
            grid=(rows // SEQ,),
            in_specs=in_specs,
            out_specs=[by_row(width), by_patch, by_patch],
        ),
        out_shape=[jax.ShapeDtypeStruct((rows, width), bf16), whole, whole],
        input_output_aliases=aliases,
        compiler_params=params(),
        cost_estimate=attention_cost(rows // SEQ, width, patch, 4, rows * width * 32),
    )(*operands)


def other_core():
    me = lax.axis_index("mp")
    return me + 1 - 2 * lax.rem(me, 2)


def meet(partner):
    barrier = pltpu.get_barrier_semaphore()
    pl.semaphore_signal(barrier, inc=1, device_id={"mp": partner}, device_id_type=MESH)
    pl.semaphore_wait(barrier, 1)


def to_partner(source, target, send_sem, recv_sem, partner):
    return pltpu.make_async_remote_copy(
        src_ref=source,
        dst_ref=target,
        send_sem=send_sem,
        recv_sem=recv_sem,
        device_id={"mp": partner},
        device_id_type=MESH,
    )


def columns_of(weight, tile, size, transposed):
    at = pl.ds(pl.multiple_of(tile * size, size), size)
    return weight[at, :] if transposed else weight[:, at]


def gathered_kernel(transposed, size, own, beside, across, weight, full, out, corner, sems, local):
    dot = dot_nt if transposed else dot_nn
    rows = own.shape[0]
    blocks = (own, beside, across, corner)
    partner = other_core()
    given = to_partner(across, corner, sems.at[0], sems.at[1], partner)
    keep = [
        pltpu.make_async_copy(block, full.at[pl.ds(at * rows, rows)], local.at[at])
        for at, block in enumerate(blocks)
    ]
    meet(partner)
    given.start()
    for at in range(3):
        keep[at].start()

    def multiply(places):
        @pl.loop(0, out.shape[1] // size)
        def _(tile):
            right = columns_of(weight, tile, size, transposed)
            to = pl.ds(pl.multiple_of(tile * size, size), size)
            for at in places:
                out[at * rows : (at + 1) * rows, to] = dot(blocks[at][...], right).astype(bf16)

    multiply((0, 1, 2))
    given.wait()
    keep[3].start()
    multiply((3,))
    for at in range(4):
        keep[at].wait()


IN_VMEM = pl.BlockSpec(memory_space=pltpu.VMEM)
ROOM = 24 * 1024 * 1024


def gathered_dot(own, arrived, weight, transposed, ident):
    if lax.axis_size("mp") != 4:
        dot = dot_nt if transposed else dot_nn
        return arrived, dot(arrived, weight).astype(bf16)
    across, beside = arrived
    rows, model = own.shape
    units = weight.shape[0 if transposed else 1]
    return pl.pallas_call(
        partial(gathered_kernel, transposed, 512),
        in_specs=[IN_VMEM] * 4,
        out_specs=[pl.BlockSpec(memory_space=pltpu.HBM), IN_VMEM],
        out_shape=[
            pltpu.HBM((4 * rows, model), bf16),
            jax.ShapeDtypeStruct((4 * rows, units), bf16),
        ],
        scratch_shapes=[
            pltpu.VMEM((rows, model), bf16),
            pltpu.SemaphoreType.DMA((2,)),
            pltpu.SemaphoreType.DMA((4,)),
        ],
        compiler_params=pltpu.CompilerParams(
            collective_id=ident, has_side_effects=True, vmem_limit_bytes=ROOM
        ),
        cost_estimate=pl.CostEstimate(
            flops=8 * rows * model * units,
            bytes_accessed=14 * rows * model + 4 * model * units + 8 * rows * units,
            transcendentals=0,
        ),
    )(own, beside, across, weight)


def scattered_kernel(transposed, count, size, *refs):
    dot = dot_nt if transposed else dot_nn
    lefts, weights = refs[:count], refs[count : 2 * count]
    kept, passed, ready, landed, send_sem, recv_sem = refs[2 * count :]
    rows, model = kept.shape
    tiles = model // size
    partner = other_core()

    def given(tile):
        return to_partner(
            ready.at[tile], landed.at[tile], send_sem.at[tile], recv_sem.at[tile], partner
        )

    def block(at, tile):
        return sum(
            dot(
                left[at * rows : (at + 1) * rows, :],
                columns_of(weight, tile, size, transposed),
            )
            for left, weight in zip(lefts, weights)
        )

    meet(partner)

    @pl.loop(0, tiles)
    def _(tile):
        ready[tile, :rows, :] = block(1, tile).astype(bf16)
        ready[tile, rows:, :] = block(3, tile).astype(bf16)
        given(tile).start()

    @pl.loop(0, tiles)
    def _(tile):
        mine = block(0, tile)
        across = block(2, tile)
        given(tile).wait()
        to = pl.ds(pl.multiple_of(tile * size, size), size)
        kept[:, to] = mine + landed[tile, :rows, :].astype(f32)
        passed[:, to] = (across + landed[tile, rows:, :].astype(f32)).astype(bf16)


def scattered_dot(lefts, weights, transposed, wide, ident):
    if lax.axis_size("mp") != 4:
        dot = dot_nt if transposed else dot_nn
        term = sum(dot(left, weight) for left, weight in zip(lefts, weights))
        return (term if wide else term.astype(bf16),)
    rows = lefts[0].shape[0] // 4
    model = weights[0].shape[0 if transposed else 1]
    size = 512
    tiles = model // size
    depth = sum(item.shape[1] for item in lefts)
    return pl.pallas_call(
        partial(scattered_kernel, transposed, len(lefts), size),
        in_specs=[IN_VMEM] * (2 * len(lefts)),
        out_specs=[IN_VMEM, IN_VMEM],
        out_shape=[
            jax.ShapeDtypeStruct((rows, model), f32),
            jax.ShapeDtypeStruct((rows, model), bf16),
        ],
        scratch_shapes=[
            pltpu.VMEM((tiles, 2 * rows, size), bf16),
            pltpu.VMEM((tiles, 2 * rows, size), bf16),
            pltpu.SemaphoreType.DMA((tiles,)),
            pltpu.SemaphoreType.DMA((tiles,)),
        ],
        compiler_params=pltpu.CompilerParams(
            collective_id=ident,
            has_side_effects=True,
            vmem_limit_bytes=ROOM if depth < 2048 else 2 * ROOM,
        ),
        cost_estimate=pl.CostEstimate(
            flops=8 * rows * model * depth,
            bytes_accessed=8 * rows * depth + 4 * model * depth + 14 * rows * model,
            transcendentals=0,
        ),
    )(*lefts, *weights)


def mlp_rows(norm, grad, gate_ref, up_ref, down_ref):
    curve = 0.7978845608028654
    gate = dot_nn(norm, gate_ref[...])
    up = dot_nn(norm, up_ref[...])
    d_hidden = dot_nt(grad, down_ref[...])
    square = gate * gate
    bend = jnp.tanh(curve * gate * (1.0 + 0.044715 * square))
    half = 0.5 * (1.0 + bend)
    value = gate * half
    slope = half + 0.5 * curve * gate * (1.0 - bend * bend) * (1.0 + 0.134145 * square)
    return (
        (value * up).astype(bf16),
        (d_hidden * up * slope).astype(bf16),
        (d_hidden * value).astype(bf16),
    )


def mlp_kernel(norm_ref, grad_ref, gate_ref, up_ref, down_ref, hidden_ref, d_gate_ref, d_up_ref):
    rows = norm_ref.shape[0]
    step = min(rows, 256)
    for start in range(0, rows, step):
        at = slice(start, start + step)
        hidden_ref[at, :], d_gate_ref[at, :], d_up_ref[at, :] = mlp_rows(
            norm_ref[at, :], grad_ref[at, :], gate_ref, up_ref, down_ref
        )


def gathered_mlp_kernel(tiles, *refs):
    norms, grads = refs[:3], refs[3:6]
    gate_ref, up_ref, down_ref = refs[6:9]
    full_norm, full_grad, hidden_ref, d_gate_ref, d_up_ref = refs[9:14]
    corner_norm, corner_grad, sems, local = refs[14:]
    tile = pl.program_id(0)
    rows = norms[0].shape[0]
    partner = other_core()
    norms = (*norms, corner_norm)
    grads = (*grads, corner_grad)

    def given(at):
        source, target = ((norms[2], corner_norm), (grads[2], corner_grad))[at]
        return to_partner(source, target, sems.at[2 * at], sems.at[2 * at + 1], partner)

    def keep(which, at):
        source, target = ((norms, full_norm), (grads, full_grad))[which]
        return pltpu.make_async_copy(
            source[at], target.at[pl.ds(at * rows, rows)], local.at[which, at]
        )

    @pl.when(tile == 0)
    def _():
        meet(partner)
        for which in range(2):
            given(which).start()
        for which in range(2):
            for at in range(3):
                keep(which, at).start()

    for at in range(4):
        if at == 3:

            @pl.when(tile == 0)
            def _():
                for which in range(2):
                    given(which).wait()
                    keep(which, 3).start()

        place = slice(at * rows, (at + 1) * rows)
        hidden_ref[place, :], d_gate_ref[place, :], d_up_ref[place, :] = mlp_rows(
            norms[at][...], grads[at][...], gate_ref, up_ref, down_ref
        )

    @pl.when(tile == tiles - 1)
    def _():
        for which in range(2):
            for at in range(4):
                keep(which, at).wait()


def gathered_mlp(own_norm, arrived_norm, own_grad, arrived_grad, w_gate, w_up, w_down, ident):
    model, units = w_gate.shape
    if lax.axis_size("mp") != 4:
        return (
            arrived_norm,
            arrived_grad,
            *mlp(arrived_norm, arrived_grad, w_gate, w_up, w_down),
        )
    rows = own_norm.shape[0]
    tile = 256
    whole = pl.BlockSpec((rows, model), lambda i: (0, 0))
    columns = pl.BlockSpec((model, tile), lambda i: (0, i))
    out = pl.BlockSpec((4 * rows, tile), lambda i: (0, i))
    full = pl.BlockSpec(memory_space=pltpu.HBM)
    shape = jax.ShapeDtypeStruct((4 * rows, units), bf16)
    full_shape = pltpu.HBM((4 * rows, model), bf16)
    return pl.pallas_call(
        partial(gathered_mlp_kernel, units // tile),
        grid=(units // tile,),
        in_specs=[whole] * 6 + [columns, columns, pl.BlockSpec((tile, model), lambda i: (i, 0))],
        out_specs=[full, full, out, out, out],
        out_shape=[full_shape, full_shape, shape, shape, shape],
        scratch_shapes=[
            pltpu.VMEM((rows, model), bf16),
            pltpu.VMEM((rows, model), bf16),
            pltpu.SemaphoreType.DMA((4,)),
            pltpu.SemaphoreType.DMA((2, 4)),
        ],
        compiler_params=pltpu.CompilerParams(
            collective_id=ident, has_side_effects=True, vmem_limit_bytes=VMEM_LIMIT
        ),
        cost_estimate=pl.CostEstimate(
            flops=24 * rows * model * units,
            bytes_accessed=28 * rows * model + 6 * model * units + 24 * rows * units,
            transcendentals=4 * rows * units,
        ),
    )(
        own_norm,
        arrived_norm[1],
        arrived_norm[0],
        own_grad,
        arrived_grad[1],
        arrived_grad[0],
        w_gate,
        w_up,
        w_down,
    )


def mlp(norm, grad, w_gate, w_up, w_down):
    rows, model = norm.shape
    units = w_gate.shape[1]
    tile = 256 if units % 256 == 0 else units
    whole = pl.BlockSpec((rows, model), lambda i: (0, 0))
    columns = pl.BlockSpec((model, tile), lambda i: (0, i))
    out = pl.BlockSpec((rows, tile), lambda i: (0, i))
    shape = jax.ShapeDtypeStruct((rows, units), bf16)
    return pl.pallas_call(
        mlp_kernel,
        grid=(units // tile,),
        in_specs=[whole, whole, columns, columns, pl.BlockSpec((tile, model), lambda i: (i, 0))],
        out_specs=[out, out, out],
        out_shape=[shape, shape, shape],
        compiler_params=params(),
        cost_estimate=pl.CostEstimate(
            flops=6 * rows * model * units,
            bytes_accessed=4 * rows * model + 6 * model * units + 6 * rows * units,
            transcendentals=rows * units,
        ),
    )(norm, grad, w_gate, w_up, w_down)


def flip(tensor, axis, bit):
    count = lax.axis_size(axis)
    return lax.ppermute(tensor, axis, [(i, i ^ bit) for i in range(count)])


def butterfly(tensor, axis):
    count = lax.axis_size(axis)
    if count & (count - 1):
        return lax.psum(tensor, axis)
    bit = 1
    while bit < count:
        tensor = tensor + flip(tensor, axis, bit)
        bit *= 2
    return tensor


def block_owners():
    blocks = jnp.arange(lax.axis_size("mp"), dtype=jnp.int32)
    return lax.axis_index("mp") ^ blocks if lax.axis_size("mp") == 4 else blocks


def fence(*values):
    return lax.optimization_barrier(values)


def gather_start(rows_local):
    if lax.axis_size("mp") != 4:
        return lax.all_gather(rows_local, "mp", axis=0, tiled=True)
    return flip(rows_local, "mp", 2), flip(rows_local, "mp", 1)


def scatter_move(sent):
    if lax.axis_size("mp") != 4:
        return None, lax.psum_scatter(sent[0], "mp", scatter_dimension=0, tiled=True)
    return sent[0], flip(sent[1], "mp", 2)


def scatter_end(arrived):
    if lax.axis_size("mp") != 4:
        return arrived[1].astype(f32)
    return arrived[0] + arrived[1].astype(f32)


CHUNK = 256
WIDE = 256
LANDINGS = 7
PERIOD = 9
PAIRED = 6
LAST_HOP = (8, 9, 11, 13, 15, 16)


class Late:
    def __init__(self, make):
        self.make = make

    def start(self):
        self.make().start()

    def wait(self):
        self.make().wait()

    def wait_send(self):
        self.make().wait_send()

    def wait_recv(self):
        self.make().wait_recv()


def sum_kernel(cycles, paired_count, late, *refs):
    inputs, refs = refs[: 8 + 2 * paired_count], refs[8 + 2 * paired_count :]
    factors = (inputs[0:4], inputs[4:8])
    paired_in = inputs[8 : 8 + paired_count]
    arrived_in = list(inputs[8 + paired_count :])
    late_other = arrived_in[late]
    open_out, paired_out, late_arrived = refs[:3]
    arrived_in[late] = late_arrived
    (
        opened,
        paired,
        open_land,
        paired_land,
        open_send,
        open_recv,
        open_local,
        paired_send,
        paired_recv,
        paired_local,
        fill_sem,
        ring,
        ring_sem,
        factor,
        factor_sem,
        late_send,
        late_recv,
    ) = refs[3:]
    at = lax.axis_index("dp")
    y = lax.rem(at, 2)
    z = lax.div(at, 2)
    inner = (z == 1) | (z == 2)
    outer = (z == 0) | (z == 3)
    beside = z * 2 + (1 - y)
    along = at + jnp.where(lax.rem(z, 2) == 0, 2, -2)
    facing = (3 - z) * 2 + y
    side = z - 1
    paired_chunks = paired.shape[0] // CHUNK

    def rows_of(index):
        return pl.ds(pl.multiple_of(index * CHUNK, CHUNK), CHUNK)

    barrier = pltpu.get_barrier_semaphore()

    def greet(target):
        pl.semaphore_signal(barrier, inc=1, device_id={"dp": target}, device_id_type=MESH)

    greet(beside)
    greet(along)

    fills = []
    start = 0
    for source in paired_in:
        place = paired.at[pl.ds(start, source.shape[0])]
        fills.append(pltpu.make_async_copy(source, place, fill_sem.at[len(fills)]))
        start += source.shape[0]
    for fill in fills:
        fill.start()

    first_height, first_width = factors[0][0].shape[1], factors[0][2].shape[1]
    first_pieces = first_width // WIDE
    first_groups = first_height * first_width // (CHUNK * WIDE * 4)
    second_pieces = factors[1][2].shape[1] // WIDE
    chunk_count = cycles * 8

    def place_of(number):
        group = (number // 4 % 2) * cycles + number // 8
        return group, number % 4

    def factor_copies(which, left_at, right_at, slot):
        copies = []
        for at in range(4):
            column = left_at if at < 2 else right_at
            columns = pl.ds(pl.multiple_of(column * WIDE, WIDE), WIDE)
            copies.append(
                pltpu.make_async_copy(
                    factors[which][at].at[:, columns], factor.at[slot, at], factor_sem.at[slot, at]
                )
            )
        return copies

    def load(number):
        group, member = place_of(number)
        slot = lax.rem(number, 2)

        @pl.when((number < chunk_count) & (group < first_groups))
        def _():
            left = (group // first_pieces) * (first_height // 2 // WIDE) + member
            for copy in factor_copies(0, left, group % first_pieces, slot):
                copy.start()

        @pl.when((number < chunk_count) & (group >= first_groups))
        def _():
            chunk = (group - first_groups) * 4 + member
            for copy in factor_copies(1, chunk // second_pieces, chunk % second_pieces, slot):
                copy.start()

    def multiply(number):
        group, member = place_of(number)
        slot = lax.rem(number, 2)
        load(number + 1)
        for copy in factor_copies(0, 0, 0, slot):
            copy.wait()
        product = dot_tn(factor[slot, 0], factor[slot, 2]) + dot_tn(
            factor[slot, 1], factor[slot, 3]
        )
        opened[rows_of(group * 4 + member), :] = product.astype(bf16)

    load(0)

    @pl.loop(0, 8)
    def _(number):
        multiply(number)

    @pl.when(inner)
    def _():
        greet(facing)
        pl.semaphore_wait(barrier, 3)

    @pl.when(outer)
    def _():
        pl.semaphore_wait(barrier, 2)

    for fill in fills:
        fill.wait()

    def remote(source, target, send_sem, recv_sem, device):
        return Late(
            lambda: pltpu.make_async_remote_copy(
                src_ref=source,
                dst_ref=target,
                send_sem=send_sem,
                recv_sem=recv_sem,
                device_id={"dp": device},
                device_id_type=MESH,
            )
        )

    def add(place, landing):
        @pl.loop(0, CHUNK // 32)
        def _(step):
            rows = pl.ds(pl.multiple_of(step * 32, 32), 32)
            place[rows, :] = (
                place[rows, :].astype(f32) + landing[rows, :].astype(f32)
            ).astype(bf16)

    def everyone(descriptor, after):
        def finish():
            descriptor.wait()
            after()

        return descriptor.start, finish

    def inward(descriptor, place, landed):
        def start():
            pl.when(outer)(descriptor.start)

        def finish():
            pl.when(outer)(descriptor.wait_send)

            @pl.when(inner)
            def _():
                descriptor.wait_recv()
                add(place, landed)

        return start, finish

    def between(descriptor, after, local=None):
        def start():
            @pl.when(inner)
            def _():
                descriptor.start()
                if local is not None:
                    local.start()

        def finish():
            @pl.when(inner)
            def _():
                descriptor.wait()
                if local is not None:
                    local.wait()
                after()

        return start, finish

    def outward(descriptor, local=None):
        def start():
            @pl.when(inner)
            def _():
                descriptor.start()
                if local is not None:
                    local.start()

        def finish():
            @pl.when(inner)
            def _():
                descriptor.wait_send()
                if local is not None:
                    local.wait()

            pl.when(outer)(descriptor.wait_recv)

        return start, finish

    def nothing():
        return None

    def open_stages(stream, cycle):
        first = (stream * cycles + cycle) * 4
        x = [opened.at[rows_of(first + i)] for i in (y, 1 - y, 2, 3, 2 + side, 3 - side)]
        out = [open_out.at[rows_of(first + i)] for i in (y, 1 - y, 2, 3, 2 + side, 3 - side)]
        mine, other, low, high, own, given = range(6)
        land = [open_land.at[stream, cycle, i] for i in range(LANDINGS)]

        def copy(slot, source, target, device):
            return remote(
                source,
                target,
                open_send.at[stream, cycle, slot],
                open_recv.at[stream, cycle, slot],
                device,
            )

        def keep(which, slot):
            return Late(
                lambda: pltpu.make_async_copy(
                    x[which], out[which], open_local.at[stream, cycle, slot]
                )
            )

        return [
            (0, inward(copy(0, x[low], land[0], along), x[low], land[0])),
            (1, inward(copy(1, x[high], land[1], along), x[high], land[1])),
            (2, between(copy(2, x[given], land[2], facing), lambda: add(x[own], land[2]))),
            (3, between(copy(3, x[own], land[3], beside), lambda: add(x[own], land[3]))),
            (4, between(copy(4, x[own], out[own], facing), nothing, keep(own, 0))),
            (5, outward(copy(5, out[low], out[low], along))),
            (6, outward(copy(6, out[high], out[high], along))),
            (1, everyone(copy(7, x[other], land[4], beside), lambda: add(x[mine], land[4]))),
            (2, inward(copy(8, x[mine], land[5], along), x[mine], land[5])),
            (3, between(copy(9, x[mine], land[6], facing), lambda: add(x[mine], land[6]))),
            (4, outward(copy(10, x[mine], out[mine], along), keep(mine, 1))),
            (5, everyone(copy(11, out[mine], out[mine], beside), nothing)),
        ]

    def paired_stages(stream, cycle, index):
        chunk = (stream * cycles + cycle) * PAIRED + index
        x = paired.at[rows_of(chunk)]
        out = paired_out.at[y, rows_of(chunk)]
        land = [paired_land.at[chunk, i] for i in range(2)]

        def copy(slot, source, target, device):
            return remote(
                source, target, paired_send.at[chunk, slot], paired_recv.at[chunk, slot], device
            )

        keep = Late(lambda: pltpu.make_async_copy(x, out, paired_local.at[chunk]))
        slot, slot_sem = ring.at[stream, index], ring_sem.at[stream, index]

        def fetch():
            begin = 0
            for source in arrived_in:
                count = source.shape[0] // CHUNK

                @pl.when((chunk >= begin) & (chunk < begin + count))
                def _(source=source, begin=begin):
                    pltpu.make_async_copy(
                        source.at[rows_of(chunk - begin)], slot, slot_sem
                    ).start()

                begin += count

        def fetched():
            pltpu.make_async_copy(arrived_in[0].at[rows_of(0)], slot, slot_sem).wait()
            add(x, slot)

        return [
            (2 + index, (fetch, fetched)),
            (3 + index, inward(copy(0, x, land[0], along), x, land[0])),
            (5 + index, between(copy(1, x, land[1], facing), lambda: add(x, land[1]))),
            (7 + index, outward(copy(2, x, out, along), keep)),
            (LAST_HOP[index], everyone(copy(3, out, out, beside), nothing)),
        ]

    offsets = range(max(LAST_HOP) + 1)

    def run(step, stream, offset, back, what):
        cycle = step - back

        @pl.when((cycle >= 0) & (cycle < cycles))
        def _():
            for when, pair in open_stages(stream, cycle):
                if when == offset:
                    pair[what]()
            for index in range(PAIRED):
                chunk = (stream * cycles + cycle) * PAIRED + index

                def each(index=index):
                    for when, pair in paired_stages(stream, cycle, index):
                        if when == offset:
                            pair[what]()

                if offset in (2 + index, 3 + index, 5 + index, 7 + index, LAST_HOP[index]):
                    pl.when(chunk < paired_chunks)(each)

    def late_copy(piece):
        rows = rows_of(piece)
        return pltpu.make_async_remote_copy(
            src_ref=late_other.at[rows],
            dst_ref=late_arrived.at[rows],
            send_sem=late_send.at[piece],
            recv_sem=late_recv.at[piece],
            device_id={"dp": beside},
            device_id_type=MESH,
        )

    late_count = late_other.shape[0] // CHUNK

    def body(step, carry):
        for phase in range(PERIOD):
            if phase == 0:

                @pl.when(step == 1)
                def _():
                    @pl.loop(0, late_count)
                    def _(piece):
                        late_copy(piece).wait()

            @pl.loop(0, 2)
            def _(stream):
                if phase in (0, 2, 4, 6):
                    piece = phase + stream

                    @pl.when((step == 0) & (piece < late_count))
                    def _():
                        late_copy(piece).start()

                for offset in offsets:
                    if (offset + 1) % PERIOD == phase:
                        run(step, stream, offset, (offset + 1) // PERIOD, 1)
                for offset in offsets:
                    if offset % PERIOD == phase:
                        run(step, stream, offset, offset // PERIOD, 0)

            if phase < 8:
                number = (step + 1) * 8 + phase
                pl.when(number < chunk_count)(partial(multiply, number))

        return carry

    lax.fori_loop(0, cycles + 2, body, 0)


def sum_chunks(factors, paired, arrived, late):
    open_rows = sum(item[0].shape[1] * item[2].shape[1] // WIDE for item in factors)
    paired_rows = sum(item.shape[0] for item in paired)
    depth = factors[0][0].shape[0]
    cycles = open_rows // (CHUNK * 8)
    chunks = paired_rows // CHUNK
    late_chunks = paired[late].shape[0] // CHUNK
    late_first = sum(item.shape[0] for item in paired[:late]) // CHUNK % (cycles * PAIRED)
    assert cycles * CHUNK * 8 == open_rows and chunks <= 2 * cycles * PAIRED
    assert late_chunks <= 8 and 3 * PAIRED <= late_first <= cycles * PAIRED - late_chunks
    return pl.pallas_call(
        partial(sum_kernel, cycles, len(paired), late),
        in_specs=[pl.BlockSpec(memory_space=pl.ANY)] * (8 + 2 * len(paired)),
        out_specs=[pl.BlockSpec(memory_space=pl.ANY)] * 3,
        out_shape=[
            jax.ShapeDtypeStruct((open_rows, WIDE), bf16),
            jax.ShapeDtypeStruct((2, paired_rows, WIDE), bf16),
            jax.ShapeDtypeStruct(paired[late].shape, bf16),
        ],
        scratch_shapes=[
            pltpu.VMEM((open_rows, WIDE), bf16),
            pltpu.VMEM((paired_rows, WIDE), bf16),
            pltpu.VMEM((2, cycles, LANDINGS, CHUNK, WIDE), bf16),
            pltpu.VMEM((chunks, 2, CHUNK, WIDE), bf16),
            pltpu.SemaphoreType.DMA((2, cycles, 12)),
            pltpu.SemaphoreType.DMA((2, cycles, 12)),
            pltpu.SemaphoreType.DMA((2, cycles, 2)),
            pltpu.SemaphoreType.DMA((chunks, 4)),
            pltpu.SemaphoreType.DMA((chunks, 4)),
            pltpu.SemaphoreType.DMA((chunks,)),
            pltpu.SemaphoreType.DMA((len(paired),)),
            pltpu.VMEM((2, PAIRED, CHUNK, WIDE), bf16),
            pltpu.SemaphoreType.DMA((2, PAIRED)),
            pltpu.VMEM((2, 4, depth, WIDE), bf16),
            pltpu.SemaphoreType.DMA((2, 4)),
            pltpu.SemaphoreType.DMA((8,)),
            pltpu.SemaphoreType.DMA((8,)),
        ],
        compiler_params=pltpu.CompilerParams(
            collective_id=0, has_side_effects=True, vmem_limit_bytes=63 * 1024 * 1024
        ),
        cost_estimate=pl.CostEstimate(
            flops=open_rows * WIDE * 4 * depth,
            bytes_accessed=(open_rows + 2 * paired_rows) * WIDE * 8,
            transcendentals=0,
        ),
    )(*factors[0], *factors[1], *paired, *arrived)


def side_grads_kernel(steps, count, y_ref, *refs):
    lefts, rights = refs[:count], refs[count : 2 * count]
    total = sum(dot_tn(left[...], right[...]) for left, right in zip(lefts, rights))
    for turn, out in enumerate(refs[-2:]):

        @pl.when(pl.program_id(0) // steps == turn)
        def _():
            for piece in range(out.shape[0]):
                out[piece] = total[:, piece * WIDE : (piece + 1) * WIDE].astype(bf16)


def side_grads(lefts, rights):
    depth, height = lefts[0].shape
    width = rights[0].shape[1]
    half, pieces = height // 2, width // WIDE
    tile = half if half <= 640 else 512
    steps = half // tile
    count = len(lefts)
    y = (lax.axis_index("dp") % 2).astype(jnp.int32).reshape(1)

    def left_at(i, y):
        owner = (i // steps) * y[0] + (1 - i // steps) * (1 - y[0])
        return (0, owner * steps + i % steps)

    shape = jax.ShapeDtypeStruct((pieces, half, WIDE), bf16)
    return pl.pallas_call(
        partial(side_grads_kernel, steps, count),
        grid_spec=pltpu.PrefetchScalarGridSpec(
            num_scalar_prefetch=1,
            grid=(2 * steps,),
            in_specs=[pl.BlockSpec((depth, tile), left_at)] * count
            + [pl.BlockSpec((depth, width), lambda i, y: (0, 0))] * count,
            out_specs=[
                pl.BlockSpec((pieces, tile, WIDE), lambda i, y: (0, jnp.minimum(i, steps - 1), 0)),
                pl.BlockSpec((pieces, tile, WIDE), lambda i, y: (0, jnp.maximum(i - steps, 0), 0)),
            ],
        ),
        out_shape=[shape, shape],
        compiler_params=pltpu.CompilerParams(vmem_limit_bytes=VMEM_LIMIT),
        cost_estimate=pl.CostEstimate(
            flops=2 * count * depth * height * width,
            bytes_accessed=2 * (count * depth * (height + width) + height * width),
            transcendentals=0,
        ),
    )(y, *lefts, *rights)


def stacked(grads):
    return grads.reshape(-1, WIDE)


def unpack_kernel(pieces, *refs):
    count = len(refs) // (pieces + 1)
    for at in range(count):
        out = refs[count * pieces + at]
        for piece in range(pieces):
            out[:, piece * WIDE : (piece + 1) * WIDE] = refs[at * pieces + piece][0].astype(f32)


def unpack(height, width, tile, *places):
    half, pieces = height // 2, width // WIDE
    steps = half // tile

    def piece_spec(first, second, piece):
        begin, step = first[1] // tile, (second[1] - first[1]) // tile
        assert first[1] % tile == 0 and second[1] % tile == 0
        return pl.BlockSpec(
            (1, tile, WIDE),
            lambda i, j: (
                first[0] + i * (second[0] - first[0]),
                begin + i * step + piece * steps + j,
                0,
            ),
        )

    count = len(places)
    return pl.pallas_call(
        partial(unpack_kernel, pieces),
        grid=(2, steps),
        in_specs=[
            piece_spec(first, second, piece)
            for _, first, second in places
            for piece in range(pieces)
        ],
        out_specs=[pl.BlockSpec((tile, width), lambda i, j: (i * steps + j, 0))] * count,
        out_shape=[jax.ShapeDtypeStruct((height, width), f32)] * count,
        compiler_params=pltpu.CompilerParams(vmem_limit_bytes=60 * 1024 * 1024),
        cost_estimate=pl.CostEstimate(
            flops=count * height * width,
            bytes_accessed=6 * count * height * width,
            transcendentals=0,
        ),
    )(*[stack for stack, _, _ in places for _ in range(pieces)])


def on_device(
    tokens,
    patches,
    text_lengths,
    prefix_lengths,
    group_map,
    ratio,
    cotangent,
    q_self,
    k_self,
    v_self,
    o_self,
    q_cross,
    k_cross,
    v_cross,
    o_cross,
    w_gate,
    w_up,
    w_down,
    gain_attn,
    gain_cross,
    gain_mlp,
):
    local_rows = tokens.shape[0]
    examples = text_lengths.shape[0]
    patch = patches.shape[0] // examples
    local_examples = local_rows // SEQ
    fast = lax.axis_size("mp") == 4 and lax.axis_size("dp") == 8 and local_examples % 2 == 0
    batches = 2 if fast else 1
    each = local_examples // batches
    rows = each * SEQ
    width = q_self.shape[1]

    lens_f = text_lengths.astype(f32)
    robot = (group_map == 0).astype(f32)
    web = 1.0 - robot
    local_counts = jnp.stack([jnp.sum(lens_f * robot), jnp.sum(lens_f * web)])
    counts = butterfly(jnp.broadcast_to(local_counts[:, None], (2, 128)), "dp")[:, 0]
    ratio_f = ratio.astype(f32)
    share = ratio_f / jnp.sum(ratio_f)
    group_scale = share * jnp.sum(counts) / jnp.maximum(counts, 1.0)
    example_scale = robot * group_scale[0] + web * group_scale[1]
    mine = lax.axis_index("mp") * local_examples
    own_scale = lax.dynamic_slice_in_dim(example_scale, mine, local_examples, 0)
    own_length = lax.dynamic_slice_in_dim(text_lengths, mine, local_examples, 0)
    place = jnp.arange(SEQ, dtype=jnp.int32)
    live = (place[None, :] < own_length[:, None]).astype(f32)
    row_weight = (own_scale[:, None] * live).reshape(local_rows)

    owners = block_owners()
    which, lengths, prefixes = [], [], []
    for b in range(batches):
        ids = (
            owners[:, None] * local_examples + b * each + jnp.arange(each, dtype=jnp.int32)[None, :]
        ).reshape(-1).astype(jnp.int32)
        which.append(ids)
        lengths.append(jnp.take(text_lengths, ids))
        prefixes.append(jnp.take(prefix_lengths, ids))

    w_qkv = jnp.concatenate([q_self, k_self, v_self], axis=1)

    each_batch = range(batches)
    last = batches - 1

    def part(tensor, b):
        return tensor[b * rows : (b + 1) * rows]

    def product(left, right, dot):
        return lambda low, high: dot(left[low:high], right)

    outer = [part(cotangent, b).astype(f32) * part(row_weight, b)[:, None] for b in each_batch]
    outer_low = [item.astype(bf16) for item in outer]
    x_zero = [part(tokens, b).astype(f32) for b in each_batch]
    norm_one = [normalize(x_zero[b], gain_attn) for b in each_batch]
    scale_one = [item[1] for item in norm_one]
    norm_one = [item[0] for item in norm_one]

    none = [None] * batches
    self_probs, cross_probs = list(none), list(none)
    full_one, qkv, mixed_self, x_one, norm_two, scale_two = ([None] * batches for _ in range(6))
    full_two, query, mixed_cross, x_two, norm_three, scale_three = (
        [None] * batches for _ in range(6)
    )
    full_three, grad_three, hidden, d_gate, d_up, back_three = ([None] * batches for _ in range(6))
    grad_two_rows, grad_two, d_query, grad_one_rows, grad_one, d_qkv = (
        [None] * batches for _ in range(6)
    )
    gain_mlp_parts, gain_cross_parts, gain_attn_parts, grad_input, output = (
        [None] * batches for _ in range(5)
    )

    def self_block(b, arrived):
        full_one[b], qkv[b] = gathered_dot(norm_one[b], arrived, w_qkv, False, 1)
        mixed_self[b], self_probs[b] = self_forward(qkv[b], lengths[b], prefixes[b])
        return scattered_dot([mixed_self[b]], [o_self], False, True, 2)

    def self_norm(b, arrived):
        x_one[b] = x_zero[b] + scatter_end(arrived)
        norm_two[b], scale_two[b] = normalize(x_one[b], gain_cross)

    def cross_block(b, arrived, keys, values):
        full_two[b], query[b] = gathered_dot(norm_two[b], arrived, q_cross, False, 3)
        mixed_cross[b], cross_probs[b] = cross_forward(query[b], keys, values, which[b], patch)
        return scattered_dot([mixed_cross[b]], [o_cross], False, True, 4)

    def cross_norm(b, arrived):
        x_two[b] = x_one[b] + scatter_end(arrived)
        norm_three[b], scale_three[b] = normalize(x_two[b], gain_mlp)

    def mlp_block(b, arrived_norm, arrived_grad):
        full_three[b], grad_three[b], hidden[b], d_gate[b], d_up[b] = gathered_mlp(
            norm_three[b], arrived_norm, outer_low[b], arrived_grad, w_gate, w_up, w_down, 5
        )

    def mlp_back(b):
        return scattered_dot([d_gate[b], d_up[b]], [w_gate, w_up], True, False, 6)

    def mlp_norm_back(b, arrived):
        back, gain_mlp_parts[b] = norm_back(
            x_two[b], scale_three[b], gain_mlp, scatter_end(arrived)
        )
        grad_two_rows[b] = outer[b] + back
        return grad_two_rows[b].astype(bf16)

    def cross_back(b, own, arrived, keys, values, earlier):
        grad_two[b], d_mixed = gathered_dot(own, arrived, o_cross, True, 7)
        d_query[b], *d_kv = cross_backward(
            query[b], keys, values, cross_probs[b], d_mixed, which[b], patch, earlier
        )
        return scattered_dot([d_query[b]], [q_cross], True, False, 8), d_kv

    def cross_norm_back(b, arrived):
        back, gain_cross_parts[b] = norm_back(
            x_one[b], scale_two[b], gain_cross, scatter_end(arrived)
        )
        grad_one_rows[b] = grad_two_rows[b] + back
        return grad_one_rows[b].astype(bf16)

    def self_back(b, own, arrived):
        grad_one[b], d_mixed = gathered_dot(own, arrived, o_self, True, 9)
        d_qkv[b] = self_backward(qkv[b], self_probs[b], d_mixed)
        return scattered_dot([d_qkv[b]], [w_qkv], True, False, 10)

    def self_norm_back(b, arrived):
        back, gain_attn_parts[b] = norm_back(
            x_zero[b], scale_one[b], gain_attn, scatter_end(arrived)
        )
        grad_input[b] = grad_one_rows[b] + back

    def project_out(b):
        return scattered_dot([hidden[b]], [w_down], False, True, 11)

    sent = list(none)
    got = list(none)
    back = list(none)
    grads = list(none)
    own = list(none)
    shown = list(none)
    if fast:
        got[0] = gather_start(norm_one[0])
        got[0], norm_one[1], w_qkv, outer_low, outer, which, lengths, prefixes = fence(
            got[0], norm_one[1], w_qkv, outer_low, outer, which, lengths, prefixes
        )
        got[1] = gather_start(norm_one[1])
        sent[0] = self_block(0, got[0])
        sent[0], got[1], outer_low = fence(sent[0], got[1], outer_low)
        grads[0] = gather_start(outer_low[0])
        sent[1] = self_block(1, got[1])
        sent, grads[0], k_cross = fence(sent, grads[0], k_cross)
        back[0] = scatter_move(sent[0])
        keys = dot_nn(patches, k_cross).astype(bf16)
        back[0], sent[1], keys, v_cross = fence(back[0], sent[1], keys, v_cross)
        back[1] = scatter_move(sent[1])
        self_norm(0, back[0])
        values = dot_nn(patches, v_cross).astype(bf16)
        norm_two[0], back[1], values = fence(norm_two[0], back[1], values)
        got[0] = gather_start(norm_two[0])
        self_norm(1, back[1])
        norm_two[1], got[0], outer_low = fence(norm_two[1], got[0], outer_low)
        got[1] = gather_start(norm_two[1])
        sent[0] = cross_block(0, got[0], keys, values)
        sent[0], got[1] = fence(sent[0], got[1])
        back[0] = scatter_move(sent[0])
        sent[1] = cross_block(1, got[1], keys, values)
        sent[1], back[0] = fence(sent[1], back[0])
        back[1] = scatter_move(sent[1])
        cross_norm(0, back[0])
        norm_three[0], back[1], outer_low = fence(norm_three[0], back[1], outer_low)
        got[0] = gather_start(norm_three[0])
        cross_norm(1, back[1])
        got[0], outer_low, norm_three[1] = fence(got[0], outer_low, norm_three[1])
        got[1] = gather_start(norm_three[1])
        mlp_block(0, got[0], grads[0])
        got[1], d_gate[0], d_up[0], outer_low[1] = fence(
            got[1], d_gate[0], d_up[0], outer_low[1]
        )
        grads[1] = gather_start(outer_low[1])
        sent[0] = mlp_back(0)
        grads[1], got[1], sent[0] = fence(grads[1], got[1], sent[0])
        back[0] = scatter_move(sent[0])
        mlp_block(1, got[1], grads[1])
        down_other, down_mine = side_grads(hidden, grad_three)
        back[0], d_gate[1], d_up[1], down_other = fence(
            back[0], d_gate[1], d_up[1], down_other
        )
        own[0] = mlp_norm_back(0, back[0])
        got[0] = gather_start(own[0])
        down_sent = flip(down_other, "dp", 1)
        sent[1] = mlp_back(1)
        own[0], got[0], sent[1], d_gate, d_up = fence(own[0], got[0], sent[1], d_gate, d_up)
        back[1] = scatter_move(sent[1])
        gate_other, gate_mine = side_grads(full_three, d_gate)
        up_other, up_mine = side_grads(full_three, d_up)
        back[1], gate_other, up_other = fence(back[1], gate_other, up_other)
        own[1] = mlp_norm_back(1, back[1])
        got[1] = gather_start(own[1])
        gate_sent = flip(gate_other, "dp", 1)
        sent[0], d_kv = cross_back(0, own[0], got[0], keys, values, ())
        own[1], got[1], sent[0], d_kv, down_sent, up_other = fence(
            own[1], got[1], sent[0], d_kv, down_sent, up_other
        )
        back[0] = scatter_move(sent[0])
        up_sent = flip(up_other, "dp", 1)
        sent[1], d_kv = cross_back(1, own[1], got[1], keys, values, d_kv)
        sent[1], back[0], d_kv, mixed_cross, hidden = fence(
            sent[1], back[0], d_kv, mixed_cross, hidden
        )
        back[1] = scatter_move(sent[1])
        own[0] = cross_norm_back(0, back[0])
        o_other, o_mine = side_grads(mixed_cross, grad_two)
        q_other, q_mine = side_grads(full_two, d_query)
        shown[0] = project_out(0)
        own[0], back[1], d_kv, o_other, q_other, shown[0], gate_sent, down_mine = fence(
            own[0], back[1], d_kv, o_other, q_other, shown[0], gate_sent, down_mine
        )
        got[0] = gather_start(own[0])
        own[1] = cross_norm_back(1, back[1])
        k_other, k_mine = side_grads([patches], [d_kv[0]])
        v_other, v_mine = side_grads([patches], [d_kv[1]])
        got[0], own[1], k_other, v_other, hidden, gate_mine = fence(
            got[0], own[1], k_other, v_other, hidden, gate_mine
        )
        got[1] = gather_start(own[1])
        o_sent = flip(o_other, "dp", 1)
        sent[0] = self_back(0, own[0], got[0])
        got[1], sent[0], up_sent, o_sent, q_other = fence(
            got[1], sent[0], up_sent, o_sent, q_other
        )
        q_sent = flip(q_other, "dp", 1)
        back[0] = scatter_move(sent[0])
        sent[1] = self_back(1, own[1], got[1])
        back[0], sent[1], mixed_self, hidden, q_sent, k_other = fence(
            back[0], sent[1], mixed_self, hidden, q_sent, k_other
        )
        k_sent = flip(k_other, "dp", 1)
        back[1] = scatter_move(sent[1])
        self_norm_back(0, back[0])
        shown[1] = project_out(1)
        back[1], grad_input[0], shown, k_sent = fence(back[1], grad_input[0], shown, k_sent)
        self_norm_back(1, back[1])
        back = [scatter_move(shown[b]) for b in each_batch]
        factors = [[*full_one, *d_qkv], [*mixed_self, *grad_one]]
        paired = [down_mine, gate_mine, up_mine, q_mine, k_mine, v_mine, o_mine]
        arrived = [down_sent, gate_sent, up_sent, q_sent, k_sent, v_other, o_sent]
        open_sum, paired_sum, _ = sum_chunks(
            factors, *([stacked(item) for item in items] for items in (paired, arrived)), 5
        )
    else:
        sent[0] = self_block(0, gather_start(norm_one[0]))
        self_norm(0, scatter_move(sent[0]))
        keys = dot_nn(patches, k_cross).astype(bf16)
        values = dot_nn(patches, v_cross).astype(bf16)
        sent[0] = cross_block(0, gather_start(norm_two[0]), keys, values)
        cross_norm(0, scatter_move(sent[0]))
        mlp_block(0, gather_start(norm_three[0]), gather_start(outer_low[0]))
        own[0] = mlp_norm_back(0, scatter_move(mlp_back(0)))
        sent[0], d_kv = cross_back(0, own[0], gather_start(own[0]), keys, values, ())
        own[0] = cross_norm_back(0, scatter_move(sent[0]))
        sent[0] = self_back(0, own[0], gather_start(own[0]))
        self_norm_back(0, scatter_move(sent[0]))
        sums = lax.psum(
            [
                item.astype(bf16)
                for item in (
                    dot_tn(full_one[0], d_qkv[0]),
                    dot_tn(mixed_self[0], grad_one[0]),
                    dot_tn(full_two[0], d_query[0]),
                    dot_tn(patches, d_kv[0]),
                    dot_tn(patches, d_kv[1]),
                    dot_tn(mixed_cross[0], grad_two[0]),
                    dot_tn(full_three[0], d_gate[0]),
                    dot_tn(full_three[0], d_up[0]),
                    dot_tn(hidden[0], grad_three[0]),
                )
            ],
            "dp",
        )
        back = [scatter_move(project_out(0))]
    gains = jnp.stack(
        [sum(parts) for parts in (gain_attn_parts, gain_cross_parts, gain_mlp_parts)]
    )
    if fast:
        open_sum, paired_sum, back, gains = fence(open_sum, paired_sum, back, gains)

        whole = open_sum[None]
        half = q_self.shape[0] // 2
        pieces = width // WIDE
        places, start = [], 0
        for weight in (w_down, w_gate, w_up, q_cross, k_cross, v_cross, o_cross):
            places.append((paired_sum, (0, start), (1, start)))
            start += weight.size // WIDE // 2
        self_places = [
            (whole, (0, at * pieces * half), (0, (3 + at) * pieces * half)) for at in range(3)
        ]
        start = w_qkv.size // WIDE
        o_place = (whole, (0, start), (0, start + o_self.size // WIDE // 2))
        groups = [
            unpack(*w_down.shape, w_down.shape[0] // 4, places[0]),
            unpack(*w_gate.shape, 256, *places[1:3]),
            unpack(*q_self.shape, 256, *places[3:6], *self_places),
            unpack(*o_self.shape, o_self.shape[0] // 4, places[6], o_place),
        ]
        gains = gains + flip(gains, "mp", 1)
        for at, (axis, bit) in enumerate((("mp", 2), ("dp", 1), ("dp", 2), ("dp", 4))):
            arrived, groups[at] = fence(flip(gains, axis, bit), groups[at])
            gains = gains + arrived
        (d_wdown,), (d_wgate, d_wup), shared, (d_ocross, d_oself) = groups
        d_qcross, d_kcross, d_vcross, *d_self = shared
    else:
        (
            d_wqkv,
            d_oself,
            d_qcross,
            d_kcross,
            d_vcross,
            d_ocross,
            d_wgate,
            d_wup,
            d_wdown,
        ) = [item.astype(f32) for item in sums]
        d_self = [d_wqkv[:, at * width : (at + 1) * width] for at in range(3)]
    output = jnp.concatenate(
        [(x_two[b] + scatter_end(back[b])).astype(bf16) for b in each_batch], axis=0
    )
    grad_input = jnp.concatenate(grad_input, axis=0)
    if not fast:
        gains = butterfly(butterfly(gains, "mp"), "dp")
    return (
        output,
        grad_input,
        *d_self,
        d_oself,
        d_qcross,
        d_kcross,
        d_vcross,
        d_ocross,
        d_wgate,
        d_wup,
        d_wdown,
        gains[0],
        gains[1],
        gains[2],
    )


def solution(mesh):
    by_rows = P(("dp", "mp"), None)
    columns = P(None, "mp")
    rows = P("mp", None)
    weights = (columns, columns, columns, rows, columns, columns, columns, rows, columns, columns, rows)
    in_specs = (
        (by_rows, P("dp", None), P("dp"), P("dp"), P("dp"), P(), by_rows) + weights + (P(), P(), P())
    )
    out_specs = (by_rows, by_rows) + weights + (P(), P(), P())
    return jax.shard_map(
        on_device, mesh=mesh, in_specs=in_specs, out_specs=out_specs, check_vma=False
    )
```

```python
from functools import partial

import jax
import jax.numpy as jnp
from jax import lax
from jax.experimental import pallas as pl
from jax.experimental.pallas import tpu as pltpu
from jax.sharding import PartitionSpec as P

HEAD = 64
SEQ = 128
PAIR = 2 * HEAD
epsilon = 1e-06
f32 = jnp.float32
bf16 = jnp.bfloat16
VMEM_LIMIT = 56 * 1024 * 1024
MESH = pl.DeviceIdType.MESH


def dot_nn(left, right):
    return jnp.dot(left, right, preferred_element_type=f32)


def dot_tn(left, right):
    return lax.dot_general(left, right, (((0,), (0,)), ((), ())), preferred_element_type=f32)


def dot_nt(left, right):
    return lax.dot_general(left, right, (((1,), (1,)), ((), ())), preferred_element_type=f32)


def normalize(values_in, gain):
    row_scale = lax.rsqrt(jnp.mean(values_in * values_in, axis=-1, keepdims=True) + epsilon)
    return ((values_in * row_scale * gain).astype(bf16), row_scale)


def norm_back(values_in, row_scale, gain, incoming):
    weighted = incoming * gain
    inner = jnp.mean(weighted * values_in, axis=-1, keepdims=True)
    return (
        row_scale * weighted - values_in * row_scale**3 * inner,
        jnp.sum(incoming * values_in * row_scale, axis=0),
    )


def first_head():
    return lax.broadcasted_iota(jnp.int32, (SEQ, PAIR), 1) < HEAD


def stack_pair(rows, first):
    zero = jnp.zeros_like(rows)
    return jnp.concatenate([jnp.where(first, rows, zero), jnp.where(first, zero, rows)], axis=0)


def unstack_pair(stacked, first):
    return jnp.where(first, stacked[:SEQ], stacked[SEQ:])


def self_mask(length, prefix):
    query_at = lax.broadcasted_iota(jnp.int32, (2 * SEQ, SEQ), 0) % SEQ
    key_at = lax.broadcasted_iota(jnp.int32, (2 * SEQ, SEQ), 1)
    return (key_at < length) & ((key_at <= query_at) | (key_at < prefix))


def pair_probs(stacked_query, keys, mask):
    scores = dot_nt(stacked_query, keys)
    if mask is not None:
        scores = jnp.where(mask, scores, -1e30)
    expd = jnp.exp(scores - jnp.max(scores, axis=-1, keepdims=True))
    return expd * (1.0 / jnp.sum(expd, axis=-1, keepdims=True))


def pair_forward(query, keys, values, mask, first):
    scaled = stack_pair(query * jnp.asarray(HEAD**-0.5, bf16), first)
    probs = pair_probs(scaled, keys, mask).astype(bf16)
    return unstack_pair(dot_nn(probs, values), first).astype(bf16), probs


def pair_backward(grad, query, keys, values, probs, first):
    scaled = stack_pair(query * jnp.asarray(HEAD**-0.5, bf16), first)
    grads = stack_pair(grad, first)
    d_probs = dot_nt(grads, values)
    wide = probs.astype(f32)
    weighted = wide * d_probs
    d_scores = (weighted - wide * jnp.sum(weighted, axis=-1, keepdims=True)).astype(bf16)
    d_query = unstack_pair(dot_nn(d_scores, keys), first) * HEAD**-0.5
    d_keys = dot_tn(d_scores, scaled)
    d_values = dot_tn(probs, grads)
    return d_query.astype(bf16), d_keys.astype(bf16), d_values.astype(bf16)


def lanes(part, width, pair):
    return slice(part * width + pair * PAIR, part * width + (pair + 1) * PAIR)


def self_forward_kernel(length_ref, prefix_ref, qkv_ref, out_ref, probs_ref):
    at = pl.program_id(0)
    width = out_ref.shape[1]
    first = first_head()
    mask = self_mask(length_ref[at], prefix_ref[at])
    for pair in range(width // PAIR):
        out_ref[:, lanes(0, width, pair)], probs_ref[0, pair] = pair_forward(
            qkv_ref[:, lanes(0, width, pair)],
            qkv_ref[:, lanes(1, width, pair)],
            qkv_ref[:, lanes(2, width, pair)],
            mask,
            first,
        )


def self_backward_kernel(qkv_ref, probs_ref, grad_ref, out_ref):
    width = grad_ref.shape[1]
    first = first_head()
    for pair in range(width // PAIR):
        for part, value in enumerate(
            pair_backward(
                grad_ref[:, lanes(0, width, pair)],
                qkv_ref[:, lanes(0, width, pair)],
                qkv_ref[:, lanes(1, width, pair)],
                qkv_ref[:, lanes(2, width, pair)],
                probs_ref[0, pair],
                first,
            )
        ):
            out_ref[:, lanes(part, width, pair)] = value


def cross_forward_kernel(which_ref, query_ref, key_ref, value_ref, out_ref, probs_ref):
    width = out_ref.shape[1]
    first = first_head()
    for pair in range(width // PAIR):
        at = lanes(0, width, pair)
        out_ref[:, at], probs_ref[0, pair] = pair_forward(
            query_ref[:, at], key_ref[:, at], value_ref[:, at], None, first
        )


def cross_backward_kernel(which_ref, query_ref, key_ref, value_ref, probs_ref, grad_ref, *rest):
    d_query_ref, d_key_ref, d_value_ref = rest[-3:]
    width = query_ref.shape[1]
    first = first_head()
    for pair in range(width // PAIR):
        at = lanes(0, width, pair)
        d_query_ref[:, at], d_key_ref[:, at], d_value_ref[:, at] = pair_backward(
            grad_ref[:, at],
            query_ref[:, at],
            key_ref[:, at],
            value_ref[:, at],
            probs_ref[0, pair],
            first,
        )


def params():
    return pltpu.CompilerParams(vmem_limit_bytes=ROOM)


def by_row(width):
    return pl.BlockSpec((SEQ, width), lambda i, *_: (i, 0))


def attention_cost(examples, width, keys, dots, moved):
    return pl.CostEstimate(
        flops=dots * 2 * examples * SEQ * keys * width * 2,
        bytes_accessed=moved,
        transcendentals=examples * SEQ * keys * width // HEAD,
    )


def probs_spec(width, keys):
    return pl.BlockSpec((1, width // PAIR, 2 * SEQ, keys), lambda i, *_: (i, 0, 0, 0))


def probs_shape(rows, width, keys):
    return pltpu.HBM((rows // SEQ, width // PAIR, 2 * SEQ, keys), bf16)


def self_forward(qkv, length, prefix):
    rows, triple = qkv.shape
    width = triple // 3
    return pl.pallas_call(
        self_forward_kernel,
        grid_spec=pltpu.PrefetchScalarGridSpec(
            num_scalar_prefetch=2,
            grid=(rows // SEQ,),
            in_specs=[by_row(triple)],
            out_specs=[by_row(width), probs_spec(width, SEQ)],
        ),
        out_shape=[
            jax.ShapeDtypeStruct((rows, width), bf16),
            probs_shape(rows, width, SEQ),
        ],
        compiler_params=params(),
        cost_estimate=attention_cost(rows // SEQ, width, SEQ, 2, rows * width * 12),
    )(length, prefix, qkv)


def self_backward(qkv, probs, grad):
    rows, triple = qkv.shape
    width = triple // 3
    return pl.pallas_call(
        self_backward_kernel,
        grid=(rows // SEQ,),
        in_specs=[by_row(triple), probs_spec(width, SEQ), by_row(width)],
        out_specs=by_row(triple),
        out_shape=jax.ShapeDtypeStruct((rows, triple), bf16),
        compiler_params=params(),
        cost_estimate=attention_cost(rows // SEQ, width, SEQ, 4, rows * width * 18),
    )(qkv, probs, grad)


def cross_forward(query, keys, values, which, patch):
    rows, width = query.shape
    by_patch = pl.BlockSpec((patch, width), lambda i, which: (which[i], 0))
    return pl.pallas_call(
        cross_forward_kernel,
        grid_spec=pltpu.PrefetchScalarGridSpec(
            num_scalar_prefetch=1,
            grid=(rows // SEQ,),
            in_specs=[by_row(width), by_patch, by_patch],
            out_specs=[by_row(width), probs_spec(width, patch)],
        ),
        out_shape=[
            jax.ShapeDtypeStruct((rows, width), bf16),
            probs_shape(rows, width, patch),
        ],
        compiler_params=params(),
        cost_estimate=attention_cost(rows // SEQ, width, patch, 2, rows * width * 20),
    )(which, query, keys, values)


def cross_backward(query, keys, values, probs, grad, which, patch, earlier):
    rows, width = query.shape
    by_patch = pl.BlockSpec((patch, width), lambda i, which: (which[i], 0))
    in_specs = [by_row(width), by_patch, by_patch, probs_spec(width, patch), by_row(width)]
    operands = [which, query, keys, values, probs, grad]
    aliases = {}
    for at, item in enumerate(earlier):
        in_specs.append(pl.BlockSpec(memory_space=pl.ANY))
        aliases[len(operands)] = 1 + at
        operands.append(item)
    whole = pltpu.HBM(keys.shape, bf16)
    return pl.pallas_call(
        cross_backward_kernel,
        grid_spec=pltpu.PrefetchScalarGridSpec(
            num_scalar_prefetch=1,
            grid=(rows // SEQ,),
            in_specs=in_specs,
            out_specs=[by_row(width), by_patch, by_patch],
        ),
        out_shape=[jax.ShapeDtypeStruct((rows, width), bf16), whole, whole],
        input_output_aliases=aliases,
        compiler_params=params(),
        cost_estimate=attention_cost(rows // SEQ, width, patch, 4, rows * width * 32),
    )(*operands)


def other_core():
    me = lax.axis_index("mp")
    return me + 1 - 2 * lax.rem(me, 2)


def meet(partner):
    barrier = pltpu.get_barrier_semaphore()
    pl.semaphore_signal(barrier, inc=1, device_id={"mp": partner}, device_id_type=MESH)
    pl.semaphore_wait(barrier, 1)


def to_partner(source, target, send_sem, recv_sem, partner):
    return pltpu.make_async_remote_copy(
        src_ref=source,
        dst_ref=target,
        send_sem=send_sem,
        recv_sem=recv_sem,
        device_id={"mp": partner},
        device_id_type=MESH,
    )


def columns_of(weight, tile, size, transposed):
    at = pl.ds(pl.multiple_of(tile * size, size), size)
    return weight[at, :] if transposed else weight[:, at]


def gathered_kernel(transposed, size, own, beside, across, weight, full, out, corner, sems, local):
    dot = dot_nt if transposed else dot_nn
    rows = own.shape[0]
    blocks = (own, beside, across, corner)
    partner = other_core()
    given = to_partner(across, corner, sems.at[0], sems.at[1], partner)
    keep = [
        pltpu.make_async_copy(block, full.at[pl.ds(at * rows, rows)], local.at[at])
        for at, block in enumerate(blocks)
    ]
    meet(partner)
    given.start()
    for at in range(3):
        keep[at].start()

    def multiply(places):
        @pl.loop(0, out.shape[1] // size)
        def _(tile):
            right = columns_of(weight, tile, size, transposed)
            to = pl.ds(pl.multiple_of(tile * size, size), size)
            for at in places:
                out[at * rows : (at + 1) * rows, to] = dot(blocks[at][...], right).astype(bf16)

    multiply((0, 1, 2))
    given.wait()
    keep[3].start()
    multiply((3,))
    for at in range(4):
        keep[at].wait()


IN_VMEM = pl.BlockSpec(memory_space=pltpu.VMEM)
ROOM = 24 * 1024 * 1024


def gathered_dot(own, arrived, weight, transposed, ident):
    if lax.axis_size("mp") != 4:
        dot = dot_nt if transposed else dot_nn
        return arrived, dot(arrived, weight).astype(bf16)
    across, beside = arrived
    rows, model = own.shape
    units = weight.shape[0 if transposed else 1]
    return pl.pallas_call(
        partial(gathered_kernel, transposed, 512),
        in_specs=[IN_VMEM] * 4,
        out_specs=[pl.BlockSpec(memory_space=pltpu.HBM), IN_VMEM],
        out_shape=[
            pltpu.HBM((4 * rows, model), bf16),
            jax.ShapeDtypeStruct((4 * rows, units), bf16),
        ],
        scratch_shapes=[
            pltpu.VMEM((rows, model), bf16),
            pltpu.SemaphoreType.DMA((2,)),
            pltpu.SemaphoreType.DMA((4,)),
        ],
        compiler_params=pltpu.CompilerParams(
            collective_id=ident, has_side_effects=True, vmem_limit_bytes=ROOM
        ),
        cost_estimate=pl.CostEstimate(
            flops=8 * rows * model * units,
            bytes_accessed=14 * rows * model + 4 * model * units + 8 * rows * units,
            transcendentals=0,
        ),
    )(own, beside, across, weight)


def scattered_kernel(transposed, count, size, *refs):
    dot = dot_nt if transposed else dot_nn
    lefts, weights = refs[:count], refs[count : 2 * count]
    kept, passed, ready, landed, send_sem, recv_sem = refs[2 * count :]
    rows, model = kept.shape
    tiles = model // size
    partner = other_core()

    def given(tile):
        return to_partner(
            ready.at[tile], landed.at[tile], send_sem.at[tile], recv_sem.at[tile], partner
        )

    def block(at, tile):
        return sum(
            dot(
                left[at * rows : (at + 1) * rows, :],
                columns_of(weight, tile, size, transposed),
            )
            for left, weight in zip(lefts, weights)
        )

    meet(partner)

    @pl.loop(0, tiles)
    def _(tile):
        ready[tile, :rows, :] = block(1, tile).astype(bf16)
        ready[tile, rows:, :] = block(3, tile).astype(bf16)
        given(tile).start()

    @pl.loop(0, tiles)
    def _(tile):
        mine = block(0, tile)
        across = block(2, tile)
        given(tile).wait()
        to = pl.ds(pl.multiple_of(tile * size, size), size)
        kept[:, to] = mine + landed[tile, :rows, :].astype(f32)
        passed[:, to] = (across + landed[tile, rows:, :].astype(f32)).astype(bf16)


def scattered_dot(lefts, weights, transposed, wide, ident):
    if lax.axis_size("mp") != 4:
        dot = dot_nt if transposed else dot_nn
        term = sum(dot(left, weight) for left, weight in zip(lefts, weights))
        return (term if wide else term.astype(bf16),)
    rows = lefts[0].shape[0] // 4
    model = weights[0].shape[0 if transposed else 1]
    size = 512
    tiles = model // size
    depth = sum(item.shape[1] for item in lefts)
    return pl.pallas_call(
        partial(scattered_kernel, transposed, len(lefts), size),
        in_specs=[IN_VMEM] * (2 * len(lefts)),
        out_specs=[IN_VMEM, IN_VMEM],
        out_shape=[
            jax.ShapeDtypeStruct((rows, model), f32),
            jax.ShapeDtypeStruct((rows, model), bf16),
        ],
        scratch_shapes=[
            pltpu.VMEM((tiles, 2 * rows, size), bf16),
            pltpu.VMEM((tiles, 2 * rows, size), bf16),
            pltpu.SemaphoreType.DMA((tiles,)),
            pltpu.SemaphoreType.DMA((tiles,)),
        ],
        compiler_params=pltpu.CompilerParams(
            collective_id=ident,
            has_side_effects=True,
            vmem_limit_bytes=ROOM if depth < 2048 else 2 * ROOM,
        ),
        cost_estimate=pl.CostEstimate(
            flops=8 * rows * model * depth,
            bytes_accessed=8 * rows * depth + 4 * model * depth + 14 * rows * model,
            transcendentals=0,
        ),
    )(*lefts, *weights)


def mlp_rows(norm, grad, gate_ref, up_ref, down_ref):
    curve = 0.7978845608028654
    gate = dot_nn(norm, gate_ref[...])
    up = dot_nn(norm, up_ref[...])
    d_hidden = dot_nt(grad, down_ref[...])
    square = gate * gate
    bend = jnp.tanh(curve * gate * (1.0 + 0.044715 * square))
    half = 0.5 * (1.0 + bend)
    value = gate * half
    slope = half + 0.5 * curve * gate * (1.0 - bend * bend) * (1.0 + 0.134145 * square)
    return (
        (value * up).astype(bf16),
        (d_hidden * up * slope).astype(bf16),
        (d_hidden * value).astype(bf16),
    )


def mlp_kernel(norm_ref, grad_ref, gate_ref, up_ref, down_ref, hidden_ref, d_gate_ref, d_up_ref):
    rows = norm_ref.shape[0]
    step = min(rows, 256)
    for start in range(0, rows, step):
        at = slice(start, start + step)
        hidden_ref[at, :], d_gate_ref[at, :], d_up_ref[at, :] = mlp_rows(
            norm_ref[at, :], grad_ref[at, :], gate_ref, up_ref, down_ref
        )


def gathered_tiles_kernel(tiles, extra, body, *refs):
    blocks, ins, full, outs = refs[:3], refs[3 : 3 + extra], refs[3 + extra], refs[4 + extra : -3]
    corner, sems, local = refs[-3:]
    tile = pl.program_id(0)
    rows = blocks[0].shape[0]
    partner = other_core()
    blocks = (*blocks, corner)

    def given():
        return to_partner(blocks[2], corner, sems.at[0], sems.at[1], partner)

    def keep(at):
        return pltpu.make_async_copy(blocks[at], full.at[pl.ds(at * rows, rows)], local.at[at])

    @pl.when(tile == 0)
    def _():
        meet(partner)
        given().start()
        for at in range(3):
            keep(at).start()

    for at in range(4):
        if at == 3:

            @pl.when(tile == 0)
            def _():
                given().wait()
                keep(3).start()

        body(slice(at * rows, (at + 1) * rows), blocks[at][...], ins, outs)

    @pl.when(tile == tiles - 1)
    def _():
        for at in range(4):
            keep(at).wait()


def up_body(place, norm, ins, outs):
    gate = dot_nn(norm, ins[0][...])
    up = dot_nn(norm, ins[1][...])
    curve = 0.7978845608028654
    square = gate * gate
    bend = jnp.tanh(curve * gate * (1.0 + 0.044715 * square))
    half = 0.5 * (1.0 + bend)
    value = gate * half
    slope = half + 0.5 * curve * gate * (1.0 - bend * bend) * (1.0 + 0.134145 * square)
    outs[0][place, :] = (value * up).astype(bf16)
    outs[1][place, :] = (up * slope).astype(bf16)
    outs[2][place, :] = value.astype(bf16)


def down_body(place, grad, ins, outs):
    d_hidden = dot_nt(grad, ins[0][...])
    outs[0][place, :] = (d_hidden * ins[1][place, :].astype(f32)).astype(bf16)
    outs[1][place, :] = (d_hidden * ins[2][place, :].astype(f32)).astype(bf16)


def gathered_tiles(own, arrived, weights, tiled, body, out_count, ident):
    across, beside = arrived
    rows, model = own.shape
    units = weights[0].shape[1 if body is up_body else 0]
    tile = 256
    whole = pl.BlockSpec((rows, model), lambda i: (0, 0))
    by_tile = pl.BlockSpec((4 * rows, tile), lambda i: (0, i))
    weight_specs = [
        pl.BlockSpec((model, tile), lambda i: (0, i))
        if body is up_body
        else pl.BlockSpec((tile, model), lambda i: (i, 0))
        for _ in weights
    ]
    return pl.pallas_call(
        partial(gathered_tiles_kernel, units // tile, len(weights) + len(tiled), body),
        grid=(units // tile,),
        in_specs=[whole] * 3 + weight_specs + [by_tile] * len(tiled),
        out_specs=[pl.BlockSpec(memory_space=pltpu.HBM)] + [by_tile] * out_count,
        out_shape=[pltpu.HBM((4 * rows, model), bf16)]
        + [jax.ShapeDtypeStruct((4 * rows, units), bf16)] * out_count,
        scratch_shapes=[
            pltpu.VMEM((rows, model), bf16),
            pltpu.SemaphoreType.DMA((2,)),
            pltpu.SemaphoreType.DMA((4,)),
        ],
        compiler_params=pltpu.CompilerParams(
            collective_id=ident, has_side_effects=True, vmem_limit_bytes=VMEM_LIMIT
        ),
        cost_estimate=pl.CostEstimate(
            flops=8 * rows * model * units * len(weights),
            bytes_accessed=14 * rows * model + 2 * len(weights) * model * units + 24 * rows * units,
            transcendentals=4 * rows * units,
        ),
    )(own, beside, across, *weights, *tiled)


def mlp(norm, grad, w_gate, w_up, w_down):
    rows, model = norm.shape
    units = w_gate.shape[1]
    tile = 256 if units % 256 == 0 else units
    whole = pl.BlockSpec((rows, model), lambda i: (0, 0))
    columns = pl.BlockSpec((model, tile), lambda i: (0, i))
    out = pl.BlockSpec((rows, tile), lambda i: (0, i))
    shape = jax.ShapeDtypeStruct((rows, units), bf16)
    return pl.pallas_call(
        mlp_kernel,
        grid=(units // tile,),
        in_specs=[whole, whole, columns, columns, pl.BlockSpec((tile, model), lambda i: (i, 0))],
        out_specs=[out, out, out],
        out_shape=[shape, shape, shape],
        compiler_params=params(),
        cost_estimate=pl.CostEstimate(
            flops=6 * rows * model * units,
            bytes_accessed=4 * rows * model + 6 * model * units + 6 * rows * units,
            transcendentals=rows * units,
        ),
    )(norm, grad, w_gate, w_up, w_down)


def flip(tensor, axis, bit):
    count = lax.axis_size(axis)
    return lax.ppermute(tensor, axis, [(i, i ^ bit) for i in range(count)])


def butterfly(tensor, axis):
    count = lax.axis_size(axis)
    if count & (count - 1):
        return lax.psum(tensor, axis)
    bit = 1
    while bit < count:
        tensor = tensor + flip(tensor, axis, bit)
        bit *= 2
    return tensor


def block_owners():
    blocks = jnp.arange(lax.axis_size("mp"), dtype=jnp.int32)
    return lax.axis_index("mp") ^ blocks if lax.axis_size("mp") == 4 else blocks


def fence(*values):
    return lax.optimization_barrier(values)


def gather_start(rows_local):
    if lax.axis_size("mp") != 4:
        return lax.all_gather(rows_local, "mp", axis=0, tiled=True)
    return flip(rows_local, "mp", 2), flip(rows_local, "mp", 1)


def scatter_move(sent):
    if lax.axis_size("mp") != 4:
        return None, lax.psum_scatter(sent[0], "mp", scatter_dimension=0, tiled=True)
    return sent[0], flip(sent[1], "mp", 2)


def scatter_end(arrived):
    if lax.axis_size("mp") != 4:
        return arrived[1].astype(f32)
    return arrived[0] + arrived[1].astype(f32)


CHUNK = 256
WIDE = 256
LANDINGS = 7
PERIOD = 9
PAIRED = 6
LAST_HOP = (8, 9, 11, 13, 15, 16)


class Late:
    def __init__(self, make):
        self.make = make

    def start(self):
        self.make().start()

    def wait(self):
        self.make().wait()

    def wait_send(self):
        self.make().wait_send()

    def wait_recv(self):
        self.make().wait_recv()


def sum_kernel(cycles, paired_count, late, *refs):
    inputs, refs = refs[: 8 + 2 * paired_count], refs[8 + 2 * paired_count :]
    factors = (inputs[0:4], inputs[4:8])
    paired_in = inputs[8 : 8 + paired_count]
    arrived_in = list(inputs[8 + paired_count :])
    late_other = arrived_in[late]
    open_out, paired_out, late_arrived = refs[:3]
    arrived_in[late] = late_arrived
    (
        opened,
        paired,
        open_land,
        paired_land,
        open_send,
        open_recv,
        open_local,
        paired_send,
        paired_recv,
        paired_local,
        fill_sem,
        ring,
        ring_sem,
        factor,
        factor_sem,
        late_send,
        late_recv,
    ) = refs[3:]
    at = lax.axis_index("dp")
    y = lax.rem(at, 2)
    z = lax.div(at, 2)
    inner = (z == 1) | (z == 2)
    outer = (z == 0) | (z == 3)
    beside = z * 2 + (1 - y)
    along = at + jnp.where(lax.rem(z, 2) == 0, 2, -2)
    facing = (3 - z) * 2 + y
    side = z - 1
    paired_chunks = paired.shape[0] // CHUNK

    def rows_of(index):
        return pl.ds(pl.multiple_of(index * CHUNK, CHUNK), CHUNK)

    barrier = pltpu.get_barrier_semaphore()

    def greet(target):
        pl.semaphore_signal(barrier, inc=1, device_id={"dp": target}, device_id_type=MESH)

    greet(beside)
    greet(along)

    fills = []
    start = 0
    for source in paired_in:
        place = paired.at[pl.ds(start, source.shape[0])]
        fills.append(pltpu.make_async_copy(source, place, fill_sem.at[len(fills)]))
        start += source.shape[0]
    for fill in fills:
        fill.start()

    first_height, first_width = factors[0][0].shape[1], factors[0][2].shape[1]
    first_pieces = first_width // WIDE
    first_groups = first_height * first_width // (CHUNK * WIDE * 4)
    second_pieces = factors[1][2].shape[1] // WIDE
    chunk_count = cycles * 8

    def place_of(number):
        group = (number // 4 % 2) * cycles + number // 8
        return group, number % 4

    def factor_copies(which, left_at, right_at, slot):
        copies = []
        for at in range(4):
            column = left_at if at < 2 else right_at
            columns = pl.ds(pl.multiple_of(column * WIDE, WIDE), WIDE)
            copies.append(
                pltpu.make_async_copy(
                    factors[which][at].at[:, columns], factor.at[slot, at], factor_sem.at[slot, at]
                )
            )
        return copies

    def load(number):
        group, member = place_of(number)
        slot = lax.rem(number, 2)

        @pl.when((number < chunk_count) & (group < first_groups))
        def _():
            left = (group // first_pieces) * (first_height // 2 // WIDE) + member
            for copy in factor_copies(0, left, group % first_pieces, slot):
                copy.start()

        @pl.when((number < chunk_count) & (group >= first_groups))
        def _():
            chunk = (group - first_groups) * 4 + member
            for copy in factor_copies(1, chunk // second_pieces, chunk % second_pieces, slot):
                copy.start()

    def multiply(number):
        group, member = place_of(number)
        slot = lax.rem(number, 2)
        load(number + 1)
        for copy in factor_copies(0, 0, 0, slot):
            copy.wait()
        product = dot_tn(factor[slot, 0], factor[slot, 2]) + dot_tn(
            factor[slot, 1], factor[slot, 3]
        )
        opened[rows_of(group * 4 + member), :] = product.astype(bf16)

    load(0)

    @pl.loop(0, 8)
    def _(number):
        multiply(number)

    @pl.when(inner)
    def _():
        greet(facing)
        pl.semaphore_wait(barrier, 3)

    @pl.when(outer)
    def _():
        pl.semaphore_wait(barrier, 2)

    for fill in fills:
        fill.wait()

    def remote(source, target, send_sem, recv_sem, device):
        return Late(
            lambda: pltpu.make_async_remote_copy(
                src_ref=source,
                dst_ref=target,
                send_sem=send_sem,
                recv_sem=recv_sem,
                device_id={"dp": device},
                device_id_type=MESH,
            )
        )

    def add(place, landing):
        @pl.loop(0, CHUNK // 32)
        def _(step):
            rows = pl.ds(pl.multiple_of(step * 32, 32), 32)
            place[rows, :] = (
                place[rows, :].astype(f32) + landing[rows, :].astype(f32)
            ).astype(bf16)

    def everyone(descriptor, after):
        def finish():
            descriptor.wait()
            after()

        return descriptor.start, finish

    def inward(descriptor, place, landed):
        def start():
            pl.when(outer)(descriptor.start)

        def finish():
            pl.when(outer)(descriptor.wait_send)

            @pl.when(inner)
            def _():
                descriptor.wait_recv()
                add(place, landed)

        return start, finish

    def between(descriptor, after, local=None):
        def start():
            @pl.when(inner)
            def _():
                descriptor.start()
                if local is not None:
                    local.start()

        def finish():
            @pl.when(inner)
            def _():
                descriptor.wait()
                if local is not None:
                    local.wait()
                after()

        return start, finish

    def outward(descriptor, local=None):
        def start():
            @pl.when(inner)
            def _():
                descriptor.start()
                if local is not None:
                    local.start()

        def finish():
            @pl.when(inner)
            def _():
                descriptor.wait_send()
                if local is not None:
                    local.wait()

            pl.when(outer)(descriptor.wait_recv)

        return start, finish

    def nothing():
        return None

    def open_stages(stream, cycle):
        first = (stream * cycles + cycle) * 4
        x = [opened.at[rows_of(first + i)] for i in (y, 1 - y, 2, 3, 2 + side, 3 - side)]
        out = [open_out.at[rows_of(first + i)] for i in (y, 1 - y, 2, 3, 2 + side, 3 - side)]
        mine, other, low, high, own, given = range(6)
        land = [open_land.at[stream, cycle, i] for i in range(LANDINGS)]

        def copy(slot, source, target, device):
            return remote(
                source,
                target,
                open_send.at[stream, cycle, slot],
                open_recv.at[stream, cycle, slot],
                device,
            )

        def keep(which, slot):
            return Late(
                lambda: pltpu.make_async_copy(
                    x[which], out[which], open_local.at[stream, cycle, slot]
                )
            )

        return [
            (0, inward(copy(0, x[low], land[0], along), x[low], land[0])),
            (1, inward(copy(1, x[high], land[1], along), x[high], land[1])),
            (2, between(copy(2, x[given], land[2], facing), lambda: add(x[own], land[2]))),
            (3, between(copy(3, x[own], land[3], beside), lambda: add(x[own], land[3]))),
            (4, between(copy(4, x[own], out[own], facing), nothing, keep(own, 0))),
            (5, outward(copy(5, out[low], out[low], along))),
            (6, outward(copy(6, out[high], out[high], along))),
            (1, everyone(copy(7, x[other], land[4], beside), lambda: add(x[mine], land[4]))),
            (2, inward(copy(8, x[mine], land[5], along), x[mine], land[5])),
            (3, between(copy(9, x[mine], land[6], facing), lambda: add(x[mine], land[6]))),
            (4, outward(copy(10, x[mine], out[mine], along), keep(mine, 1))),
            (5, everyone(copy(11, out[mine], out[mine], beside), nothing)),
        ]

    def paired_stages(stream, cycle, index):
        chunk = (stream * cycles + cycle) * PAIRED + index
        x = paired.at[rows_of(chunk)]
        out = paired_out.at[y, rows_of(chunk)]
        land = [paired_land.at[chunk, i] for i in range(2)]

        def copy(slot, source, target, device):
            return remote(
                source, target, paired_send.at[chunk, slot], paired_recv.at[chunk, slot], device
            )

        keep = Late(lambda: pltpu.make_async_copy(x, out, paired_local.at[chunk]))
        slot, slot_sem = ring.at[stream, index], ring_sem.at[stream, index]

        def fetch():
            begin = 0
            for source in arrived_in:
                count = source.shape[0] // CHUNK

                @pl.when((chunk >= begin) & (chunk < begin + count))
                def _(source=source, begin=begin):
                    pltpu.make_async_copy(
                        source.at[rows_of(chunk - begin)], slot, slot_sem
                    ).start()

                begin += count

        def fetched():
            pltpu.make_async_copy(arrived_in[0].at[rows_of(0)], slot, slot_sem).wait()
            add(x, slot)

        return [
            (2 + index, (fetch, fetched)),
            (3 + index, inward(copy(0, x, land[0], along), x, land[0])),
            (5 + index, between(copy(1, x, land[1], facing), lambda: add(x, land[1]))),
            (7 + index, outward(copy(2, x, out, along), keep)),
            (LAST_HOP[index], everyone(copy(3, out, out, beside), nothing)),
        ]

    offsets = range(max(LAST_HOP) + 1)

    def run(step, stream, offset, back, what):
        cycle = step - back

        @pl.when((cycle >= 0) & (cycle < cycles))
        def _():
            for when, pair in open_stages(stream, cycle):
                if when == offset:
                    pair[what]()
            for index in range(PAIRED):
                chunk = (stream * cycles + cycle) * PAIRED + index

                def each(index=index):
                    for when, pair in paired_stages(stream, cycle, index):
                        if when == offset:
                            pair[what]()

                if offset in (2 + index, 3 + index, 5 + index, 7 + index, LAST_HOP[index]):
                    pl.when(chunk < paired_chunks)(each)

    def late_copy(piece):
        rows = rows_of(piece)
        return pltpu.make_async_remote_copy(
            src_ref=late_other.at[rows],
            dst_ref=late_arrived.at[rows],
            send_sem=late_send.at[piece],
            recv_sem=late_recv.at[piece],
            device_id={"dp": beside},
            device_id_type=MESH,
        )

    late_count = late_other.shape[0] // CHUNK

    def body(step, carry):
        for phase in range(PERIOD):
            if phase == 0:

                @pl.when(step == 1)
                def _():
                    @pl.loop(0, late_count)
                    def _(piece):
                        late_copy(piece).wait()

            @pl.loop(0, 2)
            def _(stream):
                if phase in (0, 2, 4, 6):
                    piece = phase + stream

                    @pl.when((step == 0) & (piece < late_count))
                    def _():
                        late_copy(piece).start()

                for offset in offsets:
                    if (offset + 1) % PERIOD == phase:
                        run(step, stream, offset, (offset + 1) // PERIOD, 1)
                for offset in offsets:
                    if offset % PERIOD == phase:
                        run(step, stream, offset, offset // PERIOD, 0)

            if phase < 8:
                number = (step + 1) * 8 + phase
                pl.when(number < chunk_count)(partial(multiply, number))

        return carry

    lax.fori_loop(0, cycles + 2, body, 0)


def sum_chunks(factors, paired, arrived, late):
    open_rows = sum(item[0].shape[1] * item[2].shape[1] // WIDE for item in factors)
    paired_rows = sum(item.shape[0] for item in paired)
    depth = factors[0][0].shape[0]
    cycles = open_rows // (CHUNK * 8)
    chunks = paired_rows // CHUNK
    late_chunks = paired[late].shape[0] // CHUNK
    late_first = sum(item.shape[0] for item in paired[:late]) // CHUNK % (cycles * PAIRED)
    assert cycles * CHUNK * 8 == open_rows and chunks <= 2 * cycles * PAIRED
    assert late_chunks <= 8 and 3 * PAIRED <= late_first <= cycles * PAIRED - late_chunks
    return pl.pallas_call(
        partial(sum_kernel, cycles, len(paired), late),
        in_specs=[pl.BlockSpec(memory_space=pl.ANY)] * (8 + 2 * len(paired)),
        out_specs=[pl.BlockSpec(memory_space=pl.ANY)] * 3,
        out_shape=[
            jax.ShapeDtypeStruct((open_rows, WIDE), bf16),
            jax.ShapeDtypeStruct((2, paired_rows, WIDE), bf16),
            jax.ShapeDtypeStruct(paired[late].shape, bf16),
        ],
        scratch_shapes=[
            pltpu.VMEM((open_rows, WIDE), bf16),
            pltpu.VMEM((paired_rows, WIDE), bf16),
            pltpu.VMEM((2, cycles, LANDINGS, CHUNK, WIDE), bf16),
            pltpu.VMEM((chunks, 2, CHUNK, WIDE), bf16),
            pltpu.SemaphoreType.DMA((2, cycles, 12)),
            pltpu.SemaphoreType.DMA((2, cycles, 12)),
            pltpu.SemaphoreType.DMA((2, cycles, 2)),
            pltpu.SemaphoreType.DMA((chunks, 4)),
            pltpu.SemaphoreType.DMA((chunks, 4)),
            pltpu.SemaphoreType.DMA((chunks,)),
            pltpu.SemaphoreType.DMA((len(paired),)),
            pltpu.VMEM((2, PAIRED, CHUNK, WIDE), bf16),
            pltpu.SemaphoreType.DMA((2, PAIRED)),
            pltpu.VMEM((2, 4, depth, WIDE), bf16),
            pltpu.SemaphoreType.DMA((2, 4)),
            pltpu.SemaphoreType.DMA((8,)),
            pltpu.SemaphoreType.DMA((8,)),
        ],
        compiler_params=pltpu.CompilerParams(
            collective_id=0, has_side_effects=True, vmem_limit_bytes=63 * 1024 * 1024
        ),
        cost_estimate=pl.CostEstimate(
            flops=open_rows * WIDE * 4 * depth,
            bytes_accessed=(open_rows + 2 * paired_rows) * WIDE * 8,
            transcendentals=0,
        ),
    )(*factors[0], *factors[1], *paired, *arrived)


def side_grads_kernel(steps, count, y_ref, *refs):
    lefts, rights = refs[:count], refs[count : 2 * count]
    total = sum(dot_tn(left[...], right[...]) for left, right in zip(lefts, rights))
    for turn, out in enumerate(refs[-2:]):

        @pl.when(pl.program_id(0) // steps == turn)
        def _():
            for piece in range(out.shape[0]):
                out[piece] = total[:, piece * WIDE : (piece + 1) * WIDE].astype(bf16)


def side_grads(lefts, rights):
    depth, height = lefts[0].shape
    width = rights[0].shape[1]
    half, pieces = height // 2, width // WIDE
    tile = half if half <= 640 else 512
    steps = half // tile
    count = len(lefts)
    y = (lax.axis_index("dp") % 2).astype(jnp.int32).reshape(1)

    def left_at(i, y):
        owner = (i // steps) * y[0] + (1 - i // steps) * (1 - y[0])
        return (0, owner * steps + i % steps)

    shape = jax.ShapeDtypeStruct((pieces, half, WIDE), bf16)
    return pl.pallas_call(
        partial(side_grads_kernel, steps, count),
        grid_spec=pltpu.PrefetchScalarGridSpec(
            num_scalar_prefetch=1,
            grid=(2 * steps,),
            in_specs=[pl.BlockSpec((depth, tile), left_at)] * count
            + [pl.BlockSpec((depth, width), lambda i, y: (0, 0))] * count,
            out_specs=[
                pl.BlockSpec((pieces, tile, WIDE), lambda i, y: (0, jnp.minimum(i, steps - 1), 0)),
                pl.BlockSpec((pieces, tile, WIDE), lambda i, y: (0, jnp.maximum(i - steps, 0), 0)),
            ],
        ),
        out_shape=[shape, shape],
        compiler_params=pltpu.CompilerParams(vmem_limit_bytes=VMEM_LIMIT),
        cost_estimate=pl.CostEstimate(
            flops=2 * count * depth * height * width,
            bytes_accessed=2 * (count * depth * (height + width) + height * width),
            transcendentals=0,
        ),
    )(y, *lefts, *rights)


def stacked(grads):
    return grads.reshape(-1, WIDE)


def unpack_kernel(pieces, *refs):
    count = len(refs) // (pieces + 1)
    for at in range(count):
        out = refs[count * pieces + at]
        for piece in range(pieces):
            out[:, piece * WIDE : (piece + 1) * WIDE] = refs[at * pieces + piece][0].astype(f32)


def unpack(height, width, tile, *places):
    half, pieces = height // 2, width // WIDE
    steps = half // tile

    def piece_spec(first, second, piece):
        begin, step = first[1] // tile, (second[1] - first[1]) // tile
        assert first[1] % tile == 0 and second[1] % tile == 0
        return pl.BlockSpec(
            (1, tile, WIDE),
            lambda i, j: (
                first[0] + i * (second[0] - first[0]),
                begin + i * step + piece * steps + j,
                0,
            ),
        )

    count = len(places)
    return pl.pallas_call(
        partial(unpack_kernel, pieces),
        grid=(2, steps),
        in_specs=[
            piece_spec(first, second, piece)
            for _, first, second in places
            for piece in range(pieces)
        ],
        out_specs=[pl.BlockSpec((tile, width), lambda i, j: (i * steps + j, 0))] * count,
        out_shape=[jax.ShapeDtypeStruct((height, width), f32)] * count,
        compiler_params=pltpu.CompilerParams(vmem_limit_bytes=60 * 1024 * 1024),
        cost_estimate=pl.CostEstimate(
            flops=count * height * width,
            bytes_accessed=6 * count * height * width,
            transcendentals=0,
        ),
    )(*[stack for stack, _, _ in places for _ in range(pieces)])


def on_device(
    tokens,
    patches,
    text_lengths,
    prefix_lengths,
    group_map,
    ratio,
    cotangent,
    q_self,
    k_self,
    v_self,
    o_self,
    q_cross,
    k_cross,
    v_cross,
    o_cross,
    w_gate,
    w_up,
    w_down,
    gain_attn,
    gain_cross,
    gain_mlp,
):
    local_rows = tokens.shape[0]
    examples = text_lengths.shape[0]
    patch = patches.shape[0] // examples
    local_examples = local_rows // SEQ
    fast = lax.axis_size("mp") == 4 and lax.axis_size("dp") == 8 and local_examples % 2 == 0
    batches = 2 if fast else 1
    each = local_examples // batches
    rows = each * SEQ
    width = q_self.shape[1]

    lens_f = text_lengths.astype(f32)
    robot = (group_map == 0).astype(f32)
    web = 1.0 - robot
    local_counts = jnp.stack([jnp.sum(lens_f * robot), jnp.sum(lens_f * web)])
    counts = butterfly(jnp.broadcast_to(local_counts[:, None], (2, 128)), "dp")[:, 0]
    ratio_f = ratio.astype(f32)
    share = ratio_f / jnp.sum(ratio_f)
    group_scale = share * jnp.sum(counts) / jnp.maximum(counts, 1.0)
    example_scale = robot * group_scale[0] + web * group_scale[1]
    mine = lax.axis_index("mp") * local_examples
    own_scale = lax.dynamic_slice_in_dim(example_scale, mine, local_examples, 0)
    own_length = lax.dynamic_slice_in_dim(text_lengths, mine, local_examples, 0)
    place = jnp.arange(SEQ, dtype=jnp.int32)
    live = (place[None, :] < own_length[:, None]).astype(f32)
    row_weight = (own_scale[:, None] * live).reshape(local_rows)

    owners = block_owners()
    which, lengths, prefixes = [], [], []
    for b in range(batches):
        ids = (
            owners[:, None] * local_examples + b * each + jnp.arange(each, dtype=jnp.int32)[None, :]
        ).reshape(-1).astype(jnp.int32)
        which.append(ids)
        lengths.append(jnp.take(text_lengths, ids))
        prefixes.append(jnp.take(prefix_lengths, ids))

    w_qkv = jnp.concatenate([q_self, k_self, v_self], axis=1)

    each_batch = range(batches)
    last = batches - 1

    def part(tensor, b):
        return tensor[b * rows : (b + 1) * rows]

    def product(left, right, dot):
        return lambda low, high: dot(left[low:high], right)

    outer = [part(cotangent, b).astype(f32) * part(row_weight, b)[:, None] for b in each_batch]
    outer_low = [item.astype(bf16) for item in outer]
    x_zero = [part(tokens, b).astype(f32) for b in each_batch]
    norm_one = [normalize(x_zero[b], gain_attn) for b in each_batch]
    scale_one = [item[1] for item in norm_one]
    norm_one = [item[0] for item in norm_one]

    none = [None] * batches
    self_probs, cross_probs, slope, value = (list(none) for _ in range(4))
    full_one, qkv, mixed_self, x_one, norm_two, scale_two = ([None] * batches for _ in range(6))
    full_two, query, mixed_cross, x_two, norm_three, scale_three = (
        [None] * batches for _ in range(6)
    )
    full_three, grad_three, hidden, d_gate, d_up, back_three = ([None] * batches for _ in range(6))
    grad_two_rows, grad_two, d_query, grad_one_rows, grad_one, d_qkv = (
        [None] * batches for _ in range(6)
    )
    gain_mlp_parts, gain_cross_parts, gain_attn_parts, grad_input, output = (
        [None] * batches for _ in range(5)
    )

    def self_block(b, arrived):
        full_one[b], qkv[b] = gathered_dot(norm_one[b], arrived, w_qkv, False, 1)
        mixed_self[b], self_probs[b] = self_forward(qkv[b], lengths[b], prefixes[b])
        return scattered_dot([mixed_self[b]], [o_self], False, True, 2)

    def self_norm(b, arrived):
        x_one[b] = x_zero[b] + scatter_end(arrived)
        norm_two[b], scale_two[b] = normalize(x_one[b], gain_cross)

    def cross_block(b, arrived, keys, values):
        full_two[b], query[b] = gathered_dot(norm_two[b], arrived, q_cross, False, 3)
        mixed_cross[b], cross_probs[b] = cross_forward(query[b], keys, values, which[b], patch)
        return scattered_dot([mixed_cross[b]], [o_cross], False, True, 4)

    def cross_norm(b, arrived):
        x_two[b] = x_one[b] + scatter_end(arrived)
        norm_three[b], scale_three[b] = normalize(x_two[b], gain_mlp)

    def mlp_up(b, arrived):
        full_three[b], hidden[b], slope[b], value[b] = gathered_tiles(
            norm_three[b], arrived, [w_gate, w_up], [], up_body, 3, 5
        )

    def mlp_down(b, arrived):
        grad_three[b], d_gate[b], d_up[b] = gathered_tiles(
            outer_low[b], arrived, [w_down], [slope[b], value[b]], down_body, 2, 12
        )

    def mlp_back(b):
        return scattered_dot([d_gate[b], d_up[b]], [w_gate, w_up], True, False, 6)

    def mlp_norm_back(b, arrived):
        back, gain_mlp_parts[b] = norm_back(
            x_two[b], scale_three[b], gain_mlp, scatter_end(arrived)
        )
        grad_two_rows[b] = outer[b] + back
        return grad_two_rows[b].astype(bf16)

    def cross_back(b, own, arrived, keys, values, earlier):
        grad_two[b], d_mixed = gathered_dot(own, arrived, o_cross, True, 7)
        d_query[b], *d_kv = cross_backward(
            query[b], keys, values, cross_probs[b], d_mixed, which[b], patch, earlier
        )
        return scattered_dot([d_query[b]], [q_cross], True, False, 8), d_kv

    def cross_norm_back(b, arrived):
        back, gain_cross_parts[b] = norm_back(
            x_one[b], scale_two[b], gain_cross, scatter_end(arrived)
        )
        grad_one_rows[b] = grad_two_rows[b] + back
        return grad_one_rows[b].astype(bf16)

    def self_back(b, own, arrived):
        grad_one[b], d_mixed = gathered_dot(own, arrived, o_self, True, 9)
        d_qkv[b] = self_backward(qkv[b], self_probs[b], d_mixed)
        return scattered_dot([d_qkv[b]], [w_qkv], True, False, 10)

    def self_norm_back(b, arrived):
        back, gain_attn_parts[b] = norm_back(
            x_zero[b], scale_one[b], gain_attn, scatter_end(arrived)
        )
        grad_input[b] = grad_one_rows[b] + back

    def project_out(b):
        return scattered_dot([hidden[b]], [w_down], False, True, 11)

    sent = list(none)
    got = list(none)
    back = list(none)
    grads = list(none)
    own = list(none)
    shown = list(none)
    if fast:
        got[0] = gather_start(norm_one[0])
        got[0], norm_one[1], w_qkv, outer_low, outer, which, lengths, prefixes = fence(
            got[0], norm_one[1], w_qkv, outer_low, outer, which, lengths, prefixes
        )
        got[1] = gather_start(norm_one[1])
        sent[0] = self_block(0, got[0])
        sent[0], got[1] = fence(sent[0], got[1])
        back[0] = scatter_move(sent[0])
        sent[1] = self_block(1, got[1])
        back[0], sent[1], k_cross = fence(back[0], sent[1], k_cross)
        back[1] = scatter_move(sent[1])
        self_norm(0, back[0])
        keys = dot_nn(patches, k_cross).astype(bf16)
        norm_two[0], back[1], keys, v_cross = fence(norm_two[0], back[1], keys, v_cross)
        got[0] = gather_start(norm_two[0])
        self_norm(1, back[1])
        values = dot_nn(patches, v_cross).astype(bf16)
        norm_two[1], got[0], values = fence(norm_two[1], got[0], values)
        got[1] = gather_start(norm_two[1])
        sent[0] = cross_block(0, got[0], keys, values)
        sent[0], got[1] = fence(sent[0], got[1])
        back[0] = scatter_move(sent[0])
        sent[1] = cross_block(1, got[1], keys, values)
        sent[1], back[0] = fence(sent[1], back[0])
        back[1] = scatter_move(sent[1])
        cross_norm(0, back[0])
        norm_three[0], back[1], outer_low = fence(norm_three[0], back[1], outer_low)
        got[0] = gather_start(norm_three[0])
        cross_norm(1, back[1])
        got[0], outer_low, norm_three[1] = fence(got[0], outer_low, norm_three[1])
        got[1] = gather_start(norm_three[1])
        mlp_up(0, got[0])
        got[1], slope[0], outer_low = fence(got[1], slope[0], outer_low)
        grads[0] = gather_start(outer_low[0])
        mlp_up(1, got[1])
        grads[0], slope[1], outer_low[1] = fence(grads[0], slope[1], outer_low[1])
        grads[1] = gather_start(outer_low[1])
        mlp_down(0, grads[0])
        sent[0] = mlp_back(0)
        grads[1], sent[0] = fence(grads[1], sent[0])
        back[0] = scatter_move(sent[0])
        mlp_down(1, grads[1])
        down_other, down_mine = side_grads(hidden, grad_three)
        back[0], d_gate[1], d_up[1], down_other = fence(
            back[0], d_gate[1], d_up[1], down_other
        )
        own[0] = mlp_norm_back(0, back[0])
        got[0] = gather_start(own[0])
        down_sent = flip(down_other, "dp", 1)
        sent[1] = mlp_back(1)
        own[0], got[0], sent[1], d_gate, d_up = fence(own[0], got[0], sent[1], d_gate, d_up)
        back[1] = scatter_move(sent[1])
        gate_other, gate_mine = side_grads(full_three, d_gate)
        up_other, up_mine = side_grads(full_three, d_up)
        back[1], gate_other, up_other = fence(back[1], gate_other, up_other)
        own[1] = mlp_norm_back(1, back[1])
        got[1] = gather_start(own[1])
        gate_sent = flip(gate_other, "dp", 1)
        sent[0], d_kv = cross_back(0, own[0], got[0], keys, values, ())
        own[1], got[1], sent[0], d_kv, down_sent, up_other = fence(
            own[1], got[1], sent[0], d_kv, down_sent, up_other
        )
        back[0] = scatter_move(sent[0])
        up_sent = flip(up_other, "dp", 1)
        sent[1], d_kv = cross_back(1, own[1], got[1], keys, values, d_kv)
        sent[1], back[0], d_kv, mixed_cross, hidden = fence(
            sent[1], back[0], d_kv, mixed_cross, hidden
        )
        back[1] = scatter_move(sent[1])
        own[0] = cross_norm_back(0, back[0])
        o_other, o_mine = side_grads(mixed_cross, grad_two)
        q_other, q_mine = side_grads(full_two, d_query)
        own[0], back[1], d_kv, o_other, q_other, gate_sent, down_mine = fence(
            own[0], back[1], d_kv, o_other, q_other, gate_sent, down_mine
        )
        got[0] = gather_start(own[0])
        own[1] = cross_norm_back(1, back[1])
        k_other, k_mine = side_grads([patches], [d_kv[0]])
        v_other, v_mine = side_grads([patches], [d_kv[1]])
        got[0], own[1], k_other, v_other, hidden, gate_mine = fence(
            got[0], own[1], k_other, v_other, hidden, gate_mine
        )
        got[1] = gather_start(own[1])
        o_sent = flip(o_other, "dp", 1)
        sent[0] = self_back(0, own[0], got[0])
        got[1], sent[0], up_sent, o_sent, q_other = fence(
            got[1], sent[0], up_sent, o_sent, q_other
        )
        q_sent = flip(q_other, "dp", 1)
        back[0] = scatter_move(sent[0])
        sent[1] = self_back(1, own[1], got[1])
        back[0], sent[1], mixed_self, hidden, q_sent, k_other = fence(
            back[0], sent[1], mixed_self, hidden, q_sent, k_other
        )
        k_sent = flip(k_other, "dp", 1)
        back[1] = scatter_move(sent[1])
        self_norm_back(0, back[0])
        shown = [project_out(b) for b in each_batch]
        back[1], grad_input[0], shown, k_sent = fence(back[1], grad_input[0], shown, k_sent)
        self_norm_back(1, back[1])
        back = [scatter_move(shown[b]) for b in each_batch]
        factors = [[*full_one, *d_qkv], [*mixed_self, *grad_one]]
        paired = [down_mine, gate_mine, up_mine, q_mine, k_mine, v_mine, o_mine]
        arrived = [down_sent, gate_sent, up_sent, q_sent, k_sent, v_other, o_sent]
        open_sum, paired_sum, _ = sum_chunks(
            factors, *([stacked(item) for item in items] for items in (paired, arrived)), 5
        )
    else:
        sent[0] = self_block(0, gather_start(norm_one[0]))
        self_norm(0, scatter_move(sent[0]))
        keys = dot_nn(patches, k_cross).astype(bf16)
        values = dot_nn(patches, v_cross).astype(bf16)
        sent[0] = cross_block(0, gather_start(norm_two[0]), keys, values)
        cross_norm(0, scatter_move(sent[0]))
        full_three[0] = gather_start(norm_three[0])
        grad_three[0] = gather_start(outer_low[0])
        hidden[0], d_gate[0], d_up[0] = mlp(full_three[0], grad_three[0], w_gate, w_up, w_down)
        own[0] = mlp_norm_back(0, scatter_move(mlp_back(0)))
        sent[0], d_kv = cross_back(0, own[0], gather_start(own[0]), keys, values, ())
        own[0] = cross_norm_back(0, scatter_move(sent[0]))
        sent[0] = self_back(0, own[0], gather_start(own[0]))
        self_norm_back(0, scatter_move(sent[0]))
        sums = lax.psum(
            [
                item.astype(bf16)
                for item in (
                    dot_tn(full_one[0], d_qkv[0]),
                    dot_tn(mixed_self[0], grad_one[0]),
                    dot_tn(full_two[0], d_query[0]),
                    dot_tn(patches, d_kv[0]),
                    dot_tn(patches, d_kv[1]),
                    dot_tn(mixed_cross[0], grad_two[0]),
                    dot_tn(full_three[0], d_gate[0]),
                    dot_tn(full_three[0], d_up[0]),
                    dot_tn(hidden[0], grad_three[0]),
                )
            ],
            "dp",
        )
        back = [scatter_move(project_out(0))]
    gains = jnp.stack(
        [sum(parts) for parts in (gain_attn_parts, gain_cross_parts, gain_mlp_parts)]
    )
    if fast:
        open_sum, paired_sum, back, gains = fence(open_sum, paired_sum, back, gains)

        whole = open_sum[None]
        half = q_self.shape[0] // 2
        pieces = width // WIDE
        places, start = [], 0
        for weight in (w_down, w_gate, w_up, q_cross, k_cross, v_cross, o_cross):
            places.append((paired_sum, (0, start), (1, start)))
            start += weight.size // WIDE // 2
        self_places = [
            (whole, (0, at * pieces * half), (0, (3 + at) * pieces * half)) for at in range(3)
        ]
        start = w_qkv.size // WIDE
        o_place = (whole, (0, start), (0, start + o_self.size // WIDE // 2))
        groups = [
            unpack(*w_down.shape, w_down.shape[0] // 4, places[0]),
            unpack(*w_gate.shape, 256, *places[1:3]),
            unpack(*q_self.shape, 256, *places[3:6], *self_places),
            unpack(*o_self.shape, o_self.shape[0] // 4, places[6], o_place),
        ]
        gains = gains + flip(gains, "mp", 1)
        for at, (axis, bit) in enumerate((("mp", 2), ("dp", 1), ("dp", 2), ("dp", 4))):
            arrived, groups[at] = fence(flip(gains, axis, bit), groups[at])
            gains = gains + arrived
        (d_wdown,), (d_wgate, d_wup), shared, (d_ocross, d_oself) = groups
        d_qcross, d_kcross, d_vcross, *d_self = shared
    else:
        (
            d_wqkv,
            d_oself,
            d_qcross,
            d_kcross,
            d_vcross,
            d_ocross,
            d_wgate,
            d_wup,
            d_wdown,
        ) = [item.astype(f32) for item in sums]
        d_self = [d_wqkv[:, at * width : (at + 1) * width] for at in range(3)]
    output = jnp.concatenate(
        [(x_two[b] + scatter_end(back[b])).astype(bf16) for b in each_batch], axis=0
    )
    grad_input = jnp.concatenate(grad_input, axis=0)
    if not fast:
        gains = butterfly(butterfly(gains, "mp"), "dp")
    return (
        output,
        grad_input,
        *d_self,
        d_oself,
        d_qcross,
        d_kcross,
        d_vcross,
        d_ocross,
        d_wgate,
        d_wup,
        d_wdown,
        gains[0],
        gains[1],
        gains[2],
    )


def solution(mesh):
    by_rows = P(("dp", "mp"), None)
    columns = P(None, "mp")
    rows = P("mp", None)
    weights = (columns, columns, columns, rows, columns, columns, columns, rows, columns, columns, rows)
    in_specs = (
        (by_rows, P("dp", None), P("dp"), P("dp"), P("dp"), P(), by_rows) + weights + (P(), P(), P())
    )
    out_specs = (by_rows, by_rows) + weights + (P(), P(), P())
    return jax.shard_map(
        on_device, mesh=mesh, in_specs=in_specs, out_specs=out_specs, check_vma=False
    )
```
